128 devices in a mesh: row: 8 (over y, z_lo), col: 16 (over x, z_hi, core).
Axes of the slice: x: 4, y: 4, z: 4 (z_hi: 2, z_lo: 2; z = z_hi * 2 + z_lo), core: 2. Of those that a mesh axis runs over, the one named last changes fastest.
Arguments:
- tokens: float32 [16384, 2048], P(('row', 'col')), may hold values from -6 to 6
- cotangent: float32 [16384, 2048], P(('row', 'col'))
- doc_starts: int32 [4], replicated, may hold values from 0 to 16383, as said below
- mixer_w: float32 [4, 2048, 2048], P(None, 'row', 'col'), may hold values from -0.125 to 0.125
- ffn_w: float32 [3, 2048, 5632], P(None, 'row', 'col'), may hold values from -0.125 to 0.125
- gains: float32 [2, 2048], replicated, may hold values from 0.5 to 1.5
- taps: float32 [3, 2048], P(None, 'col'), may hold values from -3 to 3
- mixer_m: float32 [4, 2048, 2048], P(None, 'row', 'col'), may hold values from -160 to 160
- mixer_v: float32 [4, 2048, 2048], P(None, 'row', 'col'), may hold values from 3440.64 to 13762.56
- ffn_m: float32 [3, 2048, 5632], P(None, 'row', 'col'), may hold values from -128 to 128
- ffn_v: float32 [3, 2048, 5632], P(None, 'row', 'col'), may hold values from 2457.6 to 9830.4
- gain_m: float32 [2, 2048], replicated, may hold values from -320 to 320
- gain_v: float32 [2, 2048], replicated, may hold values from 13762.56 to 55705.6
- tap_m: float32 [3, 2048], P(None, 'col'), may hold values from -160 to 160
- tap_v: float32 [3, 2048], P(None, 'col'), may hold values from 3440.64 to 13762.56
Outputs:
- output: float32 [16384, 2048], P(('row', 'col'))
- input_grad: float32 [16384, 2048], P(('row', 'col'))
- mixer_grad: float32 [4, 2048, 2048], P(None, 'row', 'col')
- mixer_new: float32 [4, 2048, 2048], P(None, 'row', 'col')
- mixer_m_new: float32 [4, 2048, 2048], P(None, 'row', 'col')
- mixer_v_new: float32 [4, 2048, 2048], P(None, 'row', 'col')
- ffn_grad: float32 [3, 2048, 5632], P(None, 'row', 'col')
- ffn_new: float32 [3, 2048, 5632], P(None, 'row', 'col')
- ffn_m_new: float32 [3, 2048, 5632], P(None, 'row', 'col')
- ffn_v_new: float32 [3, 2048, 5632], P(None, 'row', 'col')
- gain_grad: float32 [2, 2048], replicated
- gain_new: float32 [2, 2048], replicated
- gain_m_new: float32 [2, 2048], replicated
- gain_v_new: float32 [2, 2048], replicated
- tap_grad: float32 [3, 2048], P(None, 'col')
- tap_new: float32 [3, 2048], P(None, 'col')
- tap_m_new: float32 [3, 2048], P(None, 'col')
- tap_v_new: float32 [3, 2048], P(None, 'col')
The draws below stay inside these ranges and needn't reach their ends.
Inputs may be any that keep to these rules, and one draw needn't show every extreme that they name: `doc_starts`: the first entry is 0, the last is 16383, and the entries strictly increase; document 1 begins within the first 2048 tokens and ends within the last 2048 tokens.
All inputs are finite; a program needn't handle non-finite values.
Results may differ from the reference program's by a relative error of at most 0.025.
Values may be sent and summed in bfloat16 or wider, within the bound.
A program may use at most 192 MiB of HBM per device.

```python
import math
import jax
import jax.numpy as jnp
from jax import lax

D = 2048
FF = 5632
STEP = 5
TOKENS = 16384
N_ROW = 8


def draw_cotangent(key, part):
    key = jax.random.fold_in(key, 7)
    places = jnp.arange(TOKENS, dtype=jnp.float32)[:, None] / (TOKENS - 1)
    noise = jax.random.normal(key, (TOKENS, D), jnp.float32)
    return noise * (1.0 + 2.0 * places)


def draw_doc_starts(key, part):
    key = jax.random.fold_in(key, 11)
    keys = jax.random.split(key, 2)
    row_tokens = TOKENS // N_ROW
    last_base = TOKENS - row_tokens
    first = jax.random.randint(keys[0], (1,), 1, row_tokens // 2 + 1)
    second = last_base + jax.random.randint(keys[1], (1,), row_tokens // 4, row_tokens // 2)
    third = jnp.full((1,), TOKENS - 1, jnp.int32)
    return jnp.concatenate([jnp.zeros((1,), jnp.int32), first.astype(jnp.int32), second.astype(jnp.int32), third]).astype(jnp.int32)


def block_levels(stream_key, extent, shards, smallest, top_value):
    def one(dim, shards_of):
        steps = jax.random.uniform(jax.random.fold_in(jax.random.fold_in(stream_key, 6), dim), (shards_of,), jnp.float32, smallest / len(shards), top_value / len(shards))
        return jnp.repeat(jnp.exp(steps), extent[dim] // shards_of).reshape((-1,) + (1,) * (len(extent) - dim - 1))

    factor_of = one(*shards[0])
    for cut in shards[1:]:
        factor_of = factor_of * one(*cut)
    return factor_of


def gaussian(key, dims, width, most, shards=(), kind=jnp.bfloat16):
    array = width * jax.random.normal(key, dims, jnp.float32)
    if shards:
        array = array * block_levels(key, dims, shards, -0.22, 0.18)
    return jnp.clip(array, -most, most).astype(kind)


def setup_inputs(seed: int = 0) -> dict:
    seeds = jax.random.split(jax.random.key(seed), 16)
    return {
        "tokens": gaussian(seeds[0], (TOKENS, D), 1.0, 6.0, ((0, 128),), jnp.float32),
        "cotangent": draw_cotangent(jax.random.fold_in(seeds[15], 71), 0),
        "doc_starts": draw_doc_starts(jax.random.fold_in(seeds[15], 71), 0),
        "mixer_w": gaussian(seeds[3], (4, D, D), D ** -0.5, 0.125, ((1, 8), (2, 16)), jnp.float32),
        "ffn_w": gaussian(seeds[4], (3, D, FF), D ** -0.5, 0.125, ((1, 8), (2, 16)), jnp.float32),
        "gains": jnp.clip(1.0 + 0.1 * jax.random.normal(seeds[5], (2, D), jnp.float32), 0.5, 1.5),
        "taps": gaussian(seeds[6], (3, D), 0.6, 3.0, ((1, 16),), jnp.float32),
        "mixer_m": gaussian(seeds[7], (4, D, D), (0.22 * TOKENS ** 0.5), 160.0, ((1, 8), (2, 16)), jnp.float32),
        "mixer_v": jnp.clip(jnp.exp(math.log(13762.56) - 1.3862944 * jax.random.uniform(seeds[8], (4, D, D), jnp.float32) ** block_levels(seeds[8], (4, D, D), ((1, 8), (2, 16)), -0.2, 0.2)), 3440.64, 13762.56),
        "ffn_m": gaussian(seeds[9], (3, D, FF), (0.19 * TOKENS ** 0.5), 128.0, ((1, 8), (2, 16)), jnp.float32),
        "ffn_v": jnp.clip(jnp.exp(math.log(9830.4) - 1.3862944 * jax.random.uniform(seeds[10], (3, D, FF), jnp.float32) ** block_levels(seeds[10], (3, D, FF), ((1, 8), (2, 16)), -0.2, 0.2)), 2457.6, 9830.4),
        "gain_m": gaussian(seeds[11], (2, D), (0.45 * TOKENS ** 0.5), 320.0, (), jnp.float32),
        "gain_v": jnp.clip(jnp.exp(jax.random.uniform(seeds[12], (2, D), jnp.float32, math.log(13762.56), math.log(55705.6))), 13762.56, 55705.6),
        "tap_m": gaussian(seeds[13], (3, D), (0.22 * TOKENS ** 0.5), 160.0, ((1, 16),), jnp.float32),
        "tap_v": jnp.clip(jnp.exp(math.log(13762.56) - 1.3862944 * jax.random.uniform(seeds[14], (3, D), jnp.float32) ** block_levels(seeds[14], (3, D), ((1, 16),), -0.2, 0.2)), 3440.64, 13762.56),
    }


@jax.custom_vjp
def low(v):
    return lax.optimization_barrier(v.astype(jnp.bfloat16)).astype(jnp.float32)

@jax.custom_vjp
def low_back(v):
    return v

def low_keep(v):
    return (low(v), None)

def low_pass(kept, grad):
    return (grad,)

def back_keep(v):
    return (v, None)

def back_low(kept, grad):
    return (low(grad),)
low.defvjp(low_keep, low_pass)
low_back.defvjp(back_keep, back_low)
NORM_EPS = 1e-05
BETA_ONE = 0.9
BETA_TWO = 0.95
ADAM_EPS = 1e-08
MATRIX_DECAY = 0.1
MATRIX_RATE = 0.03
SMALL_RATE = 0.3

def exact_dot(left, right):
    return jnp.dot(left, right, precision=lax.Precision.HIGHEST, preferred_element_type=jnp.float32)

def exact_trans(left, right):
    return lax.dot_general(left, right, (((1,), (1,)), ((), ())), precision=lax.Precision.HIGHEST, preferred_element_type=jnp.float32)

def rms_norm(values, gain):
    return values * lax.rsqrt(lax.optimization_barrier(jnp.mean(values * values, axis=1, keepdims=True)) + NORM_EPS) * gain

def shift_down(values, lag):
    return jnp.concatenate([jnp.zeros((lag, values.shape[1]), jnp.float32), values[:-lag]], axis=0)

def block_forward(tokens, mixer_w, ffn_w, gains, taps, keep_one, keep_two):
    normed = low(rms_norm(tokens, gains[0]))
    mixer_low = low(mixer_w)
    input_gate = low_back(exact_dot(normed, mixer_low[0]))
    output_gate = low_back(exact_dot(normed, mixer_low[1]))
    conv_input = low_back(exact_dot(normed, mixer_low[2]))
    mixed_bx = input_gate * conv_input
    convolved = taps[2] * mixed_bx + taps[1] * keep_one * shift_down(mixed_bx, 1) + taps[0] * keep_two * shift_down(mixed_bx, 2)
    gated_out = low(output_gate * convolved)
    residual = tokens + low_back(exact_trans(gated_out, mixer_low[3]))
    ffn_in = low(rms_norm(residual, gains[1]))
    ffn_low = low(ffn_w)
    gate_proj = low_back(exact_dot(ffn_in, ffn_low[0]))
    up_proj = low_back(exact_dot(ffn_in, ffn_low[1]))
    hidden = low(jax.nn.silu(gate_proj) * up_proj)
    return residual + low_back(exact_trans(hidden, ffn_low[2]))

def adam_update(weight, gradient, first, second, step_rate, decay_rate):
    first_new = BETA_ONE * first + (1.0 - BETA_ONE) * gradient
    second_new = BETA_TWO * second + (1.0 - BETA_TWO) * gradient * gradient
    first_hat = first_new / (1.0 - BETA_ONE ** STEP)
    second_hat = second_new / (1.0 - BETA_TWO ** STEP)
    weight_new = weight - step_rate * (first_hat / (jnp.sqrt(second_hat) + ADAM_EPS) + decay_rate * weight)
    return (weight_new, first_new, second_new)

def reference(tokens, cotangent, doc_starts, mixer_w, ffn_w, gains, taps, mixer_m, mixer_v, ffn_m, ffn_v, gain_m, gain_v, tap_m, tap_v):
    places = jnp.arange(TOKENS, dtype=jnp.int32)
    start_flags = jnp.any(places[:, None] == doc_starts[None, :].astype(jnp.int32), axis=1)
    keep_one = jnp.where(start_flags, 0.0, 1.0).astype(jnp.float32)[:, None]
    keep_prev = jnp.concatenate([jnp.ones((1, 1), jnp.float32), keep_one[:-1]], axis=0)
    keep_two = keep_one * keep_prev

    def forward(token_rows, mixer_mats, ffn_mats, gain_rows, tap_rows):
        return block_forward(token_rows, mixer_mats, ffn_mats, gain_rows, tap_rows, keep_one, keep_two)
    output, pullback = jax.vjp(forward, tokens, mixer_w, ffn_w, gains, taps)
    input_grad, mixer_grad, ffn_grad, gain_grad, tap_grad = pullback(cotangent)
    mixer_new, mixer_m_new, mixer_v_new = adam_update(mixer_w, mixer_grad, mixer_m, mixer_v, MATRIX_RATE, MATRIX_DECAY)
    ffn_new, ffn_m_new, ffn_v_new = adam_update(ffn_w, ffn_grad, ffn_m, ffn_v, MATRIX_RATE, MATRIX_DECAY)
    gain_new, gain_m_new, gain_v_new = adam_update(gains, gain_grad, gain_m, gain_v, SMALL_RATE, 0.0)
    tap_new, tap_m_new, tap_v_new = adam_update(taps, tap_grad, tap_m, tap_v, SMALL_RATE, 0.0)
    return (output, input_grad, mixer_grad, mixer_new, mixer_m_new, mixer_v_new, ffn_grad, ffn_new, ffn_m_new, ffn_v_new, gain_grad, gain_new, gain_m_new, gain_v_new, tap_grad, tap_new, tap_m_new, tap_v_new)
```

```python
import jax
import jax.numpy as jnp
from jax import lax
from jax.experimental import pallas as pl
from jax.experimental.pallas import tpu as pltpu
from jax.sharding import PartitionSpec as P

STEP = 5


NORM_EPS = 1e-05
BETA_ONE = 0.9
BETA_TWO = 0.95
ADAM_EPS = 1e-08
MATRIX_DECAY = 0.1
MATRIX_RATE = 0.03
SMALL_RATE = 0.3

MESH = pl.DeviceIdType.MESH
BF16 = jnp.bfloat16
F32 = jnp.float32
RING = 4


def place():
    row, col = lax.axis_index("row"), lax.axis_index("col")
    return {"x": col // 4, "y": row // 2, "z": (col // 2) % 2 * 2 + row % 2, "k": col % 2}


def device_at(at):
    return (at["y"] * 2 + at["z"] % 2, at["x"] * 4 + at["z"] // 2 * 2 + at["k"])


def wrap(value, length=RING):
    return lax.rem(value + length, length)


class Net:
    def __init__(self, send_sems, recv_sems, local_sems):
        self.me = place()
        self.send_sems, self.recv_sems, self.local_sems = send_sems, recv_sems, local_sems
        self.sent, self.local, self.count, self.local_count = [], [], 0, 0

    def near(self, axis, step):
        at = dict(self.me)
        at[axis] = wrap(at[axis] + step, 2 if axis == "k" else RING)
        return device_at(at)

    def barrier(self, axes):
        sem = pltpu.get_barrier_semaphore()
        targets = []
        for axis in axes:
            targets += [self.near(axis, 1)] if axis == "k" else [self.near(axis, 1), self.near(axis, -1)]
        for target in targets:
            pl.semaphore_signal(sem, inc=1, device_id=target, device_id_type=MESH)
        pl.semaphore_wait(sem, len(targets))

    def send(self, source, target, device, later=True):
        copy = pltpu.make_async_remote_copy(
            src_ref=source,
            dst_ref=target,
            send_sem=self.send_sems.at[self.count],
            recv_sem=self.recv_sems.at[self.count],
            device_id=device,
            device_id_type=MESH,
        )
        copy.start()
        self.count += 1
        if later:
            self.sent.append(copy)
        return copy

    def copy(self, source, target):
        copy = pltpu.make_async_copy(source, target, self.local_sems.at[self.local_count])
        copy.start()
        self.local_count += 1
        self.local.append(copy)
        return copy

    def finish(self):
        for copy in self.sent:
            copy.wait_send()
        for copy in self.local:
            copy.wait()


def merge(chains):
    pending = [[next(chain), number, chain] for number, chain in enumerate(chains)]
    while pending:
        pending.sort(key=lambda entry: entry[:2])
        entry = pending[0]
        yield entry[0]
        try:
            entry[0] = next(entry[2])
        except StopIteration:
            pending.pop(0)


def run(chains):
    for _ in merge(chains):
        pass


def gather_x(net, source, out, start=0.0, unit=2.75):
    x, k = net.me["x"], net.me["k"]
    rows = source.shape[0]
    half = rows // 2
    low, high = pl.ds(0, half), pl.ds(half, half)
    right, left, other = net.near("x", 1), net.near("x", -1), net.near("k", 1)
    ahead, behind, across = wrap(x + 1), wrap(x - 1), wrap(x + 2)
    own = (x, k)
    r0 = net.send(source.at[low], out.at[x, k, low], right)
    l1 = net.send(source.at[high], out.at[x, k, high], left)
    r1 = net.send(source.at[high], out.at[x, k, high], right)
    l0 = net.send(source.at[low], out.at[x, k, low], left)
    sib = [net.send(source, out.at[x, k], other)]
    net.copy(source, out.at[x, k])

    def relay(at, part):
        sib.append(net.send(out.at[at, k, part], out.at[at, k, part], other))

    yield start + unit * 2
    r0.wait_recv()
    far0 = net.send(out.at[behind, k, low], out.at[behind, k, low], right)
    relay(behind, low)
    yield start + unit * 2
    l1.wait_recv()
    far1 = net.send(out.at[ahead, k, high], out.at[ahead, k, high], left)
    relay(ahead, high)
    yield start + unit * 4
    r1.wait_recv()
    relay(behind, high)
    yield start + unit * 4
    l0.wait_recv()
    relay(ahead, low)
    yield start + unit * 6
    far0.wait_recv()
    relay(across, low)
    yield start + unit * 6
    far1.wait_recv()
    relay(across, high)
    for number, copy in enumerate(sib):
        yield start + unit * (6 + number / 4)
        copy.wait_recv()


def add_into(target, first, second):
    rows = target.shape[-2]
    lead = target.shape[:-2]
    strip = 16

    def body(step, _):
        at = pl.ds(pl.multiple_of(step * strip, strip), strip)
        for m in range(lead[0] if lead else 1):
            here = (m, at) if lead else (at,)
            target[here] = (first[here].astype(F32) + second[here].astype(F32)).astype(BF16)
        return 0

    lax.fori_loop(0, rows // strip, body, 0)


def scatter_x(net, parts, box, hop, land, out, start=0.0, unit=2.75):
    x, k = net.me["x"], net.me["k"]
    rows = out.shape[0]
    half = rows // 2
    low, high = pl.ds(0, half), pl.ds(half, half)
    right, left, other = net.near("x", 1), net.near("x", -1), net.near("k", 1)
    ahead, behind, across = wrap(x + 1), wrap(x - 1), wrap(x + 2)
    sib = {}
    for name, at in (("across", across), ("ahead", ahead), ("behind", behind), ("own", x)):
        sib[name] = net.send(parts.at[at, 1 - k], box.at[at], other)
    yield start + 2
    sib["across"].wait_recv()
    add_into(box.at[across], parts.at[across, k], box.at[across])
    far0 = net.send(box.at[across, low], hop.at[0], right)
    far1 = net.send(box.at[across, high], hop.at[1], left)
    yield start + 3
    sib["ahead"].wait_recv()
    add_into(box.at[ahead], parts.at[ahead, k], box.at[ahead])
    r1 = net.send(box.at[ahead, high], land.at[0, high], right)
    yield start + 4
    sib["behind"].wait_recv()
    add_into(box.at[behind], parts.at[behind, k], box.at[behind])
    l0 = net.send(box.at[behind, low], land.at[1, low], left)
    yield start + 2 + unit * 2
    far0.wait_recv()
    add_into(box.at[ahead, low], box.at[ahead, low], hop.at[0])
    r0 = net.send(box.at[ahead, low], land.at[0, low], right)
    yield start + 2 + unit * 2
    far1.wait_recv()
    add_into(box.at[behind, high], box.at[behind, high], hop.at[1])
    l1 = net.send(box.at[behind, high], land.at[1, high], left)
    yield start + 4 + unit * 4
    sib["own"].wait_recv()
    for turn, copy in ((4, r1), (4, l0), (6, r0), (6, l1)):
        yield start + 5 + unit * turn
        copy.wait_recv()

    def body(step, _):
        at = pl.ds(pl.multiple_of(step * 16, 16), 16)
        near = parts[x, k, at].astype(F32) + box[x, at].astype(F32)
        out[at] = near + (land[0, at].astype(F32) + land[1, at].astype(F32))
        return 0

    lax.fori_loop(0, rows // 16, body, 0)


def block(ref, y, z, half, rows):
    column = pl.multiple_of((y * 2 + z % 2) * 256 + half * 128, 128)
    return ref.at[:, z // 2, rows, pl.ds(column, 128)]


def gather_yz(net, source, out, half, start=0.0, unit=1.0):
    first, second = ("y", "z") if half == 0 else ("z", "y")
    rows = source.shape[1]
    cut = rows // 2
    low, high, whole = pl.ds(0, cut), pl.ds(cut, cut), pl.ds(0, rows)
    me = net.me

    def slot(a, b, part):
        y, z = (a, b) if half == 0 else (b, a)
        return block(out, y, z, half, part)

    a, b = me[first], me[second]
    columns = pl.ds(half * 128, 128)
    up, down = net.near(first, 1), net.near(first, -1)
    net.copy(source.at[:, :, columns], slot(a, b, whole))
    r0 = net.send(source.at[:, low, columns], slot(a, b, low), up)
    l1 = net.send(source.at[:, high, columns], slot(a, b, high), down)
    r1 = net.send(source.at[:, high, columns], slot(a, b, high), up)
    l0 = net.send(source.at[:, low, columns], slot(a, b, low), down)
    forward, backward = net.near(second, 1), net.near(second, -1)
    waits = []

    def spread(at, part, ref=None, time=0.0):
        ref = slot(at, b, part) if ref is None else ref
        waits.append((time, at, part, net.send(ref, slot(at, b, part), forward),
                      net.send(ref, slot(at, b, part), backward)))

    spread(a, low, source.at[:, low, columns], start + unit * 4)
    spread(a, high, source.at[:, high, columns], start + unit * 6)
    behind, ahead, across = wrap(a - 1), wrap(a + 1), wrap(a + 2)
    yield start + unit * 2
    r0.wait_recv()
    f0 = net.send(slot(behind, b, low), slot(behind, b, low), up)
    spread(behind, low, None, start + unit * 8)
    yield start + unit * 2
    l1.wait_recv()
    f1 = net.send(slot(ahead, b, high), slot(ahead, b, high), down)
    spread(ahead, high, None, start + unit * 10)
    yield start + unit * 4
    r1.wait_recv()
    spread(behind, high, None, start + unit * 13)
    yield start + unit * 4
    l0.wait_recv()
    spread(ahead, low, None, start + unit * 15)
    yield start + unit * 6
    f0.wait_recv()
    spread(across, low, None, start + unit * 18)
    yield start + unit * 6
    f1.wait_recv()
    spread(across, high, None, start + unit * 20)
    b_behind, b_ahead, b_across = wrap(b - 1), wrap(b + 1), wrap(b + 2)
    last = []
    for time, at, part, plus, minus in waits:
        keep = part is low
        yield time
        plus.wait_recv()
        if keep:
            last.append((time + unit * 4, net.send(slot(at, b_behind, part), slot(at, b_behind, part), forward)))
        yield time
        minus.wait_recv()
        if not keep:
            last.append((time + unit * 4, net.send(slot(at, b_ahead, part), slot(at, b_ahead, part), backward)))
    for time, copy in last:
        yield time
        copy.wait_recv()


def scatter_yz(net, parts, box, out, half, start=0.0, unit=1.0):
    first, second = ("z", "y") if half == 0 else ("y", "z")
    rows = out.shape[1]
    cut = rows // 2
    low, high, whole = pl.ds(0, cut), pl.ds(cut, cut), pl.ds(0, rows)
    a, b = net.me[first], net.me[second]
    ways = ((net.near(first, 1), net.near(first, -1)), (net.near(second, 1), net.near(second, -1)))
    a_near = (wrap(a + 1), wrap(a - 1), wrap(a + 2))
    b_near = (wrap(b + 1), wrap(b - 1), wrap(b + 2))

    def slot(at_a, at_b, part):
        y, z = (at_b, at_a) if half == 0 else (at_a, at_b)
        return block(parts, y, z, half, part)

    def ring(pick, places, way, base, time):
        up, down = way
        ahead, behind, across, own = places
        far0 = net.send(pick(across, low), box.at[base, :, low], up)
        far1 = net.send(pick(across, high), box.at[base, :, high], down)
        r1 = net.send(pick(ahead, high), box.at[base + 1, :, high], up)
        l0 = net.send(pick(behind, low), box.at[base + 2, :, low], down)
        yield time + unit * 2
        far0.wait_recv()
        add_into(pick(ahead, low), pick(ahead, low), box.at[base, :, low])
        r0 = net.send(pick(ahead, low), box.at[base + 1, :, low], up)
        yield time + unit * 2
        far1.wait_recv()
        add_into(pick(behind, high), pick(behind, high), box.at[base, :, high])
        l1 = net.send(pick(behind, high), box.at[base + 2, :, high], down)
        yield time + unit * 4
        r1.wait_recv()
        add_into(pick(own, high), pick(own, high), box.at[base + 1, :, high])
        yield time + unit * 4
        l0.wait_recv()
        add_into(pick(own, low), pick(own, low), box.at[base + 2, :, low])
        yield time + unit * 6
        r0.wait_recv()
        add_into(pick(own, low), pick(own, low), box.at[base + 1, :, low])
        yield time + unit * 6
        l1.wait_recv()
        add_into(pick(own, high), pick(own, high), box.at[base + 2, :, high])

    done = set()

    def first_ring(number, at_b):
        yield from ring(
            lambda at, part: slot(at, at_b, part), (*a_near, a), ways[0], 3 * number, start + unit * 6 * number
        )
        done.add(number)

    def second_ring():
        up, down = ways[1]
        ahead, behind, across = b_near

        def ready(number):
            while number not in done:
                yield start + unit * (6 * number + 6.5)

        yield from ready(0)
        far0 = net.send(slot(a, across, low), box.at[12, :, low], up)
        far1 = net.send(slot(a, across, high), box.at[12, :, high], down)
        yield from ready(1)
        r1 = net.send(slot(a, ahead, high), box.at[13, :, high], up)
        far0.wait_recv()
        add_into(slot(a, ahead, low), slot(a, ahead, low), box.at[12, :, low])
        r0 = net.send(slot(a, ahead, low), box.at[13, :, low], up)
        yield from ready(2)
        l0 = net.send(slot(a, behind, low), box.at[14, :, low], down)
        far1.wait_recv()
        add_into(slot(a, behind, high), slot(a, behind, high), box.at[12, :, high])
        l1 = net.send(slot(a, behind, high), box.at[14, :, high], down)
        yield from ready(3)
        own = slot(a, b, whole)
        for copy in (r1, r0, l0, l1):
            yield start + unit * 28
            copy.wait_recv()
        add_into(own, own, box.at[13])
        add_into(own, own, box.at[14])

    yield from merge(
        [first_ring(n, at_b) for n, at_b in enumerate((b_near[2], b_near[0], b_near[1], b))] + [second_ring()]
    )
    mine = slot(a, b, whole)
    for m in range(out.shape[0]):
        out[m, :, half * 128:(half + 1) * 128] = mine[m]


def sum_all(net, values, box, out, start=0.0, unit=2.5):
    out[...] = values[...]
    me = net.me
    count = 0
    for axis in ("z", "y", "x", "k"):
        for turn in range(1 if axis == "k" else 2):
            if axis == "k":
                partner = net.near("k", 1)
            else:
                step = 1 - 2 * lax.rem(me[axis] + turn, 2)
                partner = net.near(axis, step)
            copy = net.send(out, box.at[count], partner, later=False)
            count += 1
            yield start + unit * count
            copy.wait()
            out[...] = out[...] + box[count - 1]


ANY = pl.BlockSpec(memory_space=pl.ANY)
VMEM = pl.BlockSpec(memory_space=pltpu.VMEM)


def comm_kernel(name, number, body, args, in_specs, outs, out_specs, scratch, copies, local, axes, flops=0):
    def kernel(*refs):
        main, sems = refs[:-3], refs[-3:]
        net = Net(*sems)
        net.barrier(axes)
        run(body(net, *main))
        net.finish()
        assert net.count <= copies and net.local_count <= local, (net.count, net.local_count)

    return pl.pallas_call(
        kernel,
        out_shape=outs,
        in_specs=in_specs,
        out_specs=out_specs,
        scratch_shapes=list(scratch)
        + [pltpu.SemaphoreType.DMA((copies,)), pltpu.SemaphoreType.DMA((copies,)), pltpu.SemaphoreType.DMA((local,))],
        compiler_params=pltpu.CompilerParams(
            collective_id=number, has_side_effects=True, vmem_limit_bytes=56 << 20
        ),
        name=name,
    )(*args)


def bf(*shape):
    return jax.ShapeDtypeStruct(shape, BF16)


def gather_call(name, number, rows, weights):
    n, w = len(rows), len(weights)

    def body(net, *refs):
        sources, outs = refs[: n + w], refs[n + w :]
        chains = []
        for i in range(n):
            chains.append(gather_x(net, sources[i], outs[i], start=17.0 * i))
        time = 0.0
        for i in range(n, n + w):
            unit = 2 * sources[i].shape[0] * sources[i].shape[1] * 128 * 2 / 2 / 95e3
            for half in (0, 1):
                chains.append(gather_yz(net, sources[i], outs[i], half, time, unit))
            time += 15 * unit
        return chains

    return comm_kernel(
        name,
        number,
        body,
        (*rows, *weights),
        [ANY] * (n + w),
        [bf(RING, 2, *r.shape) for r in rows] + [bf(v.shape[0], 2, v.shape[1], 2048) for v in weights],
        [ANY] * (n + w),
        [],
        13 * n + 60 * w,
        n + 2 * w,
        ("x", "k", "y", "z") if w else ("x", "k"),
    )


def scatter_call(name, number, rows, weights, small=None):
    n, w = len(rows), len(weights)

    def body(net, *refs):
        ins, refs = refs[: n + w + (small is not None)], refs[n + w + (small is not None) :]
        outs, scratch = refs[: n + w + (small is not None)], list(refs[n + w + (small is not None) :])
        chains = []
        for i in range(n):
            box, hop, land = scratch[:3]
            del scratch[:3]
            chains.append(scatter_x(net, ins[i], box, hop, land, outs[i], start=17.0 * i))
        time = 0.0
        for i in range(n, n + w):
            unit = 2 * outs[i].shape[0] * outs[i].shape[1] * 128 * 2 / 2 / 95e3
            for half in (0, 1):
                chains.append(scatter_yz(net, ins[i], scratch.pop(0), outs[i], half, time, unit))
            time += 30 * unit
        if small is not None:
            chains.append(sum_all(net, ins[-1], scratch.pop(0), outs[-1]))
        return chains

    scratch = []
    for r in rows:
        t, d = r.shape[2:]
        scratch += [pltpu.VMEM((RING, t, d), BF16), pltpu.VMEM((2, t // 2, d), BF16), pltpu.VMEM((2, t, d), BF16)]
    for v in weights:
        scratch += [pltpu.VMEM((15, v.shape[0], v.shape[2], 128), BF16)] * 2
    outs = [jax.ShapeDtypeStruct(r.shape[2:], F32) for r in rows]
    outs += [bf(v.shape[0], v.shape[2], 256) for v in weights]
    args = [*rows, *weights]
    if small is not None:
        args.append(small)
        outs.append(jax.ShapeDtypeStruct(small.shape, F32))
        scratch.append(pltpu.VMEM((7, *small.shape), F32))
    return comm_kernel(
        name,
        number,
        body,
        args,
        [VMEM] * len(args),
        outs,
        [VMEM] * len(outs),
        scratch,
        10 * n + 60 * w + 7,
        1,
        ("x", "k", "y", "z"),
    )


def dot_nt(left, right):
    return lax.dot_general(left, right, (((1,), (1,)), ((), ())), preferred_element_type=F32)


def dot_tn(left, right):
    return lax.dot_general(left, right, (((0,), (0,)), ((), ())), preferred_element_type=F32)


def dot_nn(left, right):
    return lax.dot_general(left, right, (((1,), (0,)), ((), ())), preferred_element_type=F32)


def norm_scale(values):
    return lax.rsqrt(jnp.mean(values * values, axis=1, keepdims=True) + NORM_EPS)


def norm_backward(incoming, normalized, scale, gain):
    scaled = incoming * gain
    return scale * (scaled - normalized * jnp.mean(scaled * normalized, axis=1, keepdims=True))


def adam_update(weight, gradient, first, second, step_rate, decay_rate):
    first_new = BETA_ONE * first + (1.0 - BETA_ONE) * gradient
    second_new = BETA_TWO * second + (1.0 - BETA_TWO) * gradient * gradient
    first_hat = first_new / (1.0 - BETA_ONE**STEP)
    second_hat = second_new / (1.0 - BETA_TWO**STEP)
    weight_new = weight - step_rate * (
        first_hat / (jnp.sqrt(second_hat) + ADAM_EPS) + decay_rate * weight
    )
    return (weight_new, first_new, second_new)


def body(
    tokens,
    cotangent,
    doc_starts,
    mixer_w,
    ffn_w,
    gains,
    taps,
    mixer_m,
    mixer_v,
    ffn_m,
    ffn_v,
    gain_m,
    gain_v,
    tap_m,
    tap_v,
):
    width = tokens.shape[1]
    own = tokens.shape[0]
    col, row = lax.axis_index("col"), lax.axis_index("row")
    z_hi = (col // 2) % 2
    run_tokens = 2 * own
    group = RING * run_tokens
    mixer_low = jnp.swapaxes(mixer_w.astype(BF16), 1, 2)
    ffn_low = jnp.swapaxes(ffn_w.astype(BF16), 1, 2)
    partner = [(i, i ^ 2) for i in range(16)]

    def swap(values):
        return lax.ppermute(values, "col", partner)

    taps_other = swap(taps)
    low_taps = jnp.where(z_hi == 0, taps, taps_other)
    high_taps = jnp.where(z_hi == 0, taps_other, taps)
    taps_all = jnp.concatenate([low_taps, high_taps], axis=1)

    scale_one = norm_scale(tokens)
    normal_one = tokens * scale_one
    normed = (normal_one * gains[0]).astype(BF16)
    normed_all, cot_all, mixer_all, gate_w = gather_call(
        "gather_normed_cotangent_mixer_gate",
        0,
        [normed, cotangent.astype(BF16)],
        [mixer_low, ffn_low[0:1]],
    )
    normed_all = normed_all.reshape(group, width)
    cot_all = cot_all.reshape(group, width)
    channels = 2 * mixer_low.shape[1]
    hidden_units = 2 * ffn_low.shape[1]
    mixer_all = mixer_all.reshape(4, channels, width)
    projected = dot_nt(normed_all, mixer_all[:3].reshape(3 * channels, width))
    input_gate = projected[:, :channels]
    output_gate = projected[:, channels : 2 * channels]
    conv_input = projected[:, 2 * channels :]
    mixed_bx = input_gate * conv_input
    runs = mixed_bx.reshape(RING, run_tokens, channels)
    ends = runs[:, run_tokens - 2 :]
    ends_near = swap(ends)
    def index(r, c):
        return r * 16 + c

    back = [
        (index(r, x * 4 + 2 + k), index(r + 1, x * 4 + k)) for r in range(7) for x in range(4) for k in range(2)
    ]
    ends_far = lax.ppermute(ends[3:], ("row", "col"), back)
    before = jnp.where(z_hi == 1, ends_near, jnp.concatenate([ends_far, ends_near[:3]], axis=0))
    extended = jnp.concatenate([before, runs], axis=1)
    places = (
        row * (2 * group)
        + jnp.arange(RING, dtype=jnp.int32)[:, None] * (2 * run_tokens)
        + z_hi * run_tokens
        + jnp.arange(-2, run_tokens + 2, dtype=jnp.int32)[None, :]
    )
    start_flags = jnp.any(places[:, :, None] == doc_starts[None, None, :], axis=2)
    keep_all = jnp.where(start_flags, 0.0, 1.0).astype(F32)[:, :, None]
    pair_all = keep_all[:, 1:] * keep_all[:, :-1]
    lag_one = (keep_all[:, 2 : 2 + run_tokens] * extended[:, 1 : 1 + run_tokens]).reshape(group, channels)
    lag_two = (pair_all[:, 1 : 1 + run_tokens] * extended[:, :run_tokens]).reshape(group, channels)
    convolved = taps_all[2] * mixed_bx + taps_all[1] * lag_one + taps_all[0] * lag_two
    gated_out = (output_gate * convolved).astype(BF16)
    partial_out = dot_nn(gated_out, mixer_all[3]).astype(BF16)
    (mixed_out,) = scatter_call(
        "scatter_out", 1, [partial_out.reshape(RING, 2, own, width)], []
    )
    residual = tokens + mixed_out
    scale_two = norm_scale(residual)
    normal_two = residual * scale_two
    ffn_in = (normal_two * gains[1]).astype(BF16)
    ffn_in_all, up_down = gather_call("gather_ffn_in_up_down", 2, [ffn_in], [ffn_low[1:3]])
    ffn_in_all = ffn_in_all.reshape(group, width)
    gate_w = gate_w.reshape(hidden_units, width)
    up_down = up_down.reshape(2, hidden_units, width)
    gate_proj = dot_nt(ffn_in_all, gate_w)
    up_proj = dot_nt(ffn_in_all, up_down[0])
    sigmoid_gate = jax.nn.sigmoid(gate_proj)
    activated = gate_proj * sigmoid_gate
    hidden = (activated * up_proj).astype(BF16)
    down_part = dot_nn(hidden, up_down[1]).astype(BF16)
    grad_hidden = dot_nt(cot_all, up_down[1])
    grad_gate = (grad_hidden * up_proj * sigmoid_gate * (1.0 + gate_proj * (1.0 - sigmoid_gate))).astype(BF16)
    grad_up = (grad_hidden * activated).astype(BF16)
    gate_part = dot_tn(grad_gate, ffn_in_all)
    up_part = dot_tn(grad_up, ffn_in_all)
    down_grad_part = dot_tn(hidden, cot_all).astype(BF16)
    gain_two_part = (
        jnp.sum(gate_part * gate_w.astype(F32) + up_part * up_down[0].astype(F32), axis=0) / gains[1]
    )
    grad_ffn_part = (dot_nn(grad_gate, gate_w) + dot_nn(grad_up, up_down[0])).astype(BF16)
    half_units = hidden_units // 2
    gate_up_part = jnp.stack([gate_part.astype(BF16), up_part.astype(BF16)]).reshape(2, 2, half_units, width)
    ffn_out, grad_ffn_in, gate_up_grad = scatter_call(
        "scatter_down_ffn_in_gate_up",
        3,
        [down_part.reshape(RING, 2, own, width), grad_ffn_part.reshape(RING, 2, own, width)],
        [gate_up_part],
    )
    output = residual + ffn_out
    grad_residual = cotangent + norm_backward(grad_ffn_in, normal_two, scale_two, gains[1])
    (residual_grad_all,) = gather_call("gather_residual_grad", 4, [grad_residual.astype(BF16)], [])
    residual_grad_all = residual_grad_all.reshape(group, width)
    grad_gated = dot_nt(residual_grad_all, mixer_all[3])
    output_part = dot_tn(gated_out, residual_grad_all)
    grad_conv = grad_gated * output_gate
    grad_output_gate = grad_gated * convolved
    conv_runs = grad_conv.reshape(RING, run_tokens, channels)
    heads = conv_runs[:, :2]
    heads_near = swap(heads)
    forth = [
        (index(r + 1, x * 4 + k), index(r, x * 4 + 2 + k)) for r in range(7) for x in range(4) for k in range(2)
    ]
    heads_far = lax.ppermute(heads[:1], ("row", "col"), forth)
    after = jnp.where(z_hi == 0, heads_near, jnp.concatenate([heads_near[1:], heads_far], axis=0))
    ahead_rows = jnp.concatenate([conv_runs, after], axis=1)
    grad_mixed = (
        taps_all[2] * conv_runs
        + taps_all[1] * keep_all[:, 3 : 3 + run_tokens] * ahead_rows[:, 1 : 1 + run_tokens]
        + taps_all[0] * pair_all[:, 3 : 3 + run_tokens] * ahead_rows[:, 2 : 2 + run_tokens]
    ).reshape(group, channels)
    tap_part = jnp.stack(
        [
            jnp.sum(grad_conv * lag_two, axis=0),
            jnp.sum(grad_conv * lag_one, axis=0),
            jnp.sum(grad_conv * mixed_bx, axis=0),
        ]
    )
    grad_proj = jnp.concatenate(
        [grad_mixed * conv_input, grad_output_gate, grad_mixed * input_gate], axis=1
    ).astype(BF16)
    input_part = dot_tn(grad_proj, normed_all)
    in_w = mixer_all[:3].reshape(3 * channels, width)
    gain_one_part = jnp.sum(input_part * in_w.astype(F32), axis=0) / gains[0]
    grad_normed_part = dot_nn(grad_proj, in_w).astype(BF16)
    mixer_part = jnp.concatenate([input_part, output_part], axis=0).astype(BF16)
    tap_placed = lax.dynamic_update_slice(
        jnp.zeros((3, 8, channels), F32), tap_part[:, None], (0, (col // 4) * 2 + col % 2, 0)
    ).reshape(3, width)
    small = jnp.concatenate(
        [gain_one_part[None], gain_two_part[None], tap_placed, jnp.zeros((3, width), F32)], axis=0
    )
    grad_normed, mixer_grad, down_grad, total = scatter_call(
        "scatter_normed_mixer_down",
        5,
        [grad_normed_part.reshape(RING, 2, own, width)],
        [
            mixer_part.reshape(4, 2, channels // 2, width),
            down_grad_part.reshape(1, 2, half_units, width),
        ],
        small,
    )
    input_grad = grad_residual + norm_backward(grad_normed, normal_one, scale_one, gains[0])
    mixer_grad = jnp.swapaxes(mixer_grad, 1, 2).astype(F32)
    ffn_grad = jnp.swapaxes(jnp.concatenate([gate_up_grad, down_grad], axis=0), 1, 2).astype(F32)
    gain_grad = total[:2]
    tap_grad = lax.dynamic_slice_in_dim(
        total[2:5], ((col // 4) * 2 + col % 2) * channels + z_hi * (channels // 2), channels // 2, 1
    )
    mixer_new, mixer_m_new, mixer_v_new = adam_update(
        mixer_w, mixer_grad, mixer_m, mixer_v, MATRIX_RATE, MATRIX_DECAY
    )
    ffn_new, ffn_m_new, ffn_v_new = adam_update(
        ffn_w, ffn_grad, ffn_m, ffn_v, MATRIX_RATE, MATRIX_DECAY
    )
    gain_new, gain_m_new, gain_v_new = adam_update(
        gains, gain_grad, gain_m, gain_v, SMALL_RATE, 0.0
    )
    tap_new, tap_m_new, tap_v_new = adam_update(taps, tap_grad, tap_m, tap_v, SMALL_RATE, 0.0)
    return (
        output,
        input_grad,
        mixer_grad,
        mixer_new,
        mixer_m_new,
        mixer_v_new,
        ffn_grad,
        ffn_new,
        ffn_m_new,
        ffn_v_new,
        gain_grad,
        gain_new,
        gain_m_new,
        gain_v_new,
        tap_grad,
        tap_new,
        tap_m_new,
        tap_v_new,
    )


def solution(mesh):
    placed = (
        P(("row", "col"), None),
        P(("row", "col"), None),
        P(),
        P(None, "row", "col"),
        P(None, "row", "col"),
        P(),
        P(None, "col"),
        P(None, "row", "col"),
        P(None, "row", "col"),
        P(None, "row", "col"),
        P(None, "row", "col"),
        P(),
        P(),
        P(None, "col"),
        P(None, "col"),
    )
    return jax.shard_map(
        body,
        mesh=mesh,
        in_specs=placed,
        out_specs=(
            P(("row", "col"), None),
            P(("row", "col"), None),
            P(None, "row", "col"),
            P(None, "row", "col"),
            P(None, "row", "col"),
            P(None, "row", "col"),
            P(None, "row", "col"),
            P(None, "row", "col"),
            P(None, "row", "col"),
            P(None, "row", "col"),
            P(),
            P(),
            P(),
            P(),
            P(None, "col"),
            P(None, "col"),
            P(None, "col"),
            P(None, "col"),
        ),
        check_vma=False,
    )
```

```python
import jax
import jax.numpy as jnp
from jax import lax
from jax.experimental import pallas as pl
from jax.experimental.pallas import tpu as pltpu
from jax.sharding import PartitionSpec as P

STEP = 5


NORM_EPS = 1e-05
BETA_ONE = 0.9
BETA_TWO = 0.95
ADAM_EPS = 1e-08
MATRIX_DECAY = 0.1
MATRIX_RATE = 0.03
SMALL_RATE = 0.3

MESH = pl.DeviceIdType.MESH
BF16 = jnp.bfloat16
F32 = jnp.float32
RING = 4
PACE = "_sent"
ROWS = 8
LINK = 46.5e3
CORES = 280e3


def place():
    row, col = lax.axis_index("row"), lax.axis_index("col")
    return {"x": col // 4, "y": row // 2, "z": (col // 2) % 2 * 2 + row % 2, "k": col % 2}


def device_at(at):
    return (at["y"] * 2 + at["z"] % 2, at["x"] * 4 + at["z"] // 2 * 2 + at["k"])


def wrap(value, length=RING):
    return lax.rem(value + length, length)


class Work:
    def __init__(self, send_sems, recv_sems, local_sems):
        self.me = place()
        self.send_sems, self.recv_sems, self.local_sems = send_sems, recv_sems, local_sems
        self.sent, self.local = [], []
        self.count = self.local_count = 0
        self.now, self.free, self.due, self.flags, self.chains = 0.0, {}, {}, set(), []

    def near(self, axis, step):
        at = dict(self.me)
        at[axis] = wrap(at[axis] + step, 2 if axis == "k" else RING)
        return device_at(at)

    def target(self, way):
        axis, step = way
        if axis == "row":
            row, col = lax.axis_index("row"), lax.axis_index("col")
            return (wrap(row + step, ROWS), col + 2 - 4 * ((col // 2) % 2))
        return self.near(axis, step)

    def barrier(self, ways):
        sem = pltpu.get_barrier_semaphore()
        for axis, step in ways:
            pl.semaphore_signal(sem, inc=1, device_id=self.target((axis, -step)), device_id_type=MESH)
        pl.semaphore_wait(sem, len(ways))

    def send(self, source, target, way):
        copy = pltpu.make_async_remote_copy(
            src_ref=source,
            dst_ref=target,
            send_sem=self.send_sems.at[self.count],
            recv_sem=self.recv_sems.at[self.count],
            device_id=self.target(way),
            device_id_type=MESH,
        )
        copy.start()
        self.count += 1
        self.sent.append(copy)
        size = 1
        for extent in source.shape:
            size *= extent
        size *= jnp.dtype(source.dtype).itemsize
        begin = max(self.now, self.free.get(way, 0.0))
        self.free[way] = begin + size / (CORES if way[0] == "k" else LINK)
        self.due[id(copy)] = self.free[way] + (1.0 if way[0] == "k" else 2.0)
        return copy

    def copy(self, source, target, rate=1.4e6):
        copy = pltpu.make_async_copy(source, target, self.local_sems.at[self.local_count])
        copy.start()
        self.local_count += 1
        size = 1
        for extent in source.shape:
            size *= extent
        size *= jnp.dtype(source.dtype).itemsize
        begin = max(self.now, self.free.get("local", 0.0))
        self.free["local"] = begin + size / rate
        self.due[id(copy)] = self.free["local"] + 0.5
        self.local.append(copy)
        return copy

    def add(self, chain, rank=0):
        self.chains.append([next(chain), rank, len(self.chains), chain])

    def set(self, flag):
        self.flags.add(flag)

    def run(self):
        while self.chains:
            best, when = None, None
            for entry in self.chains:
                wish = entry[0]
                if isinstance(wish, str):
                    if wish not in self.flags:
                        continue
                    key = (0 if entry[1] == 0 else 1, entry[1], self.now, entry[2])
                elif isinstance(wish, float):
                    key = (0 if entry[1] == 0 else 1, entry[1], self.now, entry[2])
                else:
                    due = self.due[id(wish)]
                    if due <= self.now:
                        key = (0 if entry[1] == 0 else 1, entry[1], due, entry[2])
                    else:
                        key = (2, due, entry[1], entry[2])
                if best is None or key < when:
                    best, when = entry, key
            assert best is not None, self.flags
            wish = best[0]
            if not isinstance(wish, (str, float)):
                self.now = max(self.now, self.due[id(wish)]) + 0.05
                if any(wish is copy for copy in self.local):
                    wish.wait()
                    self.local = [copy for copy in self.local if copy is not wish]
                else:
                    wish.wait_recv()
            try:
                best[0] = next(best[3])
                if isinstance(best[0], float):
                    self.now += best[0]
            except StopIteration:
                self.chains = [entry for entry in self.chains if entry is not best]
        for copy in self.sent:
            copy.wait_send()
        for copy in self.local:
            copy.wait()


def gather_x(work, source, out, name, copy=False, hold=None):
    x, k = work.me["x"], work.me["k"]
    rows = source.shape[0]
    half = rows // 2
    low, high = pl.ds(0, half), pl.ds(half, half)
    right, left, other = ("x", 1), ("x", -1), ("k", 1)
    ahead, behind, across = wrap(x + 1), wrap(x - 1), wrap(x + 2)
    yield name + "_go"
    r0 = work.send(source.at[low], out.at[x, k, low], right)
    l1 = work.send(source.at[high], out.at[x, k, high], left)
    r1 = work.send(source.at[high], out.at[x, k, high], right)
    l0 = work.send(source.at[low], out.at[x, k, low], left)
    sib = [work.send(source, out.at[x, k], other)]
    if copy:
        work.copy(source, out.at[x, k])
    work.set(name + "_sent")

    def relay(at, part):
        sib.append(work.send(out.at[at, k, part], out.at[at, k, part], other))

    if hold is not None:
        yield hold
    yield r0
    far0 = work.send(out.at[behind, k, low], out.at[behind, k, low], right)
    relay(behind, low)
    yield l1
    far1 = work.send(out.at[ahead, k, high], out.at[ahead, k, high], left)
    relay(ahead, high)
    work.set(name + "_far")
    yield r1
    relay(behind, high)
    yield l0
    relay(ahead, low)
    yield far0
    relay(across, low)
    yield far1
    relay(across, high)
    for number, one in enumerate(sib):
        yield one
        if number == 0:
            work.set(name + "_own")
        if number == 4:
            work.set(name + "_near")
    work.set(name + "_all")


def add_into(target, first, second):
    rows = target.shape[-2]
    lead = target.shape[:-2]
    strip = 16

    def body(step, _):
        at = pl.ds(pl.multiple_of(step * strip, strip), strip)
        for m in range(lead[0] if lead else 1):
            here = (m, at) if lead else (at,)
            target[here] = (first[here].astype(F32) + second[here].astype(F32)).astype(BF16)
        return 0

    lax.fori_loop(0, rows // strip, body, 0)


def ring_places(x):
    return (wrap(x + 2), wrap(x + 1), wrap(x - 1), x)


def scatter_x(work, parts, box, hop, land, name):
    x, k = work.me["x"], work.me["k"]
    rows = box.shape[1]
    half = rows // 2
    low, high = pl.ds(0, half), pl.ds(half, half)
    right, left, other = ("x", 1), ("x", -1), ("k", 1)
    across, ahead, behind, own = ring_places(x)

    def swap():
        sib = {}
        for number, at in enumerate((across, ahead, behind, own)):
            yield name + str(number)
            sib[number] = work.send(parts.at[at, 1 - k], box.at[at], other)
            got.append(sib[number])
            work.set(name + "_swap" + str(number))

    got = []
    work.add(swap(), 0)
    yield name + "_swap0"
    yield got[0]
    add_into(box.at[across], parts.at[across, k], box.at[across])
    far0 = work.send(box.at[across, low], hop.at[0], right)
    far1 = work.send(box.at[across, high], hop.at[1], left)
    yield 0.3
    yield name + "_swap1"
    yield got[1]
    add_into(box.at[ahead], parts.at[ahead, k], box.at[ahead])
    r1 = work.send(box.at[ahead, high], land.at[0, high], right)
    yield 0.3
    yield name + "_swap2"
    yield got[2]
    add_into(box.at[behind], parts.at[behind, k], box.at[behind])
    l0 = work.send(box.at[behind, low], land.at[1, low], left)
    yield 0.3
    yield far0
    add_into(box.at[ahead, low], box.at[ahead, low], hop.at[0])
    r0 = work.send(box.at[ahead, low], land.at[0, low], right)
    yield 0.15
    yield far1
    add_into(box.at[behind, high], box.at[behind, high], hop.at[1])
    l1 = work.send(box.at[behind, high], land.at[1, high], left)
    work.set(name + "_sent")
    yield 0.15
    yield name + "_swap3"
    yield got[3]
    for copy in (r1, l0, r0, l1):
        yield copy
    work.set(name + "_done")


def block(ref, y, z, half, rows):
    column = pl.multiple_of((y * 2 + z % 2) * 256 + half * 128, 128)
    return ref.at[:, z // 2, rows, pl.ds(column, 128)]


def gather_yz(work, source, out, half, name):
    first, second = ("y", "z") if half == 0 else ("z", "y")
    rows = source.shape[1]
    cut = rows // 2
    low, high, whole = pl.ds(0, cut), pl.ds(cut, cut), pl.ds(0, rows)
    a, b = work.me[first], work.me[second]

    def slot(at_a, at_b, part):
        y, z = (at_a, at_b) if half == 0 else (at_b, at_a)
        return block(out, y, z, half, part)

    columns = pl.ds(half * 128, 128)
    up, down, forward, backward = (first, 1), (first, -1), (second, 1), (second, -1)
    a_behind, a_ahead, a_across = wrap(a - 1), wrap(a + 1), wrap(a + 2)
    b_behind, b_ahead = wrap(b - 1), wrap(b + 1)
    yield name + "_go" + str(half)
    mine = work.copy(source.at[:, :, columns], slot(a, b, whole))
    r0 = work.send(source.at[:, low, columns], slot(a, b, low), up)
    l1 = work.send(source.at[:, high, columns], slot(a, b, high), down)
    r1 = work.send(source.at[:, high, columns], slot(a, b, high), up)
    l0 = work.send(source.at[:, low, columns], slot(a, b, low), down)
    waits, last = [], []

    def spread(at, part, ref=None):
        ref = slot(at, b, part) if ref is None else ref
        waits.append(
            (
                at,
                part,
                work.send(ref, slot(at, b, part), forward),
                work.send(ref, slot(at, b, part), backward),
            )
        )

    def onward(number):
        at, part, plus, minus = waits[number]
        yield plus
        if part is low:
            last.append(work.send(slot(at, b_behind, part), slot(at, b_behind, part), forward))
        yield minus
        if part is high:
            last.append(work.send(slot(at, b_ahead, part), slot(at, b_ahead, part), backward))

    spread(a, low, source.at[:, low, columns])
    spread(a, high, source.at[:, high, columns])
    yield r0
    f0 = work.send(slot(a_behind, b, low), slot(a_behind, b, low), up)
    spread(a_behind, low)
    yield l1
    f1 = work.send(slot(a_ahead, b, high), slot(a_ahead, b, high), down)
    spread(a_ahead, high)
    yield from onward(0)
    yield r1
    spread(a_behind, high)
    yield l0
    spread(a_ahead, low)
    yield from onward(1)
    yield f0
    spread(a_across, low)
    yield f1
    spread(a_across, high)
    work.set(name + "_spread" + str(half))
    for number in range(2, 8):
        yield from onward(number)
        if number == 5:
            work.set(name + "_most" + str(half))
    work.set(name + "_sent" + str(half))
    for copy in last:
        yield copy
    yield mine
    work.set(name + "_all" + str(half))


def scatter_yz(work, parts, box, out, half, name):
    first, second = ("z", "y") if half == 0 else ("y", "z")
    rows = out.shape[1]
    cut = rows // 2
    low, high, whole = pl.ds(0, cut), pl.ds(cut, cut), pl.ds(0, rows)
    a, b = work.me[first], work.me[second]
    key = name + str(half)

    def slot(at_a, at_b, part):
        y, z = (at_b, at_a) if half == 0 else (at_a, at_b)
        return block(parts, y, z, half, part)

    across, ahead, behind, own = ring_places(a)
    up, down = (first, 1), (first, -1)

    def first_ring(number, at_b):
        base = 3 * number
        pick = lambda at, part: slot(at, at_b, part)
        yield name + "_go" + str(half)
        far0 = work.send(pick(across, low), box.at[base, :, low], up)
        far1 = work.send(pick(across, high), box.at[base, :, high], down)
        r1 = work.send(pick(ahead, high), box.at[base + 1, :, high], up)
        l0 = work.send(pick(behind, low), box.at[base + 2, :, low], down)
        yield far0
        add_into(pick(ahead, low), pick(ahead, low), box.at[base, :, low])
        r0 = work.send(pick(ahead, low), box.at[base + 1, :, low], up)
        yield far1
        add_into(pick(behind, high), pick(behind, high), box.at[base, :, high])
        l1 = work.send(pick(behind, high), box.at[base + 2, :, high], down)
        yield r1
        add_into(pick(own, high), pick(own, high), box.at[base + 1, :, high])
        yield l0
        add_into(pick(own, low), pick(own, low), box.at[base + 2, :, low])
        yield r0
        add_into(pick(own, low), pick(own, low), box.at[base + 1, :, low])
        yield l1
        add_into(pick(own, high), pick(own, high), box.at[base + 2, :, high])
        work.set(key + "_first" + str(number))

    places = ring_places(b)
    for number, at_b in enumerate(places):
        work.add(first_ring(number, at_b))
    b_across, b_ahead, b_behind, b_own = places
    forward, backward = (second, 1), (second, -1)
    yield key + "_first0"
    far0 = work.send(slot(a, b_across, low), box.at[12, :, low], forward)
    far1 = work.send(slot(a, b_across, high), box.at[12, :, high], backward)
    yield key + "_first1"
    r1 = work.send(slot(a, b_ahead, high), box.at[13, :, high], forward)
    yield far0
    add_into(slot(a, b_ahead, low), slot(a, b_ahead, low), box.at[12, :, low])
    r0 = work.send(slot(a, b_ahead, low), box.at[13, :, low], forward)
    yield key + "_first2"
    l0 = work.send(slot(a, b_behind, low), box.at[14, :, low], backward)
    yield far1
    add_into(slot(a, b_behind, high), slot(a, b_behind, high), box.at[12, :, high])
    l1 = work.send(slot(a, b_behind, high), box.at[14, :, high], backward)
    yield key + "_first3"
    mine = slot(a, b_own, whole)
    for copy in (r1, r0, l0, l1):
        yield copy
    for m in range(out.shape[0]):
        total = mine[m].astype(F32) + box[13, m].astype(F32) + box[14, m].astype(F32)
        out[m, :, half * 128 : (half + 1) * 128] = total.astype(out.dtype)
    work.set(key + "_done")


def sum_all(work, values, box, out, name):
    yield name + "_go"
    out[...] = values[...]
    me = work.me
    for turn, axis in enumerate(("z", "y", "x", "k")):
        length = 2 if axis == "k" else RING
        mine = box.at[turn, me[axis]]
        mine[...] = out[...]
        copies = [work.send(mine, mine, (axis, step)) for step in range(1, length)]
        for copy in copies:
            yield copy
        total = box[turn, 0]
        for number in range(1, length):
            total = total + box[turn, number]
        out[...] = total
    work.set(name + "_done")


ANY = pl.BlockSpec(memory_space=pl.ANY)
VMEM = pl.BlockSpec(memory_space=pltpu.VMEM)
SMEM = pl.BlockSpec(memory_space=pltpu.SMEM)
X_WAYS = (("x", 1), ("x", -1), ("k", 1))
YZ_WAYS = (("y", 1), ("y", -1), ("z", 1), ("z", -1))


def bf(*shape):
    return jax.ShapeDtypeStruct(shape, BF16)


def fl(*shape):
    return jax.ShapeDtypeStruct(shape, F32)


def call(name, number, body, args, outs, scratch, copies, local, ways, flops):
    def kernel(*refs):
        main, sems = refs[:-3], refs[-3:]
        work = Work(*sems)
        work.barrier(ways)
        body(work, *main)
        work.run()
        assert work.count <= copies and work.local_count <= local, (work.count, work.local_count)

    sems = [pltpu.SemaphoreType.DMA((copies,)), pltpu.SemaphoreType.DMA((copies,)), pltpu.SemaphoreType.DMA((local,))]
    return pl.pallas_call(
        kernel,
        out_shape=[shape for shape, _ in outs],
        in_specs=[spec for _, spec in args],
        out_specs=[spec for _, spec in outs],
        scratch_shapes=list(scratch) + sems,
        compiler_params=pltpu.CompilerParams(
            collective_id=number, has_side_effects=True, vmem_limit_bytes=60 << 20
        ),
        cost_estimate=pl.CostEstimate(flops=flops, bytes_accessed=40 << 20, transcendentals=0),
        name=name,
    )(*[array for array, _ in args])


def dot_nt(left, right):
    return lax.dot_general(left, right, (((1,), (1,)), ((), ())), preferred_element_type=F32)


def dot_tn(left, right):
    return lax.dot_general(left, right, (((0,), (0,)), ((), ())), preferred_element_type=F32)


def dot_nn(left, right):
    return lax.dot_general(left, right, (((1,), (0,)), ((), ())), preferred_element_type=F32)


def strips(rows, strip, body):
    def one(step, _):
        body(pl.ds(pl.multiple_of(step * strip, strip), strip))
        return 0

    lax.fori_loop(0, rows // strip, one, 0)


def keeps(starts, first, shape):
    places = first + lax.broadcasted_iota(jnp.int32, shape, 0)

    def keep(at):
        hit = at == starts[0]
        for number in range(1, 4):
            hit = jnp.logical_or(hit, at == starts[number])
        return jnp.where(hit, 0.0, 1.0).astype(F32)

    here = keep(places)
    return here, here * keep(places - 1)


def run_start(run, run_tokens):
    row, col = lax.axis_index("row"), lax.axis_index("col")
    return ((row * RING + run) * 2 + (col // 2) % 2) * run_tokens


SHARD, WIDTH = 128, 2048
RUN = 2 * SHARD
CH, HALF = 256, 128
HID = 352


def lags(ext, starts, run, at, lane):
    rows = 64
    lanes = slice(lane * HALF, (lane + 1) * HALF)
    one, two = keeps(starts, run_start(run, RUN) + at, (rows, HALF))
    mixed = ext[run, 8 + at : 8 + at + rows, lanes]
    return mixed, one * ext[run, 7 + at : 7 + at + rows, lanes], two * ext[run, 6 + at : 6 + at + rows, lanes]


def place_halo(ext, near, far):
    row, col = lax.axis_index("row"), lax.axis_index("col")
    late = (col // 2) % 2 == 1
    first = jnp.where(row > 0, far[...], 0.0)
    for run in range(RING):
        ext[run, 0:8] = jnp.where(late, near[run], first if run == 0 else near[run - 1])


def forward_mixer(tokens, cotangent, starts, mixer, ffn, gains, taps):
    def body(
        work, tokens, cotangent, starts, mixer, ffn, gains, taps,
        normed_out, cot_out, in_out, mix_out, ffn_out, proj_out, near_out, far_out, taps_out, residual, ffn_in_out,
        normed, weights, proj, ext, gated, parts, box, hop, land, cot, ffn_in,
    ):
        x, k = work.me["x"], work.me["k"]
        col = lax.axis_index("col")
        z_hi = (col // 2) % 2
        w_in, w_out = weights.at[0:3], weights.at[3:4]

        def opening():
            def norm(at):
                rows = tokens[at]
                scale = lax.rsqrt(jnp.mean(rows * rows, axis=1, keepdims=True) + NORM_EPS)
                normed[x, k, at] = (rows * scale * gains[0:1]).astype(BF16)

            strips(SHARD, 16, norm)
            work.set("normed_go")
            work.set("in_go0")
            work.set("in_go1")
            yield 1.0

            def cast(at):
                cot[at] = cotangent[at].astype(BF16)

            strips(SHARD, 16, cast)
            taps_out[z_hi] = taps[...]
            work.send(taps, taps_out.at[z_hi], ("z", 2))
            taps_copy.append(work.sent[-1])
            work.set("taps_sent")
            yield 0.5

        taps_copy = []

        def compute():
            yield "taps_sent"
            yield taps_copy[0]
            yield "normed_all"
            work.copy(normed, normed_out)
            yield "in_all0"
            yield "in_all1"
            tail = normed[:, 1, SHARD - 16 :].reshape(RING * 16, WIDTH)
            ends = dot_nt(tail, weights[0:3].reshape(3 * CH, WIDTH))
            mixed = (ends[:, :CH] * ends[:, 2 * CH :]).reshape(RING, 16, CH)
            ext[:, RUN - 8 : RUN + 8] = mixed
            sent = [
                work.send(ext.at[:, RUN : RUN + 8], near_out, ("z", 2)),
                work.send(ext.at[RING - 1, RUN : RUN + 8], far_out, ("row", 1)),
            ]
            yield 1.0

            def project(half, _):
                rows = normed[pl.ds(2 * half, 2)].reshape(2 * RUN, WIDTH)
                out = dot_nt(rows, weights[0:3].reshape(3 * CH, WIDTH))
                proj[pl.ds(2 * half, 2)] = out.reshape(2, RUN, 3 * CH)
                return 0

            lax.fori_loop(0, 2, project, 0)
            work.copy(proj, proj_out)
            yield 4.0

            def mix(run, _):
                for at in range(0, RUN, 64):
                    size = 64 if at + 64 < RUN else 56
                    rows = proj[run, at : at + size]
                    ext[run, 8 + at : 8 + at + size] = rows[:, :CH] * rows[:, 2 * CH :]
                return 0

            lax.fori_loop(0, RING, mix, 0)
            yield 0.7
            for copy in sent:
                yield copy
            place_halo(ext, near_out, far_out)

            def convolve(run, _):
                for at in range(0, RUN, 64):
                    for lane in range(2):
                        mixed, one, two = lags(ext, starts, run, at, lane)
                        tap = taps_out[lane]
                        total = tap[2:3] * mixed + tap[1:2] * one + tap[0:1] * two
                        gate = proj[run, at : at + 64, CH + lane * HALF : CH + (lane + 1) * HALF]
                        gated[run, at : at + 64, lane * HALF : (lane + 1) * HALF] = (gate * total).astype(BF16)
                return 0

            lax.fori_loop(0, RING, convolve, 0)
            yield 1.5
            yield "mix_all0"
            yield "mix_all1"
            work.copy(weights.at[0:3], in_out)
            work.copy(weights.at[3:4], mix_out)
            for number, at in enumerate(ring_places(x)):
                out = dot_nn(gated[at], weights[3].reshape(CH, WIDTH))
                parts[at] = out.astype(BF16).reshape(2, SHARD, WIDTH)
                work.set("out" + str(number))
                yield 0.6
            yield "out_done"

            def close(at):
                total = parts[x, k, at].astype(F32) + box[x, at].astype(F32)
                total = total + (land[0, at].astype(F32) + land[1, at].astype(F32))
                rows = tokens[at] + total
                scale = lax.rsqrt(jnp.mean(rows * rows, axis=1, keepdims=True) + NORM_EPS)
                residual[at] = rows
                ffn_in[at] = (rows * scale * gains[1:2]).astype(BF16)

            strips(SHARD, 16, close)
            yield 1.0
            work.set("ffn_in_go")

        def order():
            yield "normed_far"
            work.set("cot_go")

        def follow(half):
            names = ("in", "mix", "gate", "up", "down")
            for name, after in zip(names[:-1], names[1:]):
                yield name + PACE + str(half)
                work.set(after + "_go" + str(half))

        work.add(opening(), 1)
        work.add(gather_x(work, normed.at[x, k], normed, "normed"))
        for half in (0, 1):
            work.add(gather_yz(work, mixer.at[0:3], w_in, half, "in"))
        for half in (0, 1):
            work.add(gather_yz(work, mixer.at[3:4], w_out, half, "mix"))
        for number, name in enumerate(("gate", "up", "down")):
            for half in (0, 1):
                mat = pl.ds(number, 1)
                work.add(gather_yz(work, ffn.at[mat], ffn_out.at[mat], half, name))
        work.add(scatter_x(work, parts, box, hop, land, "out"))
        work.add(gather_x(work, ffn_in, ffn_in_out, "ffn_in", copy=True))
        work.add(gather_x(work, cot, cot_out, "cot", copy=True, hold="out_sent"), 0)
        work.add(order())
        work.add(follow(0))
        work.add(follow(1))
        work.add(compute(), 1)

    gathered = bf(RING, 2, SHARD, WIDTH)
    return call(
        "forward_mixer",
        0,
        body,
        [
            (tokens, VMEM), (cotangent, VMEM), (starts, SMEM), (mixer, VMEM), (ffn, VMEM), (gains, VMEM), (taps, VMEM),
        ],
        [
            (gathered, ANY), (gathered, ANY), (bf(3, 2, HALF, WIDTH), ANY), (bf(1, 2, HALF, WIDTH), ANY),
            (bf(3, 2, HID, WIDTH), ANY), (fl(RING, RUN, 3 * CH), ANY), (fl(RING, 8, CH), VMEM), (fl(8, CH), VMEM),
            (fl(2, 8, HALF), VMEM), (fl(SHARD, WIDTH), VMEM), (gathered, ANY),
        ],
        [
            pltpu.VMEM((RING, 2, SHARD, WIDTH), BF16),
            pltpu.VMEM((4, 2, HALF, WIDTH), BF16),
            pltpu.VMEM((RING, RUN, 3 * CH), F32),
            pltpu.VMEM((RING, RUN + 8, CH), F32),
            pltpu.VMEM((RING, RUN, CH), BF16),
            pltpu.VMEM((RING, 2, SHARD, WIDTH), BF16),
            pltpu.VMEM((RING, SHARD, WIDTH), BF16),
            pltpu.VMEM((2, SHARD // 2, WIDTH), BF16),
            pltpu.VMEM((2, SHARD, WIDTH), BF16),
            pltpu.VMEM((SHARD, WIDTH), BF16),
            pltpu.VMEM((SHARD, WIDTH), BF16),
        ],
        420,
        24,
        X_WAYS + YZ_WAYS + (("z", 2), ("row", 1)),
        int(5e9),
    )


def feed_forward(ffn_in, cot, ffn, residual, cotangent, gains):
    def body(
        work, ffn_in, cot, ffn, residual, cotangent, gains,
        output, grad_residual, grad_out, ffn_grad, gain_part,
        fa, ca, w, gate, up, hid, gg, gu, gh, grad_low,
        parts_a, box_a, hop_a, land_a, parts_b, box_b, hop_b, land_b, boxes,
    ):
        x, k = work.me["x"], work.me["k"]
        units = 2 * HID

        def mat(number):
            return w[number].reshape(units, WIDTH)

        def weight_grad(number, left, right):
            def columns(step, _):
                at = pl.ds(pl.multiple_of(step * 512, 512), 512)
                rows = right[:, :, :, at].reshape(RING * RUN, 512)
                grad = dot_tn(left[...].reshape(RING * RUN, units), rows)
                w[number, :, :, at] = grad.astype(BF16).reshape(2, HID, 512)
                return 0

            lax.fori_loop(0, WIDTH // 512, columns, 0)

        def compute():
            loads = [work.copy(ffn.at[0], w.at[0]), work.copy(ffn_in.at[0:2], fa.at[0:2])]
            loads += [work.copy(ffn.at[1], w.at[1]), work.copy(ffn_in.at[2:4], fa.at[2:4])]
            loads += [work.copy(ffn.at[2], w.at[2]), work.copy(cot, ca)]

            def activate(pair):
                def one(at):
                    for run in (2 * pair, 2 * pair + 1):
                        value = gate[run, at]
                        active = value * jax.nn.sigmoid(value)
                        hid[run, at] = (active * up[run, at]).astype(BF16)

                strips(RUN, 16, one)

            yield loads[0]
            for pair in (0, 1):
                two = pl.ds(2 * pair, 2)
                yield loads[1 if pair == 0 else 3]
                gate[two] = dot_nt(fa[two].reshape(2 * RUN, WIDTH), mat(0)).reshape(2, RUN, units)
                yield 2.0
                if pair == 0:
                    yield loads[2]
                up[two] = dot_nt(fa[two].reshape(2 * RUN, WIDTH), mat(1)).reshape(2, RUN, units)
                yield 2.0
                activate(pair)
                yield 1.2
            yield loads[4]
            for number, at in enumerate(ring_places(x)):
                parts_a[at] = dot_nn(hid[at], mat(2)).astype(BF16).reshape(2, SHARD, WIDTH)
                work.set("down" + str(number))
                yield 1.1
            yield loads[5]
            for pair in (0, 1):
                gh[...] = dot_nt(ca[pl.ds(2 * pair, 2)].reshape(2 * RUN, WIDTH), mat(2)).reshape(2, RUN, units)
                yield 2.0

                def one(at):
                    for here in (0, 1):
                        run = 2 * pair + here
                        value, grad = gate[run, at], gh[here, at]
                        sig = jax.nn.sigmoid(value)
                        gg[run, at] = (grad * up[run, at] * sig * (1.0 + value * (1.0 - sig))).astype(BF16)
                        gu[run, at] = (grad * (value * sig)).astype(BF16)

                strips(RUN, 16, one)
                yield 1.5
            weight_grad(2, hid, ca)
            for half in (0, 1):
                work.set("dwd_go" + str(half))
            yield 4.0
            for number, at in enumerate(ring_places(x)):
                grad = dot_nn(gg[at], mat(0)) + dot_nn(gu[at], mat(1))
                parts_b[at] = grad.astype(BF16).reshape(2, SHARD, WIDTH)
                work.set("gffn" + str(number))
                yield 2.2
            weight_grad(0, gg, fa)
            for half in (0, 1):
                work.set("dwg_go" + str(half))
            yield 4.0
            weight_grad(1, gu, fa)
            for half in (0, 1):
                work.set("dwu_go" + str(half))
            yield 4.0

        def close_down():
            yield "down_done"

            def one(at):
                total = parts_a[x, k, at].astype(F32) + box_a[x, at].astype(F32)
                total = total + (land_a[0, at].astype(F32) + land_a[1, at].astype(F32))
                output[at] = residual[at] + total

            strips(SHARD, 16, one)
            yield 0.4

        def close_grad():
            yield "gffn_done"
            gain_part[...] = jnp.zeros_like(gain_part)

            def one(at):
                grad = parts_b[x, k, at].astype(F32) + box_b[x, at].astype(F32)
                grad = grad + (land_b[0, at].astype(F32) + land_b[1, at].astype(F32))
                rows = residual[at]
                scale = lax.rsqrt(jnp.mean(rows * rows, axis=1, keepdims=True) + NORM_EPS)
                normal = rows * scale
                gain = grad * normal
                gain_part[...] += gain[:8] + gain[8:]
                scaled = grad * gains[1:2]
                back = scale * (scaled - normal * jnp.mean(scaled * normal, axis=1, keepdims=True))
                total = cotangent[at] + back
                grad_residual[at] = total
                grad_low[at] = total.astype(BF16)

            strips(SHARD, 16, one)
            work.set("grad_go")
            yield 1.5

        work.add(scatter_x(work, parts_a, box_a, hop_a, land_a, "down"))
        work.add(scatter_x(work, parts_b, box_b, hop_b, land_b, "gffn"))
        work.add(gather_x(work, grad_low, grad_out, "grad", copy=True))
        for number, name in ((2, "dwd"), (0, "dwg"), (1, "dwu")):
            here = pl.ds(number, 1)
            for half in (0, 1):
                work.add(
                    scatter_yz(work, w.at[here], boxes.at[2 * number + half], ffn_grad.at[here], half, name)
                )
        work.add(compute(), 2)
        work.add(close_grad(), 1)
        work.add(close_down(), 2)

    gathered = bf(RING, 2, SHARD, WIDTH)
    units = 2 * HID
    group = [
        pltpu.VMEM((RING, 2, SHARD, WIDTH), BF16),
        pltpu.VMEM((RING, SHARD, WIDTH), BF16),
        pltpu.VMEM((2, SHARD // 2, WIDTH), BF16),
        pltpu.VMEM((2, SHARD, WIDTH), BF16),
    ]
    return call(
        "feed_forward",
        1,
        body,
        [(ffn_in, ANY), (cot, ANY), (ffn, ANY), (residual, VMEM), (cotangent, VMEM), (gains, VMEM)],
        [
            (fl(SHARD, WIDTH), VMEM), (fl(SHARD, WIDTH), VMEM), (gathered, ANY), (fl(3, HID, CH), VMEM),
            (fl(8, WIDTH), VMEM),
        ],
        [
            pltpu.VMEM((RING, 2, SHARD, WIDTH), BF16),
            pltpu.VMEM((RING, 2, SHARD, WIDTH), BF16),
            pltpu.VMEM((3, 2, HID, WIDTH), BF16),
            pltpu.VMEM((RING, RUN, units), F32),
            pltpu.VMEM((RING, RUN, units), F32),
            pltpu.VMEM((RING, RUN, units), BF16),
            pltpu.VMEM((RING, RUN, units), BF16),
            pltpu.VMEM((RING, RUN, units), BF16),
            pltpu.VMEM((2, RUN, units), F32),
            pltpu.VMEM((SHARD, WIDTH), BF16),
            *group,
            *group,
            pltpu.VMEM((6, 15, 1, HID, HALF), BF16),
        ],
        240,
        12,
        X_WAYS + YZ_WAYS,
        int(27e9),
    )


def backward_mixer(
    grad_low, normed, w_in, w_out, proj, near, far, taps, starts, tokens, grad_residual, gains, gain_two
):
    def body(
        work, grad_low, normed, w_in, w_out, proj_in, near, far, taps, starts, tokens, grad_residual, gains, gain_two,
        input_grad, mixer_grad, small_out,
        ga, na, w, proj, ext, ahead, conv, gated, gp, near_next, far_next, tap_sum, gain_sum, small,
        parts, box, hop, land, box_mix, box_in, box_small,
    ):
        x, k = work.me["x"], work.me["k"]
        row, col = lax.axis_index("row"), lax.axis_index("col")
        late = (col // 2) % 2 == 1

        def mat_in():
            return w[0:3].reshape(3 * CH, WIDTH)

        def compute():
            loads = [work.copy(proj_in, proj), work.copy(w_out, w.at[3:4]), work.copy(grad_low, ga)]
            loads += [work.copy(w_in, w.at[0:3]), work.copy(normed, na)]
            yield loads[0]

            def mix(run, _):
                for at in range(0, RUN, 64):
                    rows = proj[run, at : at + 64]
                    ext[run, 8 + at : 8 + at + 64] = rows[:, :CH] * rows[:, 2 * CH :]
                return 0

            lax.fori_loop(0, RING, mix, 0)
            place_halo(ext, near, far)

            def convolve(run, _):
                for at in range(0, RUN, 64):
                    for lane in range(2):
                        lanes = slice(lane * HALF, (lane + 1) * HALF)
                        mixed, one, two = lags(ext, starts, run, at, lane)
                        tap = taps[lane]
                        total = tap[2:3] * mixed + tap[1:2] * one + tap[0:1] * two
                        gate = proj[run, at : at + 64, CH + lane * HALF : CH + (lane + 1) * HALF]
                        conv[run, at : at + 64, lanes] = total
                        gated[run, at : at + 64, lanes] = (gate * total).astype(BF16)
                return 0

            lax.fori_loop(0, RING, convolve, 0)
            yield 2.2
            yield loads[1]
            yield loads[2]

            def gate_back(pair, _):
                two = pl.ds(2 * pair, 2)
                grad = dot_nt(ga[two].reshape(2 * RUN, WIDTH), w[3].reshape(CH, WIDTH)).reshape(2, RUN, CH)
                ahead[two, 0:RUN] = grad * proj[two, :, CH : 2 * CH]
                gp[two, :, CH : 2 * CH] = (grad * conv[two]).astype(BF16)
                return 0

            lax.fori_loop(0, 2, gate_back, 0)
            sent = [
                work.send(ahead.at[:, 0:8], near_next, ("z", 2)),
                work.send(ahead.at[0, 0:8], far_next, ("row", -1)),
            ]
            yield 2.5

            def out_grad(step, _):
                at = pl.ds(pl.multiple_of(step * 512, 512), 512)
                rows = ga[:, :, :, at].reshape(RING * RUN, 512)
                grad = dot_tn(gated[...].reshape(RING * RUN, CH), rows)
                w[3, :, :, at] = grad.astype(BF16).reshape(2, HALF, 512)
                return 0

            lax.fori_loop(0, WIDTH // 512, out_grad, 0)
            for half in (0, 1):
                work.set("mix_go" + str(half))
            yield 1.7
            for copy in sent:
                yield copy
            last = jnp.where(row < ROWS - 1, far_next[...], 0.0)
            for run in range(RING):
                after = last if run == RING - 1 else near_next[run + 1]
                ahead[run, RUN : RUN + 8] = jnp.where(late, after, near_next[run])
            tap_sum[...] = jnp.zeros_like(tap_sum)

            def unmix(run, _):
                for at in range(0, RUN, 64):
                    for lane in range(2):
                        lanes = slice(lane * HALF, (lane + 1) * HALF)
                        rows = slice(at, at + 64)
                        first = run_start(run, RUN) + at
                        one, _two = keeps(starts, first + 1, (64, HALF))
                        _one, two = keeps(starts, first + 2, (64, HALF))
                        tap = taps[lane]
                        grad = ahead[run, rows, lanes]
                        mixed, lag_one, lag_two = lags(ext, starts, run, at, lane)
                        for number, value in enumerate((lag_two, lag_one, mixed)):
                            tap_sum[number, :, lanes] += jnp.sum((grad * value).reshape(8, 8, HALF), axis=0)
                        total = tap[2:3] * grad + tap[1:2] * (one * ahead[run, at + 1 : at + 65, lanes])
                        total = total + tap[0:1] * (two * ahead[run, at + 2 : at + 66, lanes])
                        conv_in = proj[run, rows, 2 * CH + lane * HALF : 2 * CH + (lane + 1) * HALF]
                        gate = proj[run, rows, lanes]
                        gp[run, rows, lanes] = (total * conv_in).astype(BF16)
                        gp[run, rows, 2 * CH + lane * HALF : 2 * CH + (lane + 1) * HALF] = (total * gate).astype(BF16)
                return 0

            lax.fori_loop(0, RING, unmix, 0)
            yield 3.0
            yield loads[3]
            for number, at in enumerate(ring_places(x)):
                parts[at] = dot_nn(gp[at], mat_in()).astype(BF16).reshape(2, SHARD, WIDTH)
                work.set("normed" + str(number))
                yield 1.1
            yield loads[4]

            def in_grad(step, _):
                at = pl.ds(pl.multiple_of(step * 512, 512), 512)
                rows = na[:, :, :, at].reshape(RING * RUN, 512)
                grad = dot_tn(gp[...].reshape(RING * RUN, 3 * CH), rows)
                old = w[0:3, :, :, at].reshape(3 * CH, 512).astype(F32)
                gain_sum[:, at] = jnp.sum((grad * old).reshape(3 * CH // 8, 8, 512), axis=0)
                w[0:3, :, :, at] = grad.astype(BF16).reshape(3, 2, HALF, 512)
                return 0

            lax.fori_loop(0, WIDTH // 512, in_grad, 0)
            for half in (0, 1):
                work.set("in_go" + str(half))
            small[...] = jnp.zeros_like(small)
            small[0:1] = jnp.sum(gain_sum[...], axis=0, keepdims=True) / gains[0:1]
            small[1:2] = jnp.sum(gain_two[...], axis=0, keepdims=True)
            mine = pl.ds(pl.multiple_of((x * 2 + k) * CH, CH), CH)
            for number in range(3):
                small[2 + number : 3 + number, mine] = jnp.sum(tap_sum[number], axis=0, keepdims=True)
            work.set("small_go")
            yield 4.5

        def close():
            yield "normed_done"

            def one(at):
                grad = parts[x, k, at].astype(F32) + box[x, at].astype(F32)
                grad = grad + (land[0, at].astype(F32) + land[1, at].astype(F32))
                rows = tokens[at]
                scale = lax.rsqrt(jnp.mean(rows * rows, axis=1, keepdims=True) + NORM_EPS)
                normal = rows * scale
                scaled = grad * gains[0:1]
                back = scale * (scaled - normal * jnp.mean(scaled * normal, axis=1, keepdims=True))
                input_grad[at] = grad_residual[at] + back

            strips(SHARD, 16, one)
            yield 1.2

        work.add(scatter_x(work, parts, box, hop, land, "normed"))
        for half in (0, 1):
            work.add(scatter_yz(work, w.at[3:4], box_mix.at[half], mixer_grad.at[3:4], half, "mix"))
        for half in (0, 1):
            work.add(scatter_yz(work, w.at[0:3], box_in.at[half], mixer_grad.at[0:3], half, "in"))
        work.add(sum_all(work, small, box_small, small_out, "small"))
        work.add(compute(), 1)
        work.add(close(), 1)

    return call(
        "backward_mixer",
        2,
        body,
        [
            (grad_low, ANY), (normed, ANY), (w_in, ANY), (w_out, ANY), (proj, ANY), (near, VMEM), (far, VMEM),
            (taps, VMEM), (starts, SMEM), (tokens, VMEM), (grad_residual, VMEM), (gains, VMEM), (gain_two, VMEM),
        ],
        [(fl(SHARD, WIDTH), VMEM), (fl(4, HALF, CH), VMEM), (fl(8, WIDTH), VMEM)],
        [
            pltpu.VMEM((RING, 2, SHARD, WIDTH), BF16),
            pltpu.VMEM((RING, 2, SHARD, WIDTH), BF16),
            pltpu.VMEM((4, 2, HALF, WIDTH), BF16),
            pltpu.VMEM((RING, RUN, 3 * CH), F32),
            pltpu.VMEM((RING, RUN + 8, CH), F32),
            pltpu.VMEM((RING, RUN + 8, CH), F32),
            pltpu.VMEM((RING, RUN, CH), F32),
            pltpu.VMEM((RING, RUN, CH), BF16),
            pltpu.VMEM((RING, RUN, 3 * CH), BF16),
            pltpu.VMEM((RING, 8, CH), F32),
            pltpu.VMEM((8, CH), F32),
            pltpu.VMEM((3, 8, CH), F32),
            pltpu.VMEM((8, WIDTH), F32),
            pltpu.VMEM((8, WIDTH), F32),
            pltpu.VMEM((RING, 2, SHARD, WIDTH), BF16),
            pltpu.VMEM((RING, SHARD, WIDTH), BF16),
            pltpu.VMEM((2, SHARD // 2, WIDTH), BF16),
            pltpu.VMEM((2, SHARD, WIDTH), BF16),
            pltpu.VMEM((2, 15, 1, HALF, HALF), BF16),
            pltpu.VMEM((2, 15, 3, HALF, HALF), BF16),
            pltpu.VMEM((4, RING, 8, WIDTH), F32),
        ],
        160,
        8,
        X_WAYS + YZ_WAYS + (("z", 2), ("y", 2), ("x", 2), ("row", -1)),
        int(9e9),
    )


def adam_update(weight, gradient, first, second, step_rate, decay_rate):
    first_new = BETA_ONE * first + (1.0 - BETA_ONE) * gradient
    second_new = BETA_TWO * second + (1.0 - BETA_TWO) * gradient * gradient
    first_hat = first_new / (1.0 - BETA_ONE**STEP)
    second_hat = second_new / (1.0 - BETA_TWO**STEP)
    weight_new = weight - step_rate * (
        first_hat / (jnp.sqrt(second_hat) + ADAM_EPS) + decay_rate * weight
    )
    return (weight_new, first_new, second_new)


def body(
    tokens,
    cotangent,
    doc_starts,
    mixer_w,
    ffn_w,
    gains,
    taps,
    mixer_m,
    mixer_v,
    ffn_m,
    ffn_v,
    gain_m,
    gain_v,
    tap_m,
    tap_v,
):
    col = lax.axis_index("col")
    mixer_low = jnp.swapaxes(mixer_w.astype(BF16), 1, 2)
    ffn_low = jnp.swapaxes(ffn_w.astype(BF16), 1, 2)
    taps_pad = jnp.concatenate([taps, jnp.zeros((5, HALF), F32)], axis=0)
    normed, cot, w_in, w_out, ffn, proj, near, far, taps_two, residual, ffn_in = forward_mixer(
        tokens, cotangent, doc_starts, mixer_low, ffn_low, gains, taps_pad
    )
    output, grad_residual, grad_low, ffn_grad, gain_two = feed_forward(
        ffn_in, cot, ffn, residual, cotangent, gains
    )
    input_grad, mixer_grad, total = backward_mixer(
        grad_low, normed, w_in, w_out, proj, near, far, taps_two, doc_starts, tokens, grad_residual, gains, gain_two
    )
    mixer_grad = jnp.swapaxes(mixer_grad, 1, 2)
    ffn_grad = jnp.swapaxes(ffn_grad, 1, 2)
    gain_grad = total[:2]
    first = ((col // 4) * 2 + col % 2) * CH + (col // 2) % 2 * HALF
    tap_grad = lax.dynamic_slice_in_dim(total[2:5], first, HALF, 1)

    mixer_new, mixer_m_new, mixer_v_new = adam_update(
        mixer_w, mixer_grad, mixer_m, mixer_v, MATRIX_RATE, MATRIX_DECAY
    )
    ffn_new, ffn_m_new, ffn_v_new = adam_update(
        ffn_w, ffn_grad, ffn_m, ffn_v, MATRIX_RATE, MATRIX_DECAY
    )
    gain_new, gain_m_new, gain_v_new = adam_update(
        gains, gain_grad, gain_m, gain_v, SMALL_RATE, 0.0
    )
    tap_new, tap_m_new, tap_v_new = adam_update(taps, tap_grad, tap_m, tap_v, SMALL_RATE, 0.0)
    return (
        output,
        input_grad,
        mixer_grad,
        mixer_new,
        mixer_m_new,
        mixer_v_new,
        ffn_grad,
        ffn_new,
        ffn_m_new,
        ffn_v_new,
        gain_grad,
        gain_new,
        gain_m_new,
        gain_v_new,
        tap_grad,
        tap_new,
        tap_m_new,
        tap_v_new,
    )


def solution(mesh):
    placed = (
        P(("row", "col"), None),
        P(("row", "col"), None),
        P(),
        P(None, "row", "col"),
        P(None, "row", "col"),
        P(),
        P(None, "col"),
        P(None, "row", "col"),
        P(None, "row", "col"),
        P(None, "row", "col"),
        P(None, "row", "col"),
        P(),
        P(),
        P(None, "col"),
        P(None, "col"),
    )
    return jax.shard_map(
        body,
        mesh=mesh,
        in_specs=placed,
        out_specs=(
            P(("row", "col"), None),
            P(("row", "col"), None),
            P(None, "row", "col"),
            P(None, "row", "col"),
            P(None, "row", "col"),
            P(None, "row", "col"),
            P(None, "row", "col"),
            P(None, "row", "col"),
            P(None, "row", "col"),
            P(None, "row", "col"),
            P(),
            P(),
            P(),
            P(),
            P(None, "col"),
            P(None, "col"),
            P(None, "col"),
            P(None, "col"),
        ),
        check_vma=False,
    )
```

```python
import jax
import jax.numpy as jnp
from jax import lax
from jax.experimental import pallas as pl
from jax.experimental.pallas import tpu as pltpu
from jax.sharding import PartitionSpec as P

STEP = 5


NORM_EPS = 1e-05
BETA_ONE = 0.9
BETA_TWO = 0.95
ADAM_EPS = 1e-08
MATRIX_DECAY = 0.1
MATRIX_RATE = 0.03
SMALL_RATE = 0.3

MESH = pl.DeviceIdType.MESH
BF16 = jnp.bfloat16
F32 = jnp.float32
RING = 4
COT_HOLD = None
ROWS = 8
(
    CA, CIN, COT, COTANGENT, COT_LOW, DOWN, DOWN_GRAD, DOWN_PART, DOWN_PARTS, DWD, DWG, ENTRY, FAR,
    FFN_LOW, FFN_W0, FFN_W1, GAINS, GAIN_TWO, GATE, GFFN, GRAD, GRAD0, GRAD1, GRAD_RESIDUAL, IN, IN_OUT,
    MIX, NEAR, NORMED, NORMED_IN, NORMED_OUT, OUT, OUT0, OUT1, OUT_A, PROJ, PROJ_OUT, RESIDUAL, SMALL,
    START, TAPS, TAPS_SENT, TOKENS, UP, USED, W0, W1, W3, WD, WEIGHTS, W_IN, W_OUT, ALL, DONE, FIRST,
    GO, MOST, OWN, READY, SENT, SIB, SPREAD, SWAP,
) = range(63)

LINK = 46.5e3
CORES = 280e3
LINK_LAG, CORE_LAG = 2.0, 1.0
SEND_LAG = 5.0
WAIT = 0.05


def place():
    row, col = lax.axis_index("row"), lax.axis_index("col")
    return {"x": col // 4, "y": row // 2, "z": (col // 2) % 2 * 2 + row % 2, "k": col % 2}


def device_at(at):
    return (at["y"] * 2 + at["z"] % 2, at["x"] * 4 + at["z"] // 2 * 2 + at["k"])


def wrap(value, length=RING):
    return lax.rem(value + length, length)


def size_of(ref):
    size = jnp.dtype(ref.dtype).itemsize
    for extent in ref.shape:
        size *= extent
    return size


class Work:
    def __init__(self, send_sems, recv_sems, local_sems):
        self.me = place()
        self.send_sems, self.recv_sems, self.local_sems = send_sems, recv_sems, local_sems
        self.sending, self.local, self.kept, self.count = [], [], [], 0
        self.now, self.free, self.due, self.flags, self.chains = 0.0, {}, {}, set(), []

    def near(self, axis, step):
        at = dict(self.me)
        at[axis] = wrap(at[axis] + step, 2 if axis == "k" else RING)
        return device_at(at)

    def target(self, way):
        axis, step = way
        if axis == "row":
            row, col = lax.axis_index("row"), lax.axis_index("col")
            return (wrap(row + step, ROWS), col + 2 - 4 * ((col // 2) % 2))
        return self.near(axis, step)

    def barrier(self, ways):
        sem = pltpu.get_barrier_semaphore()
        for axis, step in ways:
            pl.semaphore_signal(sem, inc=1, device_id=self.target((axis, -step)), device_id_type=MESH)
        pl.semaphore_wait(sem, len(ways))

    def send(self, source, target, way):
        slot = len(self.sending)
        for number, (before, finish) in enumerate(self.sending):
            if finish + SEND_LAG < self.now:
                before.wait_send()
                slot = number
                break
        copy = pltpu.make_async_remote_copy(
            src_ref=source,
            dst_ref=target,
            send_sem=self.send_sems.at[slot],
            recv_sem=self.recv_sems.at[self.count],
            device_id=self.target(way),
            device_id_type=MESH,
        )
        copy.start()
        self.count += 1
        begin = max(self.now, self.free.get(way, 0.0))
        self.free[way] = begin + size_of(source) / (CORES if way[0] == "k" else LINK)
        self.sending[slot : slot + 1] = [(copy, self.free[way])]
        self.due[id(copy)] = self.free[way] + (CORE_LAG if way[0] == "k" else LINK_LAG)
        self.kept.append(copy)
        return copy

    def copy(self, source, target, rate=1.4e6):
        slot = len(self.local)
        for number, before in enumerate(self.local):
            if before is None:
                slot = number
                break
        copy = pltpu.make_async_copy(source, target, self.local_sems.at[slot])
        copy.start()
        begin = max(self.now, self.free.get(0, 0.0))
        self.free[0] = begin + size_of(source) / rate
        self.due[id(copy)] = self.free[0] + 0.5
        self.local[slot : slot + 1] = [copy]
        self.kept.append(copy)
        return copy

    def add(self, chain, rank=0):
        self.chains.append([next(chain), rank, len(self.chains), chain])

    def set(self, flag):
        self.flags.add(flag)

    def run(self):
        while self.chains:
            best, when = None, None
            for entry in self.chains:
                wish = entry[0]
                if isinstance(wish, (int, tuple)):
                    if wish not in self.flags:
                        continue
                    key = (0 if entry[1] == 0 else 1, entry[1], self.now, entry[2])
                elif isinstance(wish, float):
                    key = (0 if entry[1] == 0 else 1, entry[1], self.now, entry[2])
                else:
                    due = self.due[id(wish)]
                    if due <= self.now:
                        key = (0 if entry[1] == 0 else 1, entry[1], due, entry[2])
                    else:
                        key = (2, due, entry[1], entry[2])
                if best is None or key < when:
                    best, when = entry, key
            assert best is not None, self.flags
            wish = best[0]
            if not isinstance(wish, (int, tuple, float)):
                self.now = max(self.now, self.due[id(wish)]) + WAIT
                if any(wish is copy for copy in self.local):
                    wish.wait()
                    self.local = [None if copy is wish else copy for copy in self.local]
                else:
                    wish.wait_recv()
            try:
                best[0] = next(best[3])
                if isinstance(best[0], float):
                    self.now += best[0]
            except StopIteration:
                self.chains = [entry for entry in self.chains if entry is not best]
        for copy, _ in self.sending:
            copy.wait_send()
        for copy in self.local:
            if copy is not None:
                copy.wait()


def stream(work, items):
    pending = []
    for wait, source, target, done in items:
        if wait is not None:
            while pending:
                yield pending[0][0]
                work.set(pending.pop(0)[1])
            yield wait
        pending.append((work.copy(source, target), done))
        if len(pending) > 1:
            yield pending[0][0]
            work.set(pending.pop(0)[1])
    while pending:
        yield pending[0][0]
        work.set(pending.pop(0)[1])


def pieces(wait, source, target, done):
    count = source.shape[0]
    return [
        (wait if number == 0 else None, source.at[number], target.at[number], done if number == count - 1 else (done, number))
        for number in range(count)
    ]


def gather_x(work, source, out, name, copy=False, hold=None):
    x, k = work.me["x"], work.me["k"]
    rows = source.shape[0]
    half = rows // 2
    low, high = pl.ds(0, half), pl.ds(half, half)
    right, left, other = ("x", 1), ("x", -1), ("k", 1)
    ahead, behind, across = wrap(x + 1), wrap(x - 1), wrap(x + 2)
    sib, own = [], []

    def relay(at, part):
        sib.append(work.send(out.at[at, k, part], out.at[at, k, part], other))
        work.set((name, SIB, len(sib)))

    def siblings():
        for number in range(1, 8):
            yield (name, SIB, number)
            yield sib[number - 1]
            if number == 1 and copy:
                yield own[0]
            if number in (1, 5, 7):
                work.set((name, {1: OWN, 5: NEAR, 7: ALL}[number]))

    work.add(siblings())
    yield (name, GO)
    r0 = work.send(source.at[low], out.at[x, k, low], right)
    l1 = work.send(source.at[high], out.at[x, k, high], left)
    r1 = work.send(source.at[high], out.at[x, k, high], right)
    l0 = work.send(source.at[low], out.at[x, k, low], left)
    sib.append(work.send(source, out.at[x, k], other))
    if copy:
        own.append(work.copy(source, out.at[x, k]))
    work.set((name, SIB, 1))
    work.set((name, SENT))
    if hold is not None:
        yield hold
    yield r0
    far0 = work.send(out.at[behind, k, low], out.at[behind, k, low], right)
    relay(behind, low)
    yield l1
    far1 = work.send(out.at[ahead, k, high], out.at[ahead, k, high], left)
    relay(ahead, high)
    work.set((name, FAR))
    yield r1
    relay(behind, high)
    yield l0
    relay(ahead, low)
    yield far0
    relay(across, low)
    yield far1
    relay(across, high)


def add_into(target, first, second):
    rows, lanes = target.shape[-2:]
    if rows * lanes <= 1 << 15:
        target[...] = first[...] + second[...]
        return
    strip = 32

    def body(step, _):
        at = pl.ds(pl.multiple_of(step * strip, strip), strip)
        target[at] = first[at] + second[at]
        return 0

    lax.fori_loop(0, rows // strip, body, 0)


def ring_places(x):
    return (wrap(x + 2), wrap(x + 1), wrap(x - 1), x)


def scatter_x(work, parts, box, hop, land, name):
    x, k = work.me["x"], work.me["k"]
    rows = box.shape[1]
    half = rows // 2
    low, high = pl.ds(0, half), pl.ds(half, half)
    right, left, other = ("x", 1), ("x", -1), ("k", 1)
    across, ahead, behind, own = ring_places(x)

    def swap():
        sib = {}
        for number, at in enumerate((across, ahead, behind, own)):
            yield (name, READY, number)
            sib[number] = work.send(parts.at[at, 1 - k], box.at[at], other)
            got.append(sib[number])
            work.set((name, SWAP, number))

    got = []
    work.add(swap(), 0)
    yield (name, SWAP, 0)
    yield got[0]
    add_into(box.at[across], parts.at[across, k], box.at[across])
    far0 = work.send(box.at[across, low], hop.at[0], right)
    far1 = work.send(box.at[across, high], hop.at[1], left)
    yield 0.3
    yield (name, SWAP, 1)
    yield got[1]
    add_into(box.at[ahead], parts.at[ahead, k], box.at[ahead])
    r1 = work.send(box.at[ahead, high], land.at[0, high], right)
    yield 0.3
    yield (name, SWAP, 2)
    yield got[2]
    add_into(box.at[behind], parts.at[behind, k], box.at[behind])
    l0 = work.send(box.at[behind, low], land.at[1, low], left)
    yield 0.3
    yield far0
    add_into(box.at[ahead, low], box.at[ahead, low], hop.at[0])
    r0 = work.send(box.at[ahead, low], land.at[0, low], right)
    yield 0.15
    yield far1
    add_into(box.at[behind, high], box.at[behind, high], hop.at[1])
    l1 = work.send(box.at[behind, high], land.at[1, high], left)
    work.set((name, SENT))
    yield 0.15
    yield (name, SWAP, 3)
    yield got[3]
    for copy in (r1, l0, r0, l1):
        yield copy
    work.set((name, DONE))


def block(ref, y, z, half, rows):
    column = pl.multiple_of((y * 2 + z % 2) * 256 + half * 128, 128)
    return ref.at[:, z // 2, rows, pl.ds(column, 128)]


def gather_yz(work, source, out, half, name):
    first, second = ("y", "z") if half == 0 else ("z", "y")
    rows = source.shape[1]
    cut = rows // 2
    low, high, whole = pl.ds(0, cut), pl.ds(cut, cut), pl.ds(0, rows)
    a, b = work.me[first], work.me[second]

    def slot(at_a, at_b, part):
        y, z = (at_a, at_b) if half == 0 else (at_b, at_a)
        return block(out, y, z, half, part)

    columns = pl.ds(half * 128, 128)
    up, down, forward, backward = (first, 1), (first, -1), (second, 1), (second, -1)
    a_behind, a_ahead, a_across = wrap(a - 1), wrap(a + 1), wrap(a + 2)
    b_behind, b_ahead = wrap(b - 1), wrap(b + 1)
    yield (name, GO, half)
    mine = work.copy(source.at[:, :, columns], slot(a, b, whole))
    r0 = work.send(source.at[:, low, columns], slot(a, b, low), up)
    l1 = work.send(source.at[:, high, columns], slot(a, b, high), down)
    r1 = work.send(source.at[:, high, columns], slot(a, b, high), up)
    l0 = work.send(source.at[:, low, columns], slot(a, b, low), down)
    waits, last = [], []

    def spread(at, part, ref=None):
        ref = slot(at, b, part) if ref is None else ref
        waits.append(
            (
                at,
                part,
                work.send(ref, slot(at, b, part), forward),
                work.send(ref, slot(at, b, part), backward),
            )
        )

    def onward(number):
        at, part, plus, minus = waits[number]
        yield plus
        if part is low:
            last.append(work.send(slot(at, b_behind, part), slot(at, b_behind, part), forward))
        yield minus
        if part is high:
            last.append(work.send(slot(at, b_ahead, part), slot(at, b_ahead, part), backward))

    spread(a, low, source.at[:, low, columns])
    spread(a, high, source.at[:, high, columns])
    yield r0
    f0 = work.send(slot(a_behind, b, low), slot(a_behind, b, low), up)
    spread(a_behind, low)
    yield l1
    f1 = work.send(slot(a_ahead, b, high), slot(a_ahead, b, high), down)
    spread(a_ahead, high)
    yield from onward(0)
    yield r1
    spread(a_behind, high)
    yield l0
    spread(a_ahead, low)
    yield from onward(1)
    yield f0
    spread(a_across, low)
    yield f1
    spread(a_across, high)
    work.set((name, SPREAD, half))
    for number in range(2, 8):
        yield from onward(number)
        if number == 5:
            work.set((name, MOST, half))
    work.set((name, SENT, half))
    for copy in last:
        yield copy
    yield mine
    work.set((name, ALL, half))


def scatter_yz(work, parts, box, out, half, name, where=None):
    first, second = ("z", "y") if half == 0 else ("y", "z")
    rows = parts.shape[2]
    cut = rows // 2
    low, high, whole = pl.ds(0, cut), pl.ds(cut, cut), pl.ds(0, rows)
    a, b = work.me[first], work.me[second]

    def slot(at_a, at_b, part):
        y, z = (at_b, at_a) if half == 0 else (at_a, at_b)
        return block(parts, y, z, half, part)

    across, ahead, behind, own = ring_places(a)
    up, down = (first, 1), (first, -1)

    def first_ring(number, at_b):
        base = 3 * number
        pick = lambda at, part: slot(at, at_b, part)
        yield (name, GO, half)
        far0 = work.send(pick(across, low), box.at[base, :, low], up)
        far1 = work.send(pick(across, high), box.at[base, :, high], down)
        r1 = work.send(pick(ahead, high), box.at[base + 1, :, high], up)
        l0 = work.send(pick(behind, low), box.at[base + 2, :, low], down)
        yield far0
        add_into(pick(ahead, low), pick(ahead, low), box.at[base, :, low])
        r0 = work.send(pick(ahead, low), box.at[base + 1, :, low], up)
        yield far1
        add_into(pick(behind, high), pick(behind, high), box.at[base, :, high])
        l1 = work.send(pick(behind, high), box.at[base + 2, :, high], down)
        yield r1
        add_into(pick(own, high), pick(own, high), box.at[base + 1, :, high])
        yield l0
        add_into(pick(own, low), pick(own, low), box.at[base + 2, :, low])
        yield r0
        add_into(pick(own, low), pick(own, low), box.at[base + 1, :, low])
        yield l1
        add_into(pick(own, high), pick(own, high), box.at[base + 2, :, high])
        work.set((name, FIRST, half, number))

    places = ring_places(b)
    for number, at_b in enumerate(places):
        work.add(first_ring(number, at_b))
    b_across, b_ahead, b_behind, b_own = places
    forward, backward = (second, 1), (second, -1)
    yield (name, FIRST, half, 0)
    far0 = work.send(slot(a, b_across, low), box.at[12, :, low], forward)
    far1 = work.send(slot(a, b_across, high), box.at[12, :, high], backward)
    yield (name, FIRST, half, 1)
    r1 = work.send(slot(a, b_ahead, high), box.at[13, :, high], forward)
    yield far0
    add_into(slot(a, b_ahead, low), slot(a, b_ahead, low), box.at[12, :, low])
    r0 = work.send(slot(a, b_ahead, low), box.at[13, :, low], forward)
    yield (name, FIRST, half, 2)
    l0 = work.send(slot(a, b_behind, low), box.at[14, :, low], backward)
    yield far1
    add_into(slot(a, b_behind, high), slot(a, b_behind, high), box.at[12, :, high])
    l1 = work.send(slot(a, b_behind, high), box.at[14, :, high], backward)
    yield (name, FIRST, half, 3)
    mine = slot(a, b_own, whole)
    for copy in (r1, r0, l0, l1):
        yield copy
    for m in range(parts.shape[0]):
        total = mine[m].astype(F32) + box[13, m].astype(F32) + box[14, m].astype(F32)
        if where is not None:
            out[where[m], half * 128 : (half + 1) * 128, :] = total.T
        else:
            out[m, :, half * 128 : (half + 1) * 128] = total
    work.set((name, DONE, half))


def sum_all(work, values, box, out, name):
    yield (name, GO)
    out[...] = values[...]
    me = work.me
    for turn, axis in enumerate(("z", "y", "x", "k")):
        length = 2 if axis == "k" else RING
        mine = box.at[turn, me[axis]]
        mine[...] = out[...]
        copies = [work.send(mine, mine, (axis, step)) for step in range(1, length)]
        for copy in copies:
            yield copy
        total = box[turn, 0]
        for number in range(1, length):
            total = total + box[turn, number]
        out[...] = total
    work.set((name, DONE))


ANY = pl.BlockSpec(memory_space=pl.ANY)
VMEM = pl.BlockSpec(memory_space=pltpu.VMEM)
SMEM = pl.BlockSpec(memory_space=pltpu.SMEM)
X_WAYS = (("x", 1), ("x", -1), ("k", 1))
YZ_WAYS = (("y", 1), ("y", -1), ("z", 1), ("z", -1))


def bf(*shape):
    return jax.ShapeDtypeStruct(shape, BF16)


def fl(*shape):
    return jax.ShapeDtypeStruct(shape, F32)


def call(name, number, body, args, outs, scratch, copies, ways, flops):
    def kernel(*refs):
        main, sems = refs[:-3], refs[-3:]
        work = Work(*sems)
        body(work, *main)
        work.barrier(ways)
        work.run()
        used = (len(work.sending), work.count, len(work.local))
        assert all(one <= most for one, most in zip(used, copies)), used

    sems = [pltpu.SemaphoreType.DMA((count,)) for count in copies]
    return pl.pallas_call(
        kernel,
        out_shape=[shape for shape, _ in outs],
        in_specs=[spec for _, spec in args],
        out_specs=[spec for _, spec in outs],
        scratch_shapes=list(scratch) + sems,
        compiler_params=pltpu.CompilerParams(
            collective_id=number, has_side_effects=True, vmem_limit_bytes=63 << 20
        ),
        cost_estimate=pl.CostEstimate(flops=flops, bytes_accessed=40 << 20, transcendentals=0),
        name=name,
    )(*[array for array, _ in args])


def dot_nt(left, right):
    return lax.dot_general(left, right, (((1,), (1,)), ((), ())), preferred_element_type=F32)


def dot_tn(left, right):
    return lax.dot_general(left, right, (((0,), (0,)), ((), ())), preferred_element_type=F32)


def dot_nn(left, right):
    return lax.dot_general(left, right, (((1,), (0,)), ((), ())), preferred_element_type=F32)


def strips(rows, strip, body):
    def one(step, _):
        body(pl.ds(pl.multiple_of(step * strip, strip), strip))
        return 0

    lax.fori_loop(0, rows // strip, one, 0)


def keeps(starts, first, shape):
    places = first + lax.broadcasted_iota(jnp.int32, shape, 0)

    def keep(at):
        hit = at == starts[0]
        for number in range(1, 4):
            hit = jnp.logical_or(hit, at == starts[number])
        return jnp.where(hit, 0.0, 1.0).astype(F32)

    here = keep(places)
    return here, here * keep(places - 1)


def run_start(run, run_tokens):
    row, col = lax.axis_index("row"), lax.axis_index("col")
    return ((row * RING + run) * 2 + (col // 2) % 2) * run_tokens


SHARD, WIDTH = 128, 2048
RUN = 2 * SHARD
CH, HALF = 256, 128
HID = 352


def lags(ext, starts, run, at, lane):
    rows = 64
    lanes = slice(lane * HALF, (lane + 1) * HALF)
    one, two = keeps(starts, run_start(run, RUN) + at, (rows, HALF))
    mixed = ext[run, 8 + at : 8 + at + rows, lanes]
    return mixed, one * ext[run, 7 + at : 7 + at + rows, lanes], two * ext[run, 6 + at : 6 + at + rows, lanes]


def place_halo(ext, near, far):
    row, col = lax.axis_index("row"), lax.axis_index("col")
    late = (col // 2) % 2 == 1
    first = jnp.where(row > 0, far[...], 0.0)
    for run in range(RING):
        ext[run, 0:8] = jnp.where(late, near[run], first if run == 0 else near[run - 1])


def forward_mixer(tokens, cotangent, starts, mixer, ffn, gains, taps):
    def body(
        work, tokens_in, cotangent_in, starts, mixer_in, ffn_in, gains_in, taps_in,
        normed_out, cot_out, in_out, mix_out, ffn_out, proj_out, near_final, far_final, taps_final, residual_out, low_out,
        gains, taps, near_out, far_out, taps_out, tokens, cotangent, mixer_wide, ffn_wide, mixer, ffn, tap_rows,
        normed, weights, proj, ext, gated, parts, box, hop, land, cot, residual, low_rows,
    ):
        x, k = work.me["x"], work.me["k"]
        z_hi = (lax.axis_index("col") // 2) % 2
        w_in, w_out = weights.at[0:3], weights.at[3:4]
        sent = {}

        def opening():
            loads = [work.copy(gains_in, gains), work.copy(tokens_in, tokens)]
            loads += [work.copy(mixer_in, mixer_wide), work.copy(taps_in, taps)]
            yield loads[0]
            yield loads[1]

            def norm(at):
                rows = tokens[at]
                scale = lax.rsqrt(jnp.mean(rows * rows, axis=1, keepdims=True) + NORM_EPS)
                normed[x, k, at] = (rows * scale * gains[0:1]).astype(BF16)

            strips(SHARD, 16, norm)
            work.set((NORMED, GO))
            yield 1.0
            yield loads[2]
            loads.append(work.copy(ffn_in.at[0:2], ffn_wide))
            for number in range(4):
                mixer[number] = mixer_wide[number].T.astype(BF16)
            work.set((IN, GO, 0))
            work.set((IN, GO, 1))
            yield 0.6
            loads.append(work.copy(cotangent_in, cotangent))
            yield loads[3]
            tap_rows[...] = jnp.zeros_like(tap_rows)
            tap_rows[0:3] = taps[...]
            taps_out[z_hi] = tap_rows[...]
            sent[TAPS] = work.send(tap_rows, taps_out.at[z_hi], ("z", 2))
            work.set(TAPS_SENT)
            yield loads[4]
            for number in range(2):
                for at in range(0, HID, 88):
                    ffn[number, at : at + 88] = ffn_wide[number, at : at + 88].astype(BF16)
            work.set(FFN_LOW)
            yield 0.5
            yield loads[5]

            def cast(at):
                cot[at] = cotangent[at].astype(BF16)

            strips(SHARD, 16, cast)
            work.set(COT_LOW)
            yield 0.5

        def compute():
            yield TAPS_SENT
            yield sent[TAPS]
            yield (NORMED, ALL)
            yield (IN, ALL, 0)
            yield (IN, ALL, 1)
            tail = normed[:, 1, SHARD - 16 :].reshape(RING * 16, WIDTH)
            ends = dot_nt(tail, weights[0:3].reshape(3 * CH, WIDTH))
            mixed = (ends[:, :CH] * ends[:, 2 * CH :]).reshape(RING, 16, CH)
            ext[:, RUN - 8 : RUN + 8] = mixed
            halo = [
                work.send(ext.at[:, RUN : RUN + 8], near_out, ("z", 2)),
                work.send(ext.at[RING - 1, RUN : RUN + 8], far_out, ("row", 1)),
            ]
            yield 1.0

            def project(half, _):
                rows = normed[pl.ds(2 * half, 2)].reshape(2 * RUN, WIDTH)
                out = dot_nt(rows, weights[0:3].reshape(3 * CH, WIDTH))
                proj[pl.ds(2 * half, 2)] = out.reshape(2, RUN, 3 * CH)
                return 0

            lax.fori_loop(0, 2, project, 0)
            work.set(PROJ)
            yield 4.0

            def mix(run, _):
                for at in range(0, RUN, 64):
                    size = 64 if at + 64 < RUN else 56
                    rows = proj[run, at : at + size]
                    ext[run, 8 + at : 8 + at + size] = rows[:, :CH] * rows[:, 2 * CH :]
                return 0

            lax.fori_loop(0, RING, mix, 0)
            yield 0.7
            for copy in halo:
                yield copy
            place_halo(ext, near_out, far_out)
            for source, target in ((near_out, near_final), (far_out, far_final), (taps_out, taps_final)):
                work.copy(source, target)

            def convolve(run, _):
                for at in range(0, RUN, 64):
                    for lane in range(2):
                        mixed, one, two = lags(ext, starts, run, at, lane)
                        tap = taps_out[lane]
                        total = tap[2:3] * mixed + tap[1:2] * one + tap[0:1] * two
                        gate = proj[run, at : at + 64, CH + lane * HALF : CH + (lane + 1) * HALF]
                        gated[run, at : at + 64, lane * HALF : (lane + 1) * HALF] = (gate * total).astype(BF16)
                return 0

            lax.fori_loop(0, RING, convolve, 0)
            yield 1.5
            yield (MIX, ALL, 0)
            yield (MIX, ALL, 1)
            work.set(WEIGHTS)
            for number, at in enumerate(ring_places(x)):
                out = dot_nn(gated[at], weights[3].reshape(CH, WIDTH))
                parts[at] = out.astype(BF16).reshape(2, SHARD, WIDTH)
                work.set((OUT, READY, number))
                yield 0.6
            yield (OUT, DONE)

            def close(at):
                total = parts[x, k, at].astype(F32) + box[x, at].astype(F32)
                total = total + (land[0, at].astype(F32) + land[1, at].astype(F32))
                rows = tokens[at] + total
                scale = lax.rsqrt(jnp.mean(rows * rows, axis=1, keepdims=True) + NORM_EPS)
                residual[at] = rows
                low_rows[at] = (rows * scale * gains[1:2]).astype(BF16)

            strips(SHARD, 16, close)
            work.copy(low_rows, low_out)
            work.copy(residual, residual_out)
            yield 1.0

        def order():
            yield (NORMED, FAR)
            yield COT_LOW
            work.set((COT, GO))

        def follow(half):
            yield FFN_LOW
            yield (IN, MOST, half)
            work.set((MIX, GO, half))
            yield (MIX, MOST, half)
            work.set((GATE, GO, half))
            yield (GATE, MOST, half)
            work.set((UP, GO, half))

        work.add(opening(), 1)
        work.add(gather_x(work, normed.at[x, k], normed, NORMED))
        for half in (0, 1):
            work.add(gather_yz(work, mixer.at[0:3], w_in, half, IN))
        for half in (0, 1):
            work.add(gather_yz(work, mixer.at[3:4], w_out, half, MIX))
        for number, name in enumerate((GATE, UP)):
            for half in (0, 1):
                mat = pl.ds(number, 1)
                work.add(gather_yz(work, ffn.at[mat], ffn_out.at[mat], half, name))
        work.add(scatter_x(work, parts, box, hop, land, OUT))
        work.add(gather_x(work, cot, cot_out, COT, copy=True, hold=COT_HOLD), 0)
        outs = pieces((NORMED, ALL), normed, normed_out, NORMED_OUT)
        outs += pieces(PROJ, proj, proj_out, PROJ_OUT)
        outs += pieces(WEIGHTS, weights.at[0:3], in_out, IN_OUT) + pieces(WEIGHTS, weights.at[3:4], mix_out, W3)
        work.add(stream(work, outs), 3)
        work.add(order())
        work.add(follow(0))
        work.add(follow(1))
        work.add(compute(), 1)

    gathered = bf(RING, 2, SHARD, WIDTH)
    return call(
        "forward_mixer",
        0,
        body,
        [(tokens, ANY), (cotangent, ANY), (starts, SMEM), (mixer, ANY), (ffn, ANY), (gains, ANY), (taps, ANY)],
        [
            (gathered, ANY), (gathered, ANY), (bf(3, 2, HALF, WIDTH), ANY), (bf(1, 2, HALF, WIDTH), ANY),
            (bf(2, 2, HID, WIDTH), ANY), (fl(RING, RUN, 3 * CH), ANY), (fl(RING, 8, CH), ANY), (fl(8, CH), ANY),
            (fl(2, 8, HALF), ANY), (fl(SHARD, WIDTH), ANY), (bf(SHARD, WIDTH), ANY),
        ],
        [
            pltpu.VMEM((2, WIDTH), F32),
            pltpu.VMEM((3, HALF), F32),
            pltpu.VMEM((RING, 8, CH), F32),
            pltpu.VMEM((8, CH), F32),
            pltpu.VMEM((2, 8, HALF), F32),
            pltpu.VMEM((SHARD, WIDTH), F32),
            pltpu.VMEM((SHARD, WIDTH), F32),
            pltpu.VMEM((4, CH, HALF), F32),
            pltpu.VMEM((2, HID, CH), F32),
            pltpu.VMEM((4, HALF, CH), BF16),
            pltpu.VMEM((2, HID, CH), BF16),
            pltpu.VMEM((8, HALF), F32),
            pltpu.VMEM((RING, 2, SHARD, WIDTH), BF16),
            pltpu.VMEM((4, 2, HALF, WIDTH), BF16),
            pltpu.VMEM((RING, RUN, 3 * CH), F32),
            pltpu.VMEM((RING, RUN + 8, CH), F32),
            pltpu.VMEM((RING, RUN, CH), BF16),
            pltpu.VMEM((RING, 2, SHARD, WIDTH), BF16),
            pltpu.VMEM((RING, SHARD, WIDTH), BF16),
            pltpu.VMEM((2, SHARD // 2, WIDTH), BF16),
            pltpu.VMEM((2, SHARD, WIDTH), BF16),
            pltpu.VMEM((SHARD, WIDTH), BF16),
            pltpu.VMEM((SHARD, WIDTH), F32),
            pltpu.VMEM((SHARD, WIDTH), BF16),
        ],
        (90, 300, 20),
        X_WAYS + YZ_WAYS + (("z", 2), ("row", 1)),
        int(5e9),
    )


def feed_forward(rows, cot, ffn, ffn_wide, residual, cotangent, gains):
    def body(
        work, rows_in, cot, ffn, ffn_wide, residual_in, cotangent_in, gains_in,
        grad_out, low_out, down_out, down_grad_out, part_out, gain_out,
        gains, gain_part, fa, ca, w, down_part, down_wide, down_low, residual, cotangent, down_grad,
        gate, up, hid, gg, gu, gh, grad_low,
        parts_a, parts_b, box_b, hop_b, land_b, boxes,
    ):
        x, k = work.me["x"], work.me["k"]
        units = 2 * HID

        def mat(number):
            return w[number].reshape(units, WIDTH)

        def weight_grad(out, left, right):
            def columns(step, _):
                at = pl.ds(pl.multiple_of(step * 512, 512), 512)
                rows = right[:, :, :, at].reshape(RING * RUN, 512)
                grad = dot_tn(left[...].reshape(RING * RUN, units), rows)
                out[:, :, at] = grad.astype(BF16).reshape(2, HID, 512)
                return 0

            lax.fori_loop(0, WIDTH // 512, columns, 0)

        def opening():
            yield START
            work.set((ENTRY, GO))
            yield work.copy(ffn_wide.at[2], down_wide)
            for at in range(0, HID, 88):
                down_low[0, at : at + 88] = down_wide[at : at + 88].astype(BF16)
            work.set((WD, GO, 0))
            work.set((WD, GO, 1))
            yield 0.2

        work.set(START)
        ins = pieces((WD, GO, 1), ffn.at[0], w.at[0], W0) + pieces(None, ffn.at[1], w.at[1], W1)
        ins += pieces(None, cot, ca, CA)
        ins += [(None, residual_in, residual, RESIDUAL), (None, cotangent_in, cotangent, COTANGENT), (None, gains_in, gains, GAINS)]
        outs = pieces(DOWN_PART, parts_a, down_out, OUT_A) + pieces(GRAD0, w.at[0], part_out.at[0], OUT0)
        outs += pieces(GRAD1, w.at[1], part_out.at[1], OUT1)

        def compute():
            across, ahead, behind, own = ring_places(x)

            def forward(at):
                rows = fa[at].reshape(RUN, WIDTH)
                gate[at] = dot_nt(rows, mat(0))
                up[at] = dot_nt(rows, mat(1))

                def activate(here):
                    value = gate[at, here]
                    hid[at, here] = (value * jax.nn.sigmoid(value) * up[at, here]).astype(BF16)

                strips(RUN, 16, activate)

            yield (ENTRY, OWN)
            yield W0
            yield W1
            forward(own)
            yield 2.9
            yield (ENTRY, NEAR)
            forward(behind)
            yield 2.9
            forward(ahead)
            yield 2.9
            yield (ENTRY, ALL)
            forward(across)
            yield 2.9
            yield CA
            weight_grad(down_part.at[0], hid, ca)
            for half in (0, 1):
                work.set((DWD, GO, half))
            yield 4.0
            yield (WD, ALL, 0)
            yield (WD, ALL, 1)
            for pair in (0, 1):
                gh[...] = dot_nt(ca[pl.ds(2 * pair, 2)].reshape(2 * RUN, WIDTH), mat(2)).reshape(2, RUN, units)
                yield 2.0

                def one(at):
                    for here in (0, 1):
                        run = 2 * pair + here
                        value, grad = gate[run, at], gh[here, at]
                        sig = jax.nn.sigmoid(value)
                        gg[run, at] = (grad * up[run, at] * sig * (1.0 + value * (1.0 - sig))).astype(BF16)
                        gu[run, at] = (grad * (value * sig)).astype(BF16)

                strips(RUN, 16, one)
                yield 1.5
            for number, at in enumerate(ring_places(x)):
                grad = dot_nn(gg[at], mat(0)) + dot_nn(gu[at], mat(1))
                parts_b[at] = grad.astype(BF16).reshape(2, SHARD, WIDTH)
                work.set((GFFN, READY, number))
                yield 2.2
            for at in range(RING):
                parts_a[at] = dot_nn(hid[at], mat(2)).astype(BF16).reshape(2, SHARD, WIDTH)
            work.set(DOWN_PART)
            yield 4.4
            weight_grad(w.at[0], gg, fa)
            work.set(GRAD0)
            yield 4.0
            weight_grad(w.at[1], gu, fa)
            work.set(GRAD1)
            yield 4.0
            yield (DWD, DONE, 0)
            yield (DWD, DONE, 1)
            work.copy(down_grad, down_grad_out)

        def close_grad():
            yield (GFFN, DONE)
            yield RESIDUAL
            yield GAINS
            gain_part[...] = jnp.zeros_like(gain_part)

            def one(at):
                grad = parts_b[x, k, at].astype(F32) + box_b[x, at].astype(F32)
                grad = grad + (land_b[0, at].astype(F32) + land_b[1, at].astype(F32))
                rows = residual[at]
                scale = lax.rsqrt(jnp.mean(rows * rows, axis=1, keepdims=True) + NORM_EPS)
                normal = rows * scale
                gain = grad * normal
                gain_part[...] += gain[:8] + gain[8:]
                scaled = grad * gains[1:2]
                back = scale * (scaled - normal * jnp.mean(scaled * normal, axis=1, keepdims=True))
                total = cotangent[at] + back
                cotangent[at] = total
                grad_low[at] = total.astype(BF16)

            strips(SHARD, 16, one)
            work.copy(grad_low, low_out)
            work.copy(cotangent, grad_out)
            work.copy(gain_part, gain_out)
            yield 1.5

        work.add(opening(), 0)
        work.add(stream(work, ins), 1)
        work.add(stream(work, outs), 1)
        work.add(gather_x(work, rows_in, fa, ENTRY, copy=True))
        for half in (0, 1):
            work.add(gather_yz(work, down_low, w.at[2:3], half, WD))
        work.add(scatter_x(work, parts_b, box_b, hop_b, land_b, GFFN))
        for half in (0, 1):
            work.add(scatter_yz(work, down_part, boxes.at[half], down_grad, half, DWD))
        work.add(compute(), 2)
        work.add(close_grad(), 1)

    units = 2 * HID
    group = [
        pltpu.VMEM((RING, 2, SHARD, WIDTH), BF16),
        pltpu.VMEM((RING, SHARD, WIDTH), BF16),
        pltpu.VMEM((2, SHARD // 2, WIDTH), BF16),
        pltpu.VMEM((2, SHARD, WIDTH), BF16),
    ]
    return call(
        "feed_forward",
        1,
        body,
        [
            (rows, ANY), (cot, ANY), (ffn, ANY), (ffn_wide, ANY), (residual, ANY), (cotangent, ANY), (gains, ANY),
        ],
        [
            (fl(SHARD, WIDTH), ANY), (bf(SHARD, WIDTH), ANY), (bf(RING, 2, SHARD, WIDTH), ANY), (fl(1, HID, CH), ANY),
            (bf(2, 2, HID, WIDTH), ANY), (fl(8, WIDTH), ANY),
        ],
        [
            pltpu.VMEM((2, WIDTH), F32),
            pltpu.VMEM((8, WIDTH), F32),
            pltpu.VMEM((RING, 2, SHARD, WIDTH), BF16),
            pltpu.VMEM((RING, 2, SHARD, WIDTH), BF16),
            pltpu.VMEM((3, 2, HID, WIDTH), BF16),
            pltpu.VMEM((1, 2, HID, WIDTH), BF16),
            pltpu.VMEM((HID, CH), F32),
            pltpu.VMEM((1, HID, CH), BF16),
            pltpu.VMEM((SHARD, WIDTH), F32),
            pltpu.VMEM((SHARD, WIDTH), F32),
            pltpu.VMEM((1, HID, CH), F32),
            pltpu.VMEM((RING, RUN, units), F32),
            pltpu.VMEM((RING, RUN, units), F32),
            pltpu.VMEM((RING, RUN, units), BF16),
            pltpu.VMEM((RING, RUN, units), BF16),
            pltpu.VMEM((RING, RUN, units), BF16),
            pltpu.VMEM((2, RUN, units), F32),
            pltpu.VMEM((SHARD, WIDTH), BF16),
            group[0],
            *group,
            pltpu.VMEM((2, 15, 1, HID, HALF), BF16),
        ],
        (90, 300, 20),
        X_WAYS + YZ_WAYS,
        int(27e9),
    )


def backward_mixer(
    grad_low, ffn_part, down_part, down_grad, normed, w_in, w_out, proj, near, far, taps, starts, tokens, residual,
    grad_residual, gains, gain_two,
):
    def body(
        work, low_in, ffn_part, down_in, down_grad, normed, w_in, w_out, proj_in, near_in, far_in, taps_in, starts,
        tokens_in, residual_in, grad_in, gains_in, gain_two_in,
        output_out, input_grad_out, mixer_grad_out, ffn_grad_out, small_final,
        near, far, taps, gains, gain_two, mixer_grad, small_out, down_parts, down_box, down_hop, down_land, residual,
        ffn_w, ffn_grad, ffn_boxes, tokens, grad_residual,
        ga, na, w, proj, ext, ahead, conv, gated, gp, near_next, far_next, tap_sum, gain_sum, small,
        new, parts, box, hop, land, box_cin, box_in, box_small,
    ):
        x, k = work.me["x"], work.me["k"]
        row, col = lax.axis_index("row"), lax.axis_index("col")
        late = (col // 2) % 2 == 1

        def mat_in():
            return w[0:3].reshape(3 * CH, WIDTH)

        ins = pieces(None, ffn_part.at[0], ffn_w.at[0], FFN_W0) + pieces(None, ffn_part.at[1], ffn_w.at[1], FFN_W1)
        ins += [(None, near_in, near, NEAR), (None, far_in, far, FAR), (None, taps_in, taps, TAPS)]
        ins += pieces(None, proj_in, proj, PROJ) + [(None, w_out, w.at[3:4], W_OUT)]
        ins += pieces(None, normed, na, NORMED_IN) + pieces(None, w_in, w.at[0:3], W_IN)
        ins += pieces(None, down_in, down_parts, DOWN_PARTS) + [
            (None, residual_in, residual, RESIDUAL),
            (None, down_grad, ffn_grad.at[2:3], DOWN_GRAD),
            (None, gains_in, gains, GAINS),
            (None, gain_two_in, gain_two, GAIN_TWO),
            (None, tokens_in, tokens, TOKENS),
            (None, grad_in, grad_residual, GRAD_RESIDUAL),
        ]
        work.set(START)

        def opening():
            yield START
            work.set((GRAD, GO))
            yield FFN_W1
            for half in (0, 1):
                work.set((DWG, GO, half))

        def in_grads(numbers):
            def columns(step, _):
                at = pl.ds(pl.multiple_of(step * 512, 512), 512)
                rows = na[:, :, :, at].reshape(RING * RUN, 512)
                for number in numbers:
                    left = gp[:, :, number * CH : (number + 1) * CH].reshape(RING * RUN, CH)
                    grad = dot_tn(left, rows)
                    old = w[number, :, :, at].reshape(CH, 512).astype(F32)
                    gain_sum[:, at] += jnp.sum((grad * old).reshape(CH // 8, 8, 512), axis=0)
                    new[(2, 0, 3)[number], :, :, at] = grad.astype(BF16).reshape(2, HALF, 512)
                return 0

            lax.fori_loop(0, WIDTH // 512, columns, 0)

        def compute():
            yield PROJ

            def mix(run, _):
                for at in range(0, RUN, 64):
                    rows = proj[run, at : at + 64]
                    ext[run, 8 + at : 8 + at + 64] = rows[:, :CH] * rows[:, 2 * CH :]
                return 0

            lax.fori_loop(0, RING, mix, 0)
            place_halo(ext, near, far)

            def convolve(run, _):
                for at in range(0, RUN, 64):
                    for lane in range(2):
                        lanes = slice(lane * HALF, (lane + 1) * HALF)
                        mixed, one, two = lags(ext, starts, run, at, lane)
                        tap = taps[lane]
                        total = tap[2:3] * mixed + tap[1:2] * one + tap[0:1] * two
                        gate = proj[run, at : at + 64, CH + lane * HALF : CH + (lane + 1) * HALF]
                        conv[run, at : at + 64, lanes] = total
                        gated[run, at : at + 64, lanes] = (gate * total).astype(BF16)
                return 0

            lax.fori_loop(0, RING, convolve, 0)
            yield 2.2
            yield W_OUT

            def gate_back(at):
                grad = dot_nt(ga[at].reshape(RUN, WIDTH), w[3].reshape(CH, WIDTH))
                ahead[at, 0:RUN] = grad * proj[at, :, CH : 2 * CH]
                gp[at, :, CH : 2 * CH] = (grad * conv[at]).astype(BF16)

            across, ahead_at, behind, own = ring_places(x)
            yield (GRAD, OWN)
            gate_back(own)
            yield 0.7
            yield (GRAD, NEAR)
            gate_back(behind)
            gate_back(ahead_at)
            yield 1.4
            yield (GRAD, ALL)
            gate_back(across)
            sent = [
                work.send(ahead.at[:, 0:8], near_next, ("z", 2)),
                work.send(ahead.at[0, 0:8], far_next, ("row", -1)),
            ]
            yield 0.7

            def out_grad(step, _):
                at = pl.ds(pl.multiple_of(step * 512, 512), 512)
                rows = ga[:, :, :, at].reshape(RING * RUN, 512)
                grad = dot_tn(gated[...].reshape(RING * RUN, CH), rows)
                new[1, :, :, at] = grad.astype(BF16).reshape(2, HALF, 512)
                return 0

            lax.fori_loop(0, WIDTH // 512, out_grad, 0)
            yield 1.7
            yield NORMED_IN
            yield W_IN
            gain_sum[...] = jnp.zeros_like(gain_sum)
            in_grads((1,))
            for half in (0, 1):
                work.set((CIN, GO, half))
            yield 1.6
            for copy in sent:
                yield copy
            last = jnp.where(row < ROWS - 1, far_next[...], 0.0)
            for run in range(RING):
                after = last if run == RING - 1 else near_next[run + 1]
                ahead[run, RUN : RUN + 8] = jnp.where(late, after, near_next[run])
            tap_sum[...] = jnp.zeros_like(tap_sum)

            def unmix(run, _):
                for at in range(0, RUN, 64):
                    for lane in range(2):
                        lanes = slice(lane * HALF, (lane + 1) * HALF)
                        rows = slice(at, at + 64)
                        first = run_start(run, RUN) + at
                        one, _two = keeps(starts, first + 1, (64, HALF))
                        _one, two = keeps(starts, first + 2, (64, HALF))
                        tap = taps[lane]
                        grad = ahead[run, rows, lanes]
                        mixed, lag_one, lag_two = lags(ext, starts, run, at, lane)
                        for number, value in enumerate((lag_two, lag_one, mixed)):
                            tap_sum[number, :, lanes] += jnp.sum((grad * value).reshape(8, 8, HALF), axis=0)
                        total = tap[2:3] * grad + tap[1:2] * (one * ahead[run, at + 1 : at + 65, lanes])
                        total = total + tap[0:1] * (two * ahead[run, at + 2 : at + 66, lanes])
                        conv_in = proj[run, rows, 2 * CH + lane * HALF : 2 * CH + (lane + 1) * HALF]
                        gate = proj[run, rows, lanes]
                        gp[run, rows, lanes] = (total * conv_in).astype(BF16)
                        gp[run, rows, 2 * CH + lane * HALF : 2 * CH + (lane + 1) * HALF] = (total * gate).astype(BF16)
                return 0

            lax.fori_loop(0, RING, unmix, 0)
            yield 3.0
            for number, at in enumerate(ring_places(x)):
                parts[at] = dot_nn(gp[at], mat_in()).astype(BF16).reshape(2, SHARD, WIDTH)
                work.set((NORMED, READY, number))
                yield 1.1
            in_grads((0, 2))
            yield GAIN_TWO
            small[...] = jnp.zeros_like(small)
            small[0:1] = jnp.sum(gain_sum[...], axis=0, keepdims=True) / gains[0:1]
            small[1:2] = jnp.sum(gain_two[...], axis=0, keepdims=True)
            mine = pl.ds(pl.multiple_of((x * 2 + k) * CH, CH), CH)
            for number in range(3):
                small[2 + number : 3 + number, mine] = jnp.sum(tap_sum[number], axis=0, keepdims=True)
            work.set((SMALL, GO))
            for half in (0, 1):
                work.set((IN, GO, half))
            yield 3.2
            yield DOWN_GRAD
            yield (DWG, DONE, 0)
            yield (DWG, DONE, 1)
            work.copy(ffn_grad, ffn_grad_out)
            for name in (CIN, IN):
                yield (name, DONE, 0)
                yield (name, DONE, 1)
            work.copy(mixer_grad, mixer_grad_out)
            yield (SMALL, DONE)
            work.copy(small_out, small_final)

        def close():
            yield (NORMED, DONE)
            yield TOKENS
            yield GRAD_RESIDUAL

            def one(at):
                grad = parts[x, k, at].astype(F32) + box[x, at].astype(F32)
                grad = grad + (land[0, at].astype(F32) + land[1, at].astype(F32))
                rows = tokens[at]
                scale = lax.rsqrt(jnp.mean(rows * rows, axis=1, keepdims=True) + NORM_EPS)
                normal = rows * scale
                scaled = grad * gains[0:1]
                back = scale * (scaled - normal * jnp.mean(scaled * normal, axis=1, keepdims=True))
                tokens[at] = grad_residual[at] + back

            strips(SHARD, 16, one)
            work.copy(tokens, input_grad_out)
            yield 1.2

        def close_down():
            yield DOWN_PARTS
            yield (GRAD, SIB, 7)
            for number in range(4):
                work.set((DOWN, READY, number))
            yield (DOWN, DONE)
            yield RESIDUAL

            def one(at):
                total = down_parts[x, k, at].astype(F32) + down_box[x, at].astype(F32)
                total = total + (down_land[0, at].astype(F32) + down_land[1, at].astype(F32))
                residual[at] = residual[at] + total

            strips(SHARD, 16, one)
            work.copy(residual, output_out)
            yield 0.4

        work.add(opening())
        work.add(gather_x(work, low_in, ga, GRAD, copy=True))
        work.add(stream(work, ins), 1)
        work.add(scatter_x(work, down_parts, down_box, down_hop, down_land, DOWN))
        work.add(scatter_x(work, parts, box, hop, land, NORMED))
        work.add(sum_all(work, small, box_small, small_out, SMALL))
        for half in (0, 1):
            work.add(scatter_yz(work, ffn_w, ffn_boxes.at[half], ffn_grad, half, DWG))
        for name, first, box_of, where in ((CIN, 0, box_cin, (1, 3)), (IN, 2, box_in, (0, 2))):
            for half in (0, 1):
                here = new.at[pl.ds(first, 2)]
                work.add(scatter_yz(work, here, box_of.at[half], mixer_grad, half, name, where))
        work.add(compute(), 1)
        work.add(close(), 1)
        work.add(close_down(), 2)

    return call(
        "backward_mixer",
        2,
        body,
        [
            (grad_low, ANY), (ffn_part, ANY), (down_part, ANY), (down_grad, ANY),
            (normed, ANY), (w_in, ANY), (w_out, ANY), (proj, ANY), (near, ANY), (far, ANY),
            (taps, ANY), (starts, SMEM), (tokens, ANY), (residual, ANY), (grad_residual, ANY), (gains, ANY),
            (gain_two, ANY),
        ],
        [
            (fl(SHARD, WIDTH), ANY), (fl(SHARD, WIDTH), ANY), (fl(4, CH, HALF), ANY), (fl(3, HID, CH), ANY),
            (fl(8, WIDTH), ANY),
        ],
        [
            pltpu.VMEM((RING, 8, CH), F32),
            pltpu.VMEM((8, CH), F32),
            pltpu.VMEM((2, 8, HALF), F32),
            pltpu.VMEM((2, WIDTH), F32),
            pltpu.VMEM((8, WIDTH), F32),
            pltpu.VMEM((4, CH, HALF), F32),
            pltpu.VMEM((8, WIDTH), F32),
            pltpu.VMEM((RING, 2, SHARD, WIDTH), BF16),
            pltpu.VMEM((RING, SHARD, WIDTH), BF16),
            pltpu.VMEM((2, SHARD // 2, WIDTH), BF16),
            pltpu.VMEM((2, SHARD, WIDTH), BF16),
            pltpu.VMEM((SHARD, WIDTH), F32),
            pltpu.VMEM((2, 2, HID, WIDTH), BF16),
            pltpu.VMEM((3, HID, CH), F32),
            pltpu.VMEM((2, 15, 2, HID, HALF), BF16),
            pltpu.VMEM((SHARD, WIDTH), F32),
            pltpu.VMEM((SHARD, WIDTH), F32),
            pltpu.VMEM((RING, 2, SHARD, WIDTH), BF16),
            pltpu.VMEM((RING, 2, SHARD, WIDTH), BF16),
            pltpu.VMEM((4, 2, HALF, WIDTH), BF16),
            pltpu.VMEM((RING, RUN, 3 * CH), F32),
            pltpu.VMEM((RING, RUN + 8, CH), F32),
            pltpu.VMEM((RING, RUN + 8, CH), F32),
            pltpu.VMEM((RING, RUN, CH), F32),
            pltpu.VMEM((RING, RUN, CH), BF16),
            pltpu.VMEM((RING, RUN, 3 * CH), BF16),
            pltpu.VMEM((RING, 8, CH), F32),
            pltpu.VMEM((8, CH), F32),
            pltpu.VMEM((3, 8, CH), F32),
            pltpu.VMEM((8, WIDTH), F32),
            pltpu.VMEM((8, WIDTH), F32),
            pltpu.VMEM((4, 2, HALF, WIDTH), BF16),
            pltpu.VMEM((RING, 2, SHARD, WIDTH), BF16),
            pltpu.VMEM((RING, SHARD, WIDTH), BF16),
            pltpu.VMEM((2, SHARD // 2, WIDTH), BF16),
            pltpu.VMEM((2, SHARD, WIDTH), BF16),
            *[pltpu.VMEM((2, 15, 2, HALF, HALF), BF16)] * 2,
            pltpu.VMEM((4, RING, 8, WIDTH), F32),
        ],
        (90, 300, 20),
        X_WAYS + YZ_WAYS + (("z", 2), ("y", 2), ("x", 2), ("row", -1)),
        int(9e9),
    )


def adam_update(weight, gradient, first, second, step_rate, decay_rate):
    first_new = BETA_ONE * first + (1.0 - BETA_ONE) * gradient
    second_new = BETA_TWO * second + (1.0 - BETA_TWO) * gradient * gradient
    first_hat = first_new / (1.0 - BETA_ONE**STEP)
    second_hat = second_new / (1.0 - BETA_TWO**STEP)
    weight_new = weight - step_rate * (
        first_hat / (jnp.sqrt(second_hat) + ADAM_EPS) + decay_rate * weight
    )
    return (weight_new, first_new, second_new)


def body(
    tokens,
    cotangent,
    doc_starts,
    mixer_w,
    ffn_w,
    gains,
    taps,
    mixer_m,
    mixer_v,
    ffn_m,
    ffn_v,
    gain_m,
    gain_v,
    tap_m,
    tap_v,
):
    col = lax.axis_index("col")
    ffn_turned = jnp.swapaxes(ffn_w, 1, 2)
    normed, cot, w_in, w_out, ffn, proj, near, far, taps_two, residual, rows = forward_mixer(
        tokens, cotangent, doc_starts, mixer_w, ffn_turned, gains, taps
    )
    grad_residual, grad_low, down_part, down_grad, ffn_part, gain_two = feed_forward(
        rows, cot, ffn, ffn_turned, residual, cotangent, gains
    )
    output, input_grad, mixer_grad, ffn_grad, total = backward_mixer(
        grad_low, ffn_part, down_part, down_grad, normed, w_in, w_out, proj, near, far, taps_two, doc_starts, tokens,
        residual, grad_residual, gains, gain_two,
    )
    ffn_grad = jnp.swapaxes(ffn_grad, 1, 2)
    gain_grad = total[:2]
    first = ((col // 4) * 2 + col % 2) * CH + (col // 2) % 2 * HALF
    tap_grad = lax.dynamic_slice_in_dim(total[2:5], first, HALF, 1)
    mixer_new, mixer_m_new, mixer_v_new = adam_update(
        mixer_w, mixer_grad, mixer_m, mixer_v, MATRIX_RATE, MATRIX_DECAY
    )
    ffn_new, ffn_m_new, ffn_v_new = adam_update(
        ffn_w, ffn_grad, ffn_m, ffn_v, MATRIX_RATE, MATRIX_DECAY
    )
    gain_new, gain_m_new, gain_v_new = adam_update(
        gains, gain_grad, gain_m, gain_v, SMALL_RATE, 0.0
    )
    tap_new, tap_m_new, tap_v_new = adam_update(taps, tap_grad, tap_m, tap_v, SMALL_RATE, 0.0)
    return (
        output,
        input_grad,
        mixer_grad,
        mixer_new,
        mixer_m_new,
        mixer_v_new,
        ffn_grad,
        ffn_new,
        ffn_m_new,
        ffn_v_new,
        gain_grad,
        gain_new,
        gain_m_new,
        gain_v_new,
        tap_grad,
        tap_new,
        tap_m_new,
        tap_v_new,
    )


def solution(mesh):
    placed = (
        P(("row", "col"), None),
        P(("row", "col"), None),
        P(),
        P(None, "row", "col"),
        P(None, "row", "col"),
        P(),
        P(None, "col"),
        P(None, "row", "col"),
        P(None, "row", "col"),
        P(None, "row", "col"),
        P(None, "row", "col"),
        P(),
        P(),
        P(None, "col"),
        P(None, "col"),
    )
    return jax.shard_map(
        body,
        mesh=mesh,
        in_specs=placed,
        out_specs=(
            P(("row", "col"), None),
            P(("row", "col"), None),
            P(None, "row", "col"),
            P(None, "row", "col"),
            P(None, "row", "col"),
            P(None, "row", "col"),
            P(None, "row", "col"),
            P(None, "row", "col"),
            P(None, "row", "col"),
            P(None, "row", "col"),
            P(),
            P(),
            P(),
            P(),
            P(None, "col"),
            P(None, "col"),
            P(None, "col"),
            P(None, "col"),
        ),
        check_vma=False,
    )
```

```python
import jax
import jax.numpy as jnp
from jax import lax
from jax.experimental import pallas as pl
from jax.experimental.pallas import tpu as pltpu
from jax.sharding import PartitionSpec as P

STEP = 5


NORM_EPS = 1e-05
BETA_ONE = 0.9
BETA_TWO = 0.95
ADAM_EPS = 1e-08
MATRIX_DECAY = 0.1
MATRIX_RATE = 0.03
SMALL_RATE = 0.3

MESH = pl.DeviceIdType.MESH
BF16 = jnp.bfloat16
F32 = jnp.float32
RING = 4
COT_HOLD = None
ROWS = 8
(
    CA, CIN, COT, COTANGENT, COT_LOW, DOWN, DOWN_GRAD, DOWN_PART, DOWN_PARTS, DWD, DWG, ENTRY, FAR,
    FFN_LOW, FFN_W0, FFN_W1, GAINS, GAIN_TWO, GATE, GFFN, GRAD, GRAD0, GRAD1, GRAD_RESIDUAL, IN, IN_OUT,
    MIX, NEAR, NORMED, NORMED_IN, NORMED_OUT, OUT, OUT0, OUT1, OUT_A, PROJ, PROJ_OUT, RESIDUAL, SMALL,
    START, TAPS, TAPS_SENT, TOKENS, UP, USED, W0, W1, W3, WD, WEIGHTS, W_IN, W_OUT, ALL, DONE, FIRST,
    GO, MOST, OWN, READY, SENT, SIB, SPREAD, SWAP,
) = range(63)

LINK = 42e3
CORES = 280e3
LINK_LAG, CORE_LAG = 3.0, 1.0
SEND_LAG = 5.0
WAIT = 0.05


def place():
    row, col = lax.axis_index("row"), lax.axis_index("col")
    return {"x": col // 4, "y": row // 2, "z": (col // 2) % 2 * 2 + row % 2, "k": col % 2}


def device_at(at):
    return (at["y"] * 2 + at["z"] % 2, at["x"] * 4 + at["z"] // 2 * 2 + at["k"])


def wrap(value, length=RING):
    return lax.rem(value + length, length)


def size_of(ref):
    size = jnp.dtype(ref.dtype).itemsize
    for extent in ref.shape:
        size *= extent
    return size


class Work:
    def __init__(self, send_sems, recv_sems, local_sems):
        self.me = place()
        self.send_sems, self.recv_sems, self.local_sems = send_sems, recv_sems, local_sems
        self.sending, self.local, self.kept, self.count = [], [], [], 0
        self.now, self.free, self.due, self.flags, self.chains = 0.0, {}, {}, set(), []

    def near(self, axis, step):
        at = dict(self.me)
        at[axis] = wrap(at[axis] + step, 2 if axis == "k" else RING)
        return device_at(at)

    def target(self, way):
        axis, step = way
        if axis == "row":
            row, col = lax.axis_index("row"), lax.axis_index("col")
            return (wrap(row + step, ROWS), col + 2 - 4 * ((col // 2) % 2))
        return self.near(axis, step)

    def barrier(self, ways):
        sem = pltpu.get_barrier_semaphore()
        for axis, step in ways:
            pl.semaphore_signal(sem, inc=1, device_id=self.target((axis, -step)), device_id_type=MESH)
        pl.semaphore_wait(sem, len(ways))

    def send(self, source, target, way):
        slot = len(self.sending)
        for number, (before, finish) in enumerate(self.sending):
            if finish + SEND_LAG < self.now:
                before.wait_send()
                slot = number
                break
        copy = pltpu.make_async_remote_copy(
            src_ref=source,
            dst_ref=target,
            send_sem=self.send_sems.at[slot],
            recv_sem=self.recv_sems.at[self.count],
            device_id=self.target(way),
            device_id_type=MESH,
        )
        copy.start()
        self.count += 1
        begin = max(self.now, self.free.get(way, 0.0))
        self.free[way] = begin + size_of(source) / (CORES if way[0] == "k" else LINK)
        self.sending[slot : slot + 1] = [(copy, self.free[way])]
        self.due[id(copy)] = self.free[way] + (CORE_LAG if way[0] == "k" else LINK_LAG)
        self.kept.append(copy)
        return copy

    def copy(self, source, target, rate=1.4e6):
        slot = len(self.local)
        for number, before in enumerate(self.local):
            if before is None:
                slot = number
                break
        copy = pltpu.make_async_copy(source, target, self.local_sems.at[slot])
        copy.start()
        begin = max(self.now, self.free.get(0, 0.0))
        self.free[0] = begin + size_of(source) / rate
        self.due[id(copy)] = self.free[0] + 0.5
        self.local[slot : slot + 1] = [copy]
        self.kept.append(copy)
        return copy

    def add(self, chain, rank=0):
        self.chains.append([next(chain), rank, len(self.chains), chain])

    def set(self, flag):
        self.flags.add(flag)

    def run(self):
        while self.chains:
            best, when = None, None
            for entry in self.chains:
                wish = entry[0]
                if isinstance(wish, (int, tuple)):
                    if wish not in self.flags:
                        continue
                    key = (0 if entry[1] == 0 else 1, entry[1], self.now, entry[2])
                elif isinstance(wish, float):
                    key = (0 if entry[1] == 0 else 1, entry[1], self.now, entry[2])
                else:
                    due = self.due[id(wish)]
                    if due <= self.now:
                        key = (0 if entry[1] == 0 else 1, entry[1], due, entry[2])
                    else:
                        key = (2, due, entry[1], entry[2])
                if best is None or key < when:
                    best, when = entry, key
            assert best is not None, self.flags
            wish = best[0]
            if not isinstance(wish, (int, tuple, float)):
                self.now = max(self.now, self.due[id(wish)]) + WAIT
                if any(wish is copy for copy in self.local):
                    wish.wait()
                    self.local = [None if copy is wish else copy for copy in self.local]
                else:
                    wish.wait_recv()
            try:
                best[0] = next(best[3])
                if isinstance(best[0], float):
                    self.now += best[0]
            except StopIteration:
                self.chains = [entry for entry in self.chains if entry is not best]
        for copy, _ in self.sending:
            copy.wait_send()
        for copy in self.local:
            if copy is not None:
                copy.wait()


def stream(work, items):
    pending = []
    for wait, source, target, done in items:
        if wait is not None:
            while pending:
                yield pending[0][0]
                work.set(pending.pop(0)[1])
            yield wait
        pending.append((work.copy(source, target), done))
        if len(pending) > 1:
            yield pending[0][0]
            work.set(pending.pop(0)[1])
    while pending:
        yield pending[0][0]
        work.set(pending.pop(0)[1])


def pieces(wait, source, target, done):
    count = source.shape[0]
    return [
        (wait if number == 0 else None, source.at[number], target.at[number], done if number == count - 1 else (done, number))
        for number in range(count)
    ]


def gather_x(work, source, out, name, copy=False, hold=None):
    x, k = work.me["x"], work.me["k"]
    rows = source.shape[0]
    half = rows // 2
    low, high = pl.ds(0, half), pl.ds(half, half)
    right, left, other = ("x", 1), ("x", -1), ("k", 1)
    ahead, behind, across = wrap(x + 1), wrap(x - 1), wrap(x + 2)
    sib, own = [], []

    def relay(at, part):
        sib.append(work.send(out.at[at, k, part], out.at[at, k, part], other))
        work.set((name, SIB, len(sib)))

    def siblings():
        for number in range(1, 8):
            yield (name, SIB, number)
            yield sib[number - 1]
            if number == 1 and copy:
                yield own[0]
            if number in (1, 5, 7):
                work.set((name, {1: OWN, 5: NEAR, 7: ALL}[number]))

    work.add(siblings())
    yield (name, GO)
    r0 = work.send(source.at[low], out.at[x, k, low], right)
    l1 = work.send(source.at[high], out.at[x, k, high], left)
    r1 = work.send(source.at[high], out.at[x, k, high], right)
    l0 = work.send(source.at[low], out.at[x, k, low], left)
    sib.append(work.send(source, out.at[x, k], other))
    if copy:
        own.append(work.copy(source, out.at[x, k]))
    work.set((name, SIB, 1))
    work.set((name, SENT))
    if hold is not None:
        yield hold
    yield r0
    far0 = work.send(out.at[behind, k, low], out.at[behind, k, low], right)
    relay(behind, low)
    yield l1
    far1 = work.send(out.at[ahead, k, high], out.at[ahead, k, high], left)
    relay(ahead, high)
    work.set((name, FAR))
    yield r1
    relay(behind, high)
    yield l0
    relay(ahead, low)
    yield far0
    relay(across, low)
    yield far1
    relay(across, high)


def add_into(target, first, second):
    rows, lanes = target.shape[-2:]
    if rows * lanes <= 1 << 15:
        target[...] = first[...] + second[...]
        return
    strip = 32

    def body(step, _):
        at = pl.ds(pl.multiple_of(step * strip, strip), strip)
        target[at] = first[at] + second[at]
        return 0

    lax.fori_loop(0, rows // strip, body, 0)


def ring_places(x):
    return (wrap(x + 2), wrap(x + 1), wrap(x - 1), x)


def scatter_x(work, parts, box, hop, land, name):
    x, k = work.me["x"], work.me["k"]
    rows = box.shape[1]
    half = rows // 2
    low, high = pl.ds(0, half), pl.ds(half, half)
    right, left, other = ("x", 1), ("x", -1), ("k", 1)
    across, ahead, behind, own = ring_places(x)

    def swap():
        sib = {}
        for number, at in enumerate((across, ahead, behind, own)):
            yield (name, READY, number)
            sib[number] = work.send(parts.at[at, 1 - k], box.at[at], other)
            got.append(sib[number])
            work.set((name, SWAP, number))

    got = []
    work.add(swap(), 0)
    yield (name, SWAP, 0)
    yield got[0]
    add_into(box.at[across], parts.at[across, k], box.at[across])
    far0 = work.send(box.at[across, low], hop.at[0], right)
    far1 = work.send(box.at[across, high], hop.at[1], left)
    yield 0.3
    yield (name, SWAP, 1)
    yield got[1]
    add_into(box.at[ahead], parts.at[ahead, k], box.at[ahead])
    r1 = work.send(box.at[ahead, high], land.at[0, high], right)
    yield 0.3
    yield (name, SWAP, 2)
    yield got[2]
    add_into(box.at[behind], parts.at[behind, k], box.at[behind])
    l0 = work.send(box.at[behind, low], land.at[1, low], left)
    yield 0.3
    yield far0
    add_into(box.at[ahead, low], box.at[ahead, low], hop.at[0])
    r0 = work.send(box.at[ahead, low], land.at[0, low], right)
    yield 0.15
    yield far1
    add_into(box.at[behind, high], box.at[behind, high], hop.at[1])
    l1 = work.send(box.at[behind, high], land.at[1, high], left)
    work.set((name, SENT))
    yield 0.15
    yield (name, SWAP, 3)
    yield got[3]
    for copy in (r1, l0, r0, l1):
        yield copy
    work.set((name, DONE))


def block(ref, y, z, half, rows):
    column = pl.multiple_of((y * 2 + z % 2) * 256 + half * 128, 128)
    return ref.at[:, z // 2, rows, pl.ds(column, 128)]


def gather_yz(work, source, out, half, name):
    first, second = ("y", "z") if half == 0 else ("z", "y")
    rows = source.shape[1]
    cut = rows // 2
    low, high, whole = pl.ds(0, cut), pl.ds(cut, cut), pl.ds(0, rows)
    a, b = work.me[first], work.me[second]

    def slot(at_a, at_b, part):
        y, z = (at_a, at_b) if half == 0 else (at_b, at_a)
        return block(out, y, z, half, part)

    columns = pl.ds(half * 128, 128)
    up, down, forward, backward = (first, 1), (first, -1), (second, 1), (second, -1)
    a_behind, a_ahead, a_across = wrap(a - 1), wrap(a + 1), wrap(a + 2)
    b_behind, b_ahead = wrap(b - 1), wrap(b + 1)
    yield (name, GO, half)
    mine = work.copy(source.at[:, :, columns], slot(a, b, whole))
    r0 = work.send(source.at[:, low, columns], slot(a, b, low), up)
    l1 = work.send(source.at[:, high, columns], slot(a, b, high), down)
    r1 = work.send(source.at[:, high, columns], slot(a, b, high), up)
    l0 = work.send(source.at[:, low, columns], slot(a, b, low), down)
    waits, last = [], []

    def spread(at, part, ref=None):
        ref = slot(at, b, part) if ref is None else ref
        waits.append(
            (
                at,
                part,
                work.send(ref, slot(at, b, part), forward),
                work.send(ref, slot(at, b, part), backward),
            )
        )

    def onward(number):
        at, part, plus, minus = waits[number]
        yield plus
        if part is low:
            last.append(work.send(slot(at, b_behind, part), slot(at, b_behind, part), forward))
        yield minus
        if part is high:
            last.append(work.send(slot(at, b_ahead, part), slot(at, b_ahead, part), backward))

    spread(a, low, source.at[:, low, columns])
    spread(a, high, source.at[:, high, columns])
    yield r0
    f0 = work.send(slot(a_behind, b, low), slot(a_behind, b, low), up)
    spread(a_behind, low)
    yield l1
    f1 = work.send(slot(a_ahead, b, high), slot(a_ahead, b, high), down)
    spread(a_ahead, high)
    yield from onward(0)
    yield r1
    spread(a_behind, high)
    yield l0
    spread(a_ahead, low)
    yield from onward(1)
    yield f0
    spread(a_across, low)
    yield f1
    spread(a_across, high)
    work.set((name, SPREAD, half))
    for number in range(2, 8):
        yield from onward(number)
        if number == 5:
            work.set((name, MOST, half))
    work.set((name, SENT, half))
    for copy in last:
        yield copy
    yield mine
    work.set((name, ALL, half))


def scatter_yz(work, parts, box, out, half, name, where=None):
    first, second = ("z", "y") if half == 0 else ("y", "z")
    rows = parts.shape[2]
    cut = rows // 2
    low, high, whole = pl.ds(0, cut), pl.ds(cut, cut), pl.ds(0, rows)
    a, b = work.me[first], work.me[second]

    def slot(at_a, at_b, part):
        y, z = (at_b, at_a) if half == 0 else (at_a, at_b)
        return block(parts, y, z, half, part)

    across, ahead, behind, own = ring_places(a)
    up, down = (first, 1), (first, -1)

    def first_ring(number, at_b):
        base = 3 * number
        pick = lambda at, part: slot(at, at_b, part)
        yield (name, GO, half)
        far0 = work.send(pick(across, low), box.at[base, :, low], up)
        far1 = work.send(pick(across, high), box.at[base, :, high], down)
        r1 = work.send(pick(ahead, high), box.at[base + 1, :, high], up)
        l0 = work.send(pick(behind, low), box.at[base + 2, :, low], down)
        yield far0
        add_into(pick(ahead, low), pick(ahead, low), box.at[base, :, low])
        r0 = work.send(pick(ahead, low), box.at[base + 1, :, low], up)
        yield far1
        add_into(pick(behind, high), pick(behind, high), box.at[base, :, high])
        l1 = work.send(pick(behind, high), box.at[base + 2, :, high], down)
        yield r1
        add_into(pick(own, high), pick(own, high), box.at[base + 1, :, high])
        yield l0
        add_into(pick(own, low), pick(own, low), box.at[base + 2, :, low])
        yield r0
        add_into(pick(own, low), pick(own, low), box.at[base + 1, :, low])
        yield l1
        add_into(pick(own, high), pick(own, high), box.at[base + 2, :, high])
        work.set((name, FIRST, half, number))

    places = ring_places(b)
    for number, at_b in enumerate(places):
        work.add(first_ring(number, at_b))
    b_across, b_ahead, b_behind, b_own = places
    forward, backward = (second, 1), (second, -1)
    yield (name, FIRST, half, 0)
    far0 = work.send(slot(a, b_across, low), box.at[12, :, low], forward)
    far1 = work.send(slot(a, b_across, high), box.at[12, :, high], backward)
    yield (name, FIRST, half, 1)
    r1 = work.send(slot(a, b_ahead, high), box.at[13, :, high], forward)
    yield far0
    add_into(slot(a, b_ahead, low), slot(a, b_ahead, low), box.at[12, :, low])
    r0 = work.send(slot(a, b_ahead, low), box.at[13, :, low], forward)
    yield (name, FIRST, half, 2)
    l0 = work.send(slot(a, b_behind, low), box.at[14, :, low], backward)
    yield far1
    add_into(slot(a, b_behind, high), slot(a, b_behind, high), box.at[12, :, high])
    l1 = work.send(slot(a, b_behind, high), box.at[14, :, high], backward)
    yield (name, FIRST, half, 3)
    mine = slot(a, b_own, whole)
    for copy in (r1, r0, l0, l1):
        yield copy
    for m in range(parts.shape[0]):
        total = mine[m].astype(F32) + box[13, m].astype(F32) + box[14, m].astype(F32)
        if where is not None:
            out[where[m], half * 128 : (half + 1) * 128, :] = total.T
        else:
            out[m, :, half * 128 : (half + 1) * 128] = total
    work.set((name, DONE, half))


def sum_all(work, values, box, out, name):
    yield (name, GO)
    out[...] = values[...]
    me = work.me
    for turn, axis in enumerate(("z", "y", "x", "k")):
        length = 2 if axis == "k" else RING
        mine = box.at[turn, me[axis]]
        mine[...] = out[...]
        copies = [work.send(mine, mine, (axis, step)) for step in range(1, length)]
        for copy in copies:
            yield copy
        total = box[turn, 0]
        for number in range(1, length):
            total = total + box[turn, number]
        out[...] = total
    work.set((name, DONE))


ANY = pl.BlockSpec(memory_space=pl.ANY)
VMEM = pl.BlockSpec(memory_space=pltpu.VMEM)
SMEM = pl.BlockSpec(memory_space=pltpu.SMEM)
X_WAYS = (("x", 1), ("x", -1), ("k", 1))
YZ_WAYS = (("y", 1), ("y", -1), ("z", 1), ("z", -1))


def bf(*shape):
    return jax.ShapeDtypeStruct(shape, BF16)


def fl(*shape):
    return jax.ShapeDtypeStruct(shape, F32)


def call(name, number, body, args, outs, scratch, copies, ways, flops, room):
    def kernel(*refs):
        main, sems = refs[:-3], refs[-3:]
        work = Work(*sems)
        body(work, *main)
        work.barrier(ways)
        work.run()
        used = (len(work.sending), work.count, len(work.local))
        assert all(one <= most for one, most in zip(used, copies)), used

    sems = [pltpu.SemaphoreType.DMA((count,)) for count in copies]
    return pl.pallas_call(
        kernel,
        out_shape=[shape for shape, _ in outs],
        in_specs=[spec for _, spec in args],
        out_specs=[spec for _, spec in outs],
        scratch_shapes=list(scratch) + sems,
        compiler_params=pltpu.CompilerParams(
            collective_id=number, has_side_effects=True, vmem_limit_bytes=room << 20
        ),
        cost_estimate=pl.CostEstimate(flops=flops, bytes_accessed=40 << 20, transcendentals=0),
        name=name,
    )(*[array for array, _ in args])


def dot_nt(left, right):
    return lax.dot_general(left, right, (((1,), (1,)), ((), ())), preferred_element_type=F32)


def dot_tn(left, right):
    return lax.dot_general(left, right, (((0,), (0,)), ((), ())), preferred_element_type=F32)


def dot_nn(left, right):
    return lax.dot_general(left, right, (((1,), (0,)), ((), ())), preferred_element_type=F32)


def strips(rows, strip, body):
    def one(step, _):
        body(pl.ds(pl.multiple_of(step * strip, strip), strip))
        return 0

    lax.fori_loop(0, rows // strip, one, 0)


def keeps(starts, first, shape):
    places = first + lax.broadcasted_iota(jnp.int32, shape, 0)

    def keep(at):
        hit = at == starts[0]
        for number in range(1, 4):
            hit = jnp.logical_or(hit, at == starts[number])
        return jnp.where(hit, 0.0, 1.0).astype(F32)

    here = keep(places)
    return here, here * keep(places - 1)


def run_start(run, run_tokens):
    row, col = lax.axis_index("row"), lax.axis_index("col")
    return ((row * RING + run) * 2 + (col // 2) % 2) * run_tokens


SHARD, WIDTH = 128, 2048
RUN = 2 * SHARD
CH, HALF = 256, 128
HID = 352


def lags(ext, starts, run, at, lane):
    rows = 64
    lanes = slice(lane * HALF, (lane + 1) * HALF)
    one, two = keeps(starts, run_start(run, RUN) + at, (rows, HALF))
    mixed = ext[run, 8 + at : 8 + at + rows, lanes]
    return mixed, one * ext[run, 7 + at : 7 + at + rows, lanes], two * ext[run, 6 + at : 6 + at + rows, lanes]


def place_halo(ext, near, far):
    row, col = lax.axis_index("row"), lax.axis_index("col")
    late = (col // 2) % 2 == 1
    first = jnp.where(row > 0, far[...], 0.0)
    for run in range(RING):
        ext[run, 0:8] = jnp.where(late, near[run], first if run == 0 else near[run - 1])


def forward_mixer(tokens, cotangent, starts, mixer, ffn, gains, taps):
    def body(
        work, tokens_in, cotangent_in, starts, mixer_in, ffn_in, gains_in, taps_in,
        normed_out, cot_out, in_out, mix_out, ffn_out, proj_out, near_final, far_final, taps_final, residual_out, low_out,
        gains, taps, near_out, far_out, taps_out, tokens, cotangent, mixer_wide, ffn_wide, mixer, ffn, tap_rows,
        normed, weights, proj, ext, gated, parts, box, hop, land, cot, residual, low_rows,
    ):
        x, k = work.me["x"], work.me["k"]
        z_hi = (lax.axis_index("col") // 2) % 2
        w_in, w_out = weights.at[0:3], weights.at[3:4]
        sent = {}

        def opening():
            loads = [work.copy(gains_in, gains), work.copy(tokens_in, tokens)]
            loads += [work.copy(mixer_in, mixer_wide), work.copy(taps_in, taps)]
            yield loads[0]
            yield loads[1]

            def norm(at):
                rows = tokens[at]
                scale = lax.rsqrt(jnp.mean(rows * rows, axis=1, keepdims=True) + NORM_EPS)
                normed[x, k, at] = (rows * scale * gains[0:1]).astype(BF16)

            strips(SHARD, 16, norm)
            work.set((NORMED, GO))
            yield 1.0
            yield loads[2]
            loads.append(work.copy(ffn_in.at[0:2], ffn_wide))
            for number in range(4):
                mixer[number] = mixer_wide[number].T.astype(BF16)
            work.set((IN, GO, 0))
            work.set((IN, GO, 1))
            yield 0.6
            loads.append(work.copy(cotangent_in, cotangent))
            yield loads[3]
            tap_rows[...] = jnp.zeros_like(tap_rows)
            tap_rows[0:3] = taps[...]
            taps_out[z_hi] = tap_rows[...]
            sent[TAPS] = work.send(tap_rows, taps_out.at[z_hi], ("z", 2))
            work.set(TAPS_SENT)
            yield loads[4]
            for number in range(2):
                for at in range(0, HID, 88):
                    ffn[number, at : at + 88] = ffn_wide[number, at : at + 88].astype(BF16)
            work.set(FFN_LOW)
            yield 0.5
            yield loads[5]

            def cast(at):
                cot[at] = cotangent[at].astype(BF16)

            strips(SHARD, 16, cast)
            work.set(COT_LOW)
            yield 0.5

        def compute():
            yield TAPS_SENT
            yield sent[TAPS]
            yield (NORMED, ALL)
            yield (IN, ALL, 0)
            yield (IN, ALL, 1)
            tail = normed[:, 1, SHARD - 16 :].reshape(RING * 16, WIDTH)
            ends = dot_nt(tail, weights[0:3].reshape(3 * CH, WIDTH))
            mixed = (ends[:, :CH] * ends[:, 2 * CH :]).reshape(RING, 16, CH)
            ext[:, RUN - 8 : RUN + 8] = mixed
            halo = [
                work.send(ext.at[:, RUN : RUN + 8], near_out, ("z", 2)),
                work.send(ext.at[RING - 1, RUN : RUN + 8], far_out, ("row", 1)),
            ]
            yield 1.0

            for half in range(2):
                rows = normed[2 * half : 2 * half + 2].reshape(2 * RUN, WIDTH)
                out = dot_nt(rows, weights[0:3].reshape(3 * CH, WIDTH))
                proj[2 * half : 2 * half + 2] = out.reshape(2, RUN, 3 * CH)
                yield 2.0
            work.set(PROJ)

            def mix(run, _):
                for at in range(0, RUN, 64):
                    size = 64 if at + 64 < RUN else 56
                    rows = proj[run, at : at + size]
                    ext[run, 8 + at : 8 + at + size] = rows[:, :CH] * rows[:, 2 * CH :]
                return 0

            lax.fori_loop(0, RING, mix, 0)
            yield 0.7
            for copy in halo:
                yield copy
            place_halo(ext, near_out, far_out)
            for source, target in ((near_out, near_final), (far_out, far_final), (taps_out, taps_final)):
                work.copy(source, target)

            def convolve(run, _):
                for at in range(0, RUN, 64):
                    for lane in range(2):
                        mixed, one, two = lags(ext, starts, run, at, lane)
                        tap = taps_out[lane]
                        total = tap[2:3] * mixed + tap[1:2] * one + tap[0:1] * two
                        gate = proj[run, at : at + 64, CH + lane * HALF : CH + (lane + 1) * HALF]
                        gated[run, at : at + 64, lane * HALF : (lane + 1) * HALF] = (gate * total).astype(BF16)
                return 0

            lax.fori_loop(0, RING, convolve, 0)
            yield 1.5
            yield (MIX, ALL, 0)
            yield (MIX, ALL, 1)
            work.set(WEIGHTS)
            for number, at in enumerate(ring_places(x)):
                out = dot_nn(gated[at], weights[3].reshape(CH, WIDTH))
                parts[at] = out.astype(BF16).reshape(2, SHARD, WIDTH)
                work.set((OUT, READY, number))
                yield 0.6
            yield (OUT, DONE)

            def close(at):
                total = parts[x, k, at].astype(F32) + box[x, at].astype(F32)
                total = total + (land[0, at].astype(F32) + land[1, at].astype(F32))
                rows = tokens[at] + total
                scale = lax.rsqrt(jnp.mean(rows * rows, axis=1, keepdims=True) + NORM_EPS)
                residual[at] = rows
                low_rows[at] = (rows * scale * gains[1:2]).astype(BF16)

            strips(SHARD, 16, close)
            work.copy(low_rows, low_out)
            work.copy(residual, residual_out)
            yield 1.0

        def order():
            yield (NORMED, FAR)
            yield COT_LOW
            work.set((COT, GO))

        def follow(half):
            yield FFN_LOW
            yield (IN, MOST, half)
            work.set((MIX, GO, half))
            yield (MIX, MOST, half)
            work.set((GATE, GO, half))
            yield (GATE, MOST, half)
            work.set((UP, GO, half))

        work.add(opening(), 1)
        work.add(gather_x(work, normed.at[x, k], normed, NORMED))
        for half in (0, 1):
            work.add(gather_yz(work, mixer.at[0:3], w_in, half, IN))
        for half in (0, 1):
            work.add(gather_yz(work, mixer.at[3:4], w_out, half, MIX))
        for number, name in enumerate((GATE, UP)):
            for half in (0, 1):
                mat = pl.ds(number, 1)
                work.add(gather_yz(work, ffn.at[mat], ffn_out.at[mat], half, name))
        work.add(scatter_x(work, parts, box, hop, land, OUT))
        work.add(gather_x(work, cot, cot_out, COT, copy=True, hold=COT_HOLD), 0)
        outs = pieces((NORMED, ALL), normed, normed_out, NORMED_OUT)
        outs += pieces(PROJ, proj, proj_out, PROJ_OUT)
        outs += pieces(WEIGHTS, weights.at[0:3], in_out, IN_OUT) + pieces(WEIGHTS, weights.at[3:4], mix_out, W3)
        work.add(stream(work, outs), 3)
        work.add(order())
        work.add(follow(0))
        work.add(follow(1))
        work.add(compute(), 1)

    gathered = bf(RING, 2, SHARD, WIDTH)
    return call(
        "forward_mixer",
        0,
        body,
        [(tokens, ANY), (cotangent, ANY), (starts, SMEM), (mixer, ANY), (ffn, ANY), (gains, ANY), (taps, ANY)],
        [
            (gathered, ANY), (gathered, ANY), (bf(3, 2, HALF, WIDTH), ANY), (bf(1, 2, HALF, WIDTH), ANY),
            (bf(2, 2, HID, WIDTH), ANY), (fl(RING, RUN, 3 * CH), ANY), (fl(RING, 8, CH), ANY), (fl(8, CH), ANY),
            (fl(2, 8, HALF), ANY), (fl(SHARD, WIDTH), ANY), (bf(SHARD, WIDTH), ANY),
        ],
        [
            pltpu.VMEM((2, WIDTH), F32),
            pltpu.VMEM((3, HALF), F32),
            pltpu.VMEM((RING, 8, CH), F32),
            pltpu.VMEM((8, CH), F32),
            pltpu.VMEM((2, 8, HALF), F32),
            pltpu.VMEM((SHARD, WIDTH), F32),
            pltpu.VMEM((SHARD, WIDTH), F32),
            pltpu.VMEM((4, CH, HALF), F32),
            pltpu.VMEM((2, HID, CH), F32),
            pltpu.VMEM((4, HALF, CH), BF16),
            pltpu.VMEM((2, HID, CH), BF16),
            pltpu.VMEM((8, HALF), F32),
            pltpu.VMEM((RING, 2, SHARD, WIDTH), BF16),
            pltpu.VMEM((4, 2, HALF, WIDTH), BF16),
            pltpu.VMEM((RING, RUN, 3 * CH), F32),
            pltpu.VMEM((RING, RUN + 8, CH), F32),
            pltpu.VMEM((RING, RUN, CH), BF16),
            pltpu.VMEM((RING, 2, SHARD, WIDTH), BF16),
            pltpu.VMEM((RING, SHARD, WIDTH), BF16),
            pltpu.VMEM((2, SHARD // 2, WIDTH), BF16),
            pltpu.VMEM((2, SHARD, WIDTH), BF16),
            pltpu.VMEM((SHARD, WIDTH), BF16),
            pltpu.VMEM((SHARD, WIDTH), F32),
            pltpu.VMEM((SHARD, WIDTH), BF16),
        ],
        (90, 300, 20),
        X_WAYS + YZ_WAYS + (("z", 2), ("row", 1)),
        int(5e9),
        63,
    )


def feed_forward(rows, cot, ffn, ffn_wide, residual, cotangent, gains):
    def body(
        work, rows_in, cot, ffn, ffn_wide, residual_in, cotangent_in, gains_in,
        grad_out, low_out, down_out, down_grad_out, part_out, gain_out,
        gains, gain_part, fa, ca, w, down_part, down_wide, down_low, residual, cotangent, down_grad,
        gate, up, hid, gg, gu, gh, grad_low,
        parts_a, parts_b, box_b, hop_b, land_b, boxes,
    ):
        x, k = work.me["x"], work.me["k"]
        units = 2 * HID

        def mat(number):
            return w[number].reshape(units, WIDTH)

        def weight_grad(out, left, right):
            for step in range(WIDTH // 512):
                at = pl.ds(step * 512, 512)
                rows = right[:, :, :, at].reshape(RING * RUN, 512)
                grad = dot_tn(left[...].reshape(RING * RUN, units), rows)
                out[:, :, at] = grad.astype(BF16).reshape(2, HID, 512)
                yield 1.0

        def opening():
            yield START
            work.set((ENTRY, GO))
            yield work.copy(ffn_wide.at[2], down_wide)
            for at in range(0, HID, 88):
                down_low[0, at : at + 88] = down_wide[at : at + 88].astype(BF16)
            work.set((WD, GO, 0))
            work.set((WD, GO, 1))
            yield 0.2

        work.set(START)
        ins = pieces((WD, GO, 1), ffn.at[0], w.at[0], W0) + pieces(None, ffn.at[1], w.at[1], W1)
        ins += pieces(None, cot, ca, CA)
        ins += [(None, residual_in, residual, RESIDUAL), (None, cotangent_in, cotangent, COTANGENT), (None, gains_in, gains, GAINS)]
        outs = pieces(DOWN_PART, parts_a, down_out, OUT_A) + pieces(GRAD0, w.at[0], part_out.at[0], OUT0)
        outs += pieces(GRAD1, w.at[1], part_out.at[1], OUT1)

        def compute():
            across, ahead, behind, own = ring_places(x)

            def forward(at):
                rows = fa[at].reshape(RUN, WIDTH)
                gate[at] = dot_nt(rows, mat(0))
                up[at] = dot_nt(rows, mat(1))

                def activate(here):
                    value = gate[at, here]
                    hid[at, here] = (value * jax.nn.sigmoid(value) * up[at, here]).astype(BF16)

                strips(RUN, 16, activate)

            yield (ENTRY, OWN)
            yield W0
            yield W1
            forward(own)
            yield 2.9
            yield (ENTRY, NEAR)
            forward(behind)
            yield 2.9
            forward(ahead)
            yield 2.9
            yield (ENTRY, ALL)
            forward(across)
            yield 2.9
            yield CA
            yield from weight_grad(down_part.at[0], hid, ca)
            for half in (0, 1):
                work.set((DWD, GO, half))
            yield (WD, ALL, 0)
            yield (WD, ALL, 1)
            for pair in (0, 1):
                gh[...] = dot_nt(ca[pl.ds(2 * pair, 2)].reshape(2 * RUN, WIDTH), mat(2)).reshape(2, RUN, units)
                yield 2.0

                def one(at):
                    for here in (0, 1):
                        run = 2 * pair + here
                        value, grad = gate[run, at], gh[here, at]
                        sig = jax.nn.sigmoid(value)
                        gg[run, at] = (grad * up[run, at] * sig * (1.0 + value * (1.0 - sig))).astype(BF16)
                        gu[run, at] = (grad * (value * sig)).astype(BF16)

                strips(RUN, 16, one)
                yield 1.5
            for number, at in enumerate(ring_places(x)):
                grad = dot_nn(gg[at], mat(0)) + dot_nn(gu[at], mat(1))
                parts_b[at] = grad.astype(BF16).reshape(2, SHARD, WIDTH)
                work.set((GFFN, READY, number))
                yield 2.2
            for at in range(RING):
                parts_a[at] = dot_nn(hid[at], mat(2)).astype(BF16).reshape(2, SHARD, WIDTH)
                yield 1.1
            work.set(DOWN_PART)
            yield from weight_grad(w.at[0], gg, fa)
            work.set(GRAD0)
            yield from weight_grad(w.at[1], gu, fa)
            work.set(GRAD1)
            yield (DWD, DONE, 0)
            yield (DWD, DONE, 1)
            work.copy(down_grad, down_grad_out)

        def close_grad():
            yield (GFFN, DONE)
            yield RESIDUAL
            yield GAINS
            gain_part[...] = jnp.zeros_like(gain_part)

            def one(at):
                grad = parts_b[x, k, at].astype(F32) + box_b[x, at].astype(F32)
                grad = grad + (land_b[0, at].astype(F32) + land_b[1, at].astype(F32))
                rows = residual[at]
                scale = lax.rsqrt(jnp.mean(rows * rows, axis=1, keepdims=True) + NORM_EPS)
                normal = rows * scale
                gain = grad * normal
                gain_part[...] += gain[:8] + gain[8:]
                scaled = grad * gains[1:2]
                back = scale * (scaled - normal * jnp.mean(scaled * normal, axis=1, keepdims=True))
                total = cotangent[at] + back
                cotangent[at] = total
                grad_low[at] = total.astype(BF16)

            strips(SHARD, 16, one)
            work.copy(grad_low, low_out)
            work.copy(cotangent, grad_out)
            work.copy(gain_part, gain_out)
            yield 1.5

        work.add(opening(), 0)
        work.add(stream(work, ins), 1)
        work.add(stream(work, outs), 1)
        work.add(gather_x(work, rows_in, fa, ENTRY, copy=True))
        for half in (0, 1):
            work.add(gather_yz(work, down_low, w.at[2:3], half, WD))
        work.add(scatter_x(work, parts_b, box_b, hop_b, land_b, GFFN))
        for half in (0, 1):
            work.add(scatter_yz(work, down_part, boxes.at[half], down_grad, half, DWD))
        work.add(compute(), 2)
        work.add(close_grad(), 1)

    units = 2 * HID
    group = [
        pltpu.VMEM((RING, 2, SHARD, WIDTH), BF16),
        pltpu.VMEM((RING, SHARD, WIDTH), BF16),
        pltpu.VMEM((2, SHARD // 2, WIDTH), BF16),
        pltpu.VMEM((2, SHARD, WIDTH), BF16),
    ]
    return call(
        "feed_forward",
        1,
        body,
        [
            (rows, ANY), (cot, ANY), (ffn, ANY), (ffn_wide, ANY), (residual, ANY), (cotangent, ANY), (gains, ANY),
        ],
        [
            (fl(SHARD, WIDTH), ANY), (bf(SHARD, WIDTH), ANY), (bf(RING, 2, SHARD, WIDTH), ANY), (fl(1, HID, CH), ANY),
            (bf(2, 2, HID, WIDTH), ANY), (fl(8, WIDTH), ANY),
        ],
        [
            pltpu.VMEM((2, WIDTH), F32),
            pltpu.VMEM((8, WIDTH), F32),
            pltpu.VMEM((RING, 2, SHARD, WIDTH), BF16),
            pltpu.VMEM((RING, 2, SHARD, WIDTH), BF16),
            pltpu.VMEM((3, 2, HID, WIDTH), BF16),
            pltpu.VMEM((1, 2, HID, WIDTH), BF16),
            pltpu.VMEM((HID, CH), F32),
            pltpu.VMEM((1, HID, CH), BF16),
            pltpu.VMEM((SHARD, WIDTH), F32),
            pltpu.VMEM((SHARD, WIDTH), F32),
            pltpu.VMEM((1, HID, CH), F32),
            pltpu.VMEM((RING, RUN, units), F32),
            pltpu.VMEM((RING, RUN, units), F32),
            pltpu.VMEM((RING, RUN, units), BF16),
            pltpu.VMEM((RING, RUN, units), BF16),
            pltpu.VMEM((RING, RUN, units), BF16),
            pltpu.VMEM((2, RUN, units), F32),
            pltpu.VMEM((SHARD, WIDTH), BF16),
            group[0],
            *group,
            pltpu.VMEM((2, 15, 1, HID, HALF), BF16),
        ],
        (90, 300, 20),
        X_WAYS + YZ_WAYS,
        int(27e9),
        63,
    )


def backward_mixer(
    grad_low, ffn_part, down_part, down_grad, normed, w_in, w_out, proj, near, far, taps, starts, tokens, residual,
    grad_residual, gains, gain_two,
):
    def body(
        work, low_in, ffn_part, down_in, down_grad, normed, w_in, w_out, proj_in, near_in, far_in, taps_in, starts,
        tokens_in, residual_in, grad_in, gains_in, gain_two_in,
        output_out, input_grad_out, mixer_grad_out, ffn_grad_out, small_final,
        near, far, taps, gains, gain_two, mixer_grad, small_out, down_parts, down_box, down_hop, down_land, residual,
        ffn_w, ffn_grad, ffn_boxes, tokens, grad_residual,
        ga, na, w, proj, ext, ahead, conv, gated, gp, near_next, far_next, tap_sum, gain_sum, small,
        new, parts, box, hop, land, box_cin, box_in, box_small,
    ):
        x, k = work.me["x"], work.me["k"]
        row, col = lax.axis_index("row"), lax.axis_index("col")
        late = (col // 2) % 2 == 1

        def mat_in():
            return w[0:3].reshape(3 * CH, WIDTH)

        ins = pieces(None, ffn_part.at[0], ffn_w.at[0], FFN_W0) + pieces(None, ffn_part.at[1], ffn_w.at[1], FFN_W1)
        ins += [(None, near_in, near, NEAR), (None, far_in, far, FAR), (None, taps_in, taps, TAPS)]
        ins += pieces(None, proj_in, proj, PROJ) + [(None, w_out, w.at[3:4], W_OUT)]
        ins += pieces(None, normed, na, NORMED_IN) + pieces(None, w_in, w.at[0:3], W_IN)
        ins += pieces(None, down_in, down_parts, DOWN_PARTS) + [
            (None, residual_in, residual, RESIDUAL),
            (None, down_grad, ffn_grad.at[2:3], DOWN_GRAD),
            (None, gains_in, gains, GAINS),
            (None, gain_two_in, gain_two, GAIN_TWO),
            (None, tokens_in, tokens, TOKENS),
            (None, grad_in, grad_residual, GRAD_RESIDUAL),
        ]
        work.set(START)

        def opening():
            yield START
            work.set((GRAD, GO))
            yield FFN_W1
            for half in (0, 1):
                work.set((DWG, GO, half))

        def in_grads(numbers):
            for step in range(WIDTH // 512):
                at = pl.ds(step * 512, 512)
                rows = na[:, :, :, at].reshape(RING * RUN, 512)
                for number in numbers:
                    left = gp[:, :, number * CH : (number + 1) * CH].reshape(RING * RUN, CH)
                    grad = dot_tn(left, rows)
                    old = w[number, :, :, at].reshape(CH, 512).astype(F32)
                    gain_sum[:, at] += jnp.sum((grad * old).reshape(CH // 8, 8, 512), axis=0)
                    new[(2, 0, 3)[number], :, :, at] = grad.astype(BF16).reshape(2, HALF, 512)
                yield 0.4 * len(numbers)

        def compute():
            yield PROJ

            def mix(run, _):
                for at in range(0, RUN, 64):
                    rows = proj[run, at : at + 64]
                    ext[run, 8 + at : 8 + at + 64] = rows[:, :CH] * rows[:, 2 * CH :]
                return 0

            lax.fori_loop(0, RING, mix, 0)
            place_halo(ext, near, far)

            def convolve(run, _):
                for at in range(0, RUN, 64):
                    for lane in range(2):
                        lanes = slice(lane * HALF, (lane + 1) * HALF)
                        mixed, one, two = lags(ext, starts, run, at, lane)
                        tap = taps[lane]
                        total = tap[2:3] * mixed + tap[1:2] * one + tap[0:1] * two
                        gate = proj[run, at : at + 64, CH + lane * HALF : CH + (lane + 1) * HALF]
                        conv[run, at : at + 64, lanes] = total
                        gated[run, at : at + 64, lanes] = (gate * total).astype(BF16)
                return 0

            lax.fori_loop(0, RING, convolve, 0)
            yield 2.2
            yield W_OUT

            def gate_back(at):
                grad = dot_nt(ga[at].reshape(RUN, WIDTH), w[3].reshape(CH, WIDTH))
                ahead[at, 0:RUN] = grad * proj[at, :, CH : 2 * CH]
                gp[at, :, CH : 2 * CH] = (grad * conv[at]).astype(BF16)

            across, ahead_at, behind, own = ring_places(x)
            yield (GRAD, OWN)
            gate_back(own)
            yield 0.7
            yield (GRAD, NEAR)
            gate_back(behind)
            gate_back(ahead_at)
            yield 1.4
            yield (GRAD, ALL)
            gate_back(across)
            sent = [
                work.send(ahead.at[:, 0:8], near_next, ("z", 2)),
                work.send(ahead.at[0, 0:8], far_next, ("row", -1)),
            ]
            yield 0.7

            def out_grad(step, _):
                at = pl.ds(pl.multiple_of(step * 512, 512), 512)
                rows = ga[:, :, :, at].reshape(RING * RUN, 512)
                grad = dot_tn(gated[...].reshape(RING * RUN, CH), rows)
                new[1, :, :, at] = grad.astype(BF16).reshape(2, HALF, 512)
                return 0

            lax.fori_loop(0, WIDTH // 512, out_grad, 0)
            yield 1.7
            yield NORMED_IN
            yield W_IN
            gain_sum[...] = jnp.zeros_like(gain_sum)
            yield from in_grads((1,))
            for half in (0, 1):
                work.set((CIN, GO, half))
            for copy in sent:
                yield copy
            last = jnp.where(row < ROWS - 1, far_next[...], 0.0)
            for run in range(RING):
                after = last if run == RING - 1 else near_next[run + 1]
                ahead[run, RUN : RUN + 8] = jnp.where(late, after, near_next[run])
            tap_sum[...] = jnp.zeros_like(tap_sum)

            def unmix(run, _):
                for at in range(0, RUN, 64):
                    for lane in range(2):
                        lanes = slice(lane * HALF, (lane + 1) * HALF)
                        rows = slice(at, at + 64)
                        first = run_start(run, RUN) + at
                        one, _two = keeps(starts, first + 1, (64, HALF))
                        _one, two = keeps(starts, first + 2, (64, HALF))
                        tap = taps[lane]
                        grad = ahead[run, rows, lanes]
                        mixed, lag_one, lag_two = lags(ext, starts, run, at, lane)
                        for number, value in enumerate((lag_two, lag_one, mixed)):
                            tap_sum[number, :, lanes] += jnp.sum((grad * value).reshape(8, 8, HALF), axis=0)
                        total = tap[2:3] * grad + tap[1:2] * (one * ahead[run, at + 1 : at + 65, lanes])
                        total = total + tap[0:1] * (two * ahead[run, at + 2 : at + 66, lanes])
                        conv_in = proj[run, rows, 2 * CH + lane * HALF : 2 * CH + (lane + 1) * HALF]
                        gate = proj[run, rows, lanes]
                        gp[run, rows, lanes] = (total * conv_in).astype(BF16)
                        gp[run, rows, 2 * CH + lane * HALF : 2 * CH + (lane + 1) * HALF] = (total * gate).astype(BF16)
                return 0

            lax.fori_loop(0, RING, unmix, 0)
            yield 3.0
            for number, at in enumerate(ring_places(x)):
                parts[at] = dot_nn(gp[at], mat_in()).astype(BF16).reshape(2, SHARD, WIDTH)
                work.set((NORMED, READY, number))
                yield 1.1
            yield from in_grads((0, 2))
            yield GAIN_TWO
            small[...] = jnp.zeros_like(small)
            small[0:1] = jnp.sum(gain_sum[...], axis=0, keepdims=True) / gains[0:1]
            small[1:2] = jnp.sum(gain_two[...], axis=0, keepdims=True)
            mine = pl.ds(pl.multiple_of((x * 2 + k) * CH, CH), CH)
            for number in range(3):
                small[2 + number : 3 + number, mine] = jnp.sum(tap_sum[number], axis=0, keepdims=True)
            work.set((SMALL, GO))
            for half in (0, 1):
                work.set((IN, GO, half))
            yield 0.2
            yield DOWN_GRAD
            yield (DWG, DONE, 0)
            yield (DWG, DONE, 1)
            work.copy(ffn_grad, ffn_grad_out)
            for name in (CIN, IN):
                yield (name, DONE, 0)
                yield (name, DONE, 1)
            work.copy(mixer_grad, mixer_grad_out)
            yield (SMALL, DONE)
            work.copy(small_out, small_final)

        def close():
            yield (NORMED, DONE)
            yield TOKENS
            yield GRAD_RESIDUAL

            def one(at):
                grad = parts[x, k, at].astype(F32) + box[x, at].astype(F32)
                grad = grad + (land[0, at].astype(F32) + land[1, at].astype(F32))
                rows = tokens[at]
                scale = lax.rsqrt(jnp.mean(rows * rows, axis=1, keepdims=True) + NORM_EPS)
                normal = rows * scale
                scaled = grad * gains[0:1]
                back = scale * (scaled - normal * jnp.mean(scaled * normal, axis=1, keepdims=True))
                tokens[at] = grad_residual[at] + back

            strips(SHARD, 16, one)
            work.copy(tokens, input_grad_out)
            yield 1.2

        def close_down():
            yield DOWN_PARTS
            yield (GRAD, SIB, 7)
            for number in range(4):
                work.set((DOWN, READY, number))
            yield (DOWN, DONE)
            yield RESIDUAL

            def one(at):
                total = down_parts[x, k, at].astype(F32) + down_box[x, at].astype(F32)
                total = total + (down_land[0, at].astype(F32) + down_land[1, at].astype(F32))
                residual[at] = residual[at] + total

            strips(SHARD, 16, one)
            work.copy(residual, output_out)
            yield 0.4

        work.add(opening())
        work.add(gather_x(work, low_in, ga, GRAD, copy=True))
        work.add(stream(work, ins), 1)
        work.add(scatter_x(work, down_parts, down_box, down_hop, down_land, DOWN))
        work.add(scatter_x(work, parts, box, hop, land, NORMED))
        work.add(sum_all(work, small, box_small, small_out, SMALL))
        for half in (0, 1):
            work.add(scatter_yz(work, ffn_w, ffn_boxes.at[half], ffn_grad, half, DWG))
        for name, first, box_of, where in ((CIN, 0, box_cin, (1, 3)), (IN, 2, box_in, (0, 2))):
            for half in (0, 1):
                here = new.at[pl.ds(first, 2)]
                work.add(scatter_yz(work, here, box_of.at[half], mixer_grad, half, name, where))
        work.add(compute(), 1)
        work.add(close(), 1)
        work.add(close_down(), 2)

    return call(
        "backward_mixer",
        2,
        body,
        [
            (grad_low, ANY), (ffn_part, ANY), (down_part, ANY), (down_grad, ANY),
            (normed, ANY), (w_in, ANY), (w_out, ANY), (proj, ANY), (near, ANY), (far, ANY),
            (taps, ANY), (starts, SMEM), (tokens, ANY), (residual, ANY), (grad_residual, ANY), (gains, ANY),
            (gain_two, ANY),
        ],
        [
            (fl(SHARD, WIDTH), ANY), (fl(SHARD, WIDTH), ANY), (fl(4, CH, HALF), ANY), (fl(3, HID, CH), ANY),
            (fl(8, WIDTH), ANY),
        ],
        [
            pltpu.VMEM((RING, 8, CH), F32),
            pltpu.VMEM((8, CH), F32),
            pltpu.VMEM((2, 8, HALF), F32),
            pltpu.VMEM((2, WIDTH), F32),
            pltpu.VMEM((8, WIDTH), F32),
            pltpu.VMEM((4, CH, HALF), F32),
            pltpu.VMEM((8, WIDTH), F32),
            pltpu.VMEM((RING, 2, SHARD, WIDTH), BF16),
            pltpu.VMEM((RING, SHARD, WIDTH), BF16),
            pltpu.VMEM((2, SHARD // 2, WIDTH), BF16),
            pltpu.VMEM((2, SHARD, WIDTH), BF16),
            pltpu.VMEM((SHARD, WIDTH), F32),
            pltpu.VMEM((2, 2, HID, WIDTH), BF16),
            pltpu.VMEM((3, HID, CH), F32),
            pltpu.VMEM((2, 15, 2, HID, HALF), BF16),
            pltpu.VMEM((SHARD, WIDTH), F32),
            pltpu.VMEM((SHARD, WIDTH), F32),
            pltpu.VMEM((RING, 2, SHARD, WIDTH), BF16),
            pltpu.VMEM((RING, 2, SHARD, WIDTH), BF16),
            pltpu.VMEM((4, 2, HALF, WIDTH), BF16),
            pltpu.VMEM((RING, RUN, 3 * CH), F32),
            pltpu.VMEM((RING, RUN + 8, CH), F32),
            pltpu.VMEM((RING, RUN + 8, CH), F32),
            pltpu.VMEM((RING, RUN, CH), F32),
            pltpu.VMEM((RING, RUN, CH), BF16),
            pltpu.VMEM((RING, RUN, 3 * CH), BF16),
            pltpu.VMEM((RING, 8, CH), F32),
            pltpu.VMEM((8, CH), F32),
            pltpu.VMEM((3, 8, CH), F32),
            pltpu.VMEM((8, WIDTH), F32),
            pltpu.VMEM((8, WIDTH), F32),
            pltpu.VMEM((4, 2, HALF, WIDTH), BF16),
            pltpu.VMEM((RING, 2, SHARD, WIDTH), BF16),
            pltpu.VMEM((RING, SHARD, WIDTH), BF16),
            pltpu.VMEM((2, SHARD // 2, WIDTH), BF16),
            pltpu.VMEM((2, SHARD, WIDTH), BF16),
            *[pltpu.VMEM((2, 15, 2, HALF, HALF), BF16)] * 2,
            pltpu.VMEM((4, RING, 8, WIDTH), F32),
        ],
        (90, 300, 20),
        X_WAYS + YZ_WAYS + (("z", 2), ("y", 2), ("x", 2), ("row", -1)),
        int(9e9),
        63,
    )


def adam_update(weight, gradient, first, second, step_rate, decay_rate):
    first_new = BETA_ONE * first + (1.0 - BETA_ONE) * gradient
    second_new = BETA_TWO * second + (1.0 - BETA_TWO) * gradient * gradient
    first_hat = first_new / (1.0 - BETA_ONE**STEP)
    second_hat = second_new / (1.0 - BETA_TWO**STEP)
    weight_new = weight - step_rate * (
        first_hat / (jnp.sqrt(second_hat) + ADAM_EPS) + decay_rate * weight
    )
    return (weight_new, first_new, second_new)


def body(
    tokens,
    cotangent,
    doc_starts,
    mixer_w,
    ffn_w,
    gains,
    taps,
    mixer_m,
    mixer_v,
    ffn_m,
    ffn_v,
    gain_m,
    gain_v,
    tap_m,
    tap_v,
):
    col = lax.axis_index("col")
    ffn_turned = jnp.swapaxes(ffn_w, 1, 2)
    normed, cot, w_in, w_out, ffn, proj, near, far, taps_two, residual, rows = forward_mixer(
        tokens, cotangent, doc_starts, mixer_w, ffn_turned, gains, taps
    )
    grad_residual, grad_low, down_part, down_grad, ffn_part, gain_two = feed_forward(
        rows, cot, ffn, ffn_turned, residual, cotangent, gains
    )
    output, input_grad, mixer_grad, ffn_grad, total = backward_mixer(
        grad_low, ffn_part, down_part, down_grad, normed, w_in, w_out, proj, near, far, taps_two, doc_starts, tokens,
        residual, grad_residual, gains, gain_two,
    )
    ffn_grad = jnp.swapaxes(ffn_grad, 1, 2)
    gain_grad = total[:2]
    first = ((col // 4) * 2 + col % 2) * CH + (col // 2) % 2 * HALF
    tap_grad = lax.dynamic_slice_in_dim(total[2:5], first, HALF, 1)
    mixer_new, mixer_m_new, mixer_v_new = adam_update(
        mixer_w, mixer_grad, mixer_m, mixer_v, MATRIX_RATE, MATRIX_DECAY
    )
    ffn_new, ffn_m_new, ffn_v_new = adam_update(
        ffn_w, ffn_grad, ffn_m, ffn_v, MATRIX_RATE, MATRIX_DECAY
    )
    gain_new, gain_m_new, gain_v_new = adam_update(
        gains, gain_grad, gain_m, gain_v, SMALL_RATE, 0.0
    )
    tap_new, tap_m_new, tap_v_new = adam_update(taps, tap_grad, tap_m, tap_v, SMALL_RATE, 0.0)
    return (
        output,
        input_grad,
        mixer_grad,
        mixer_new,
        mixer_m_new,
        mixer_v_new,
        ffn_grad,
        ffn_new,
        ffn_m_new,
        ffn_v_new,
        gain_grad,
        gain_new,
        gain_m_new,
        gain_v_new,
        tap_grad,
        tap_new,
        tap_m_new,
        tap_v_new,
    )


def solution(mesh):
    placed = (
        P(("row", "col"), None),
        P(("row", "col"), None),
        P(),
        P(None, "row", "col"),
        P(None, "row", "col"),
        P(),
        P(None, "col"),
        P(None, "row", "col"),
        P(None, "row", "col"),
        P(None, "row", "col"),
        P(None, "row", "col"),
        P(),
        P(),
        P(None, "col"),
        P(None, "col"),
    )
    return jax.shard_map(
        body,
        mesh=mesh,
        in_specs=placed,
        out_specs=(
            P(("row", "col"), None),
            P(("row", "col"), None),
            P(None, "row", "col"),
            P(None, "row", "col"),
            P(None, "row", "col"),
            P(None, "row", "col"),
            P(None, "row", "col"),
            P(None, "row", "col"),
            P(None, "row", "col"),
            P(None, "row", "col"),
            P(),
            P(),
            P(),
            P(),
            P(None, "col"),
            P(None, "col"),
            P(None, "col"),
            P(None, "col"),
        ),
        check_vma=False,
    )
```

```python
import jax
import jax.numpy as jnp
from jax import lax
from jax.experimental import pallas as pl
from jax.experimental.pallas import tpu as pltpu
from jax.sharding import PartitionSpec as P

STEP = 5


NORM_EPS = 1e-05
BETA_ONE = 0.9
BETA_TWO = 0.95
ADAM_EPS = 1e-08
MATRIX_DECAY = 0.1
MATRIX_RATE = 0.03
SMALL_RATE = 0.3

MESH = pl.DeviceIdType.MESH
BF16 = jnp.bfloat16
F32 = jnp.float32
RING = 4
COT_HOLD = None
ROWS = 8
(
    CA, CIN, COT, COTANGENT, COT_LOW, DOWN, DOWN_GRAD, DOWN_PART, DOWN_PARTS, DWD, DWG, ENTRY, FAR,
    FFN_LOW, FFN_W0, FFN_W1, GAINS, GAIN_TWO, GATE, GFFN, GRAD, GRAD0, GRAD1, GRAD_RESIDUAL, IN, IN_OUT,
    MIX, NEAR, NORMED, NORMED_IN, NORMED_OUT, OUT, OUT0, OUT1, OUT_A, PROJ, PROJ_OUT, RESIDUAL, SMALL,
    START, TAPS, TAPS_SENT, TOKENS, UP, USED, W0, W1, W3, WD, WEIGHTS, W_IN, W_OUT, ALL, DONE, FIRST,
    GO, MOST, OWN, READY, SENT, SIB, SPREAD, SWAP,
) = range(63)

LINK = 42e3
CORES = 280e3
LINK_LAG, CORE_LAG = 3.0, 1.0
SEND_LAG = 5.0
WAIT = 0.05


def place():
    row, col = lax.axis_index("row"), lax.axis_index("col")
    return {"x": col // 4, "y": row // 2, "z": (col // 2) % 2 * 2 + row % 2, "k": col % 2}


def device_at(at):
    return (at["y"] * 2 + at["z"] % 2, at["x"] * 4 + at["z"] // 2 * 2 + at["k"])


def wrap(value, length=RING):
    return lax.rem(value + length, length)


def size_of(ref):
    size = jnp.dtype(ref.dtype).itemsize
    for extent in ref.shape:
        size *= extent
    return size


class Work:
    def __init__(self, send_sems, recv_sems, local_sems):
        self.me = place()
        self.send_sems, self.recv_sems, self.local_sems = send_sems, recv_sems, local_sems
        self.sending, self.local, self.kept, self.count = [], [], [], 0
        self.now, self.free, self.due, self.flags, self.chains = 0.0, {}, {}, set(), []

    def near(self, axis, step):
        at = dict(self.me)
        at[axis] = wrap(at[axis] + step, 2 if axis == "k" else RING)
        return device_at(at)

    def target(self, way):
        axis, step = way
        if axis == "row":
            row, col = lax.axis_index("row"), lax.axis_index("col")
            return (wrap(row + step, ROWS), col + 2 - 4 * ((col // 2) % 2))
        return self.near(axis, step)

    def barrier(self, ways):
        sem = pltpu.get_barrier_semaphore()
        for axis, step in ways:
            pl.semaphore_signal(sem, inc=1, device_id=self.target((axis, -step)), device_id_type=MESH)
        pl.semaphore_wait(sem, len(ways))

    def send(self, source, target, way):
        slot = len(self.sending)
        for number, (before, finish) in enumerate(self.sending):
            if finish + SEND_LAG < self.now:
                before.wait_send()
                slot = number
                break
        copy = pltpu.make_async_remote_copy(
            src_ref=source,
            dst_ref=target,
            send_sem=self.send_sems.at[slot],
            recv_sem=self.recv_sems.at[self.count],
            device_id=self.target(way),
            device_id_type=MESH,
        )
        copy.start()
        self.count += 1
        begin = max(self.now, self.free.get(way, 0.0))
        self.free[way] = begin + size_of(source) / (CORES if way[0] == "k" else LINK)
        self.sending[slot : slot + 1] = [(copy, self.free[way])]
        self.due[id(copy)] = self.free[way] + (CORE_LAG if way[0] == "k" else LINK_LAG)
        self.kept.append(copy)
        return copy

    def copy(self, source, target, rate=1.4e6):
        slot = len(self.local)
        for number, before in enumerate(self.local):
            if before is None:
                slot = number
                break
        copy = pltpu.make_async_copy(source, target, self.local_sems.at[slot])
        copy.start()
        begin = max(self.now, self.free.get(0, 0.0))
        self.free[0] = begin + size_of(source) / rate
        self.due[id(copy)] = self.free[0] + 0.5
        self.local[slot : slot + 1] = [copy]
        self.kept.append(copy)
        return copy

    def add(self, chain, rank=0):
        self.chains.append([next(chain), rank, len(self.chains), chain])

    def set(self, flag):
        self.flags.add(flag)

    def run(self):
        while self.chains:
            best, when = None, None
            for entry in self.chains:
                wish = entry[0]
                if isinstance(wish, (int, tuple)):
                    if wish not in self.flags:
                        continue
                    key = (0 if entry[1] == 0 else 1, entry[1], self.now, entry[2])
                elif isinstance(wish, float):
                    key = (0 if entry[1] == 0 else 1, entry[1], self.now, entry[2])
                else:
                    due = self.due[id(wish)]
                    if due <= self.now:
                        key = (0 if entry[1] == 0 else 1, entry[1], due, entry[2])
                    else:
                        key = (2, due, entry[1], entry[2])
                if best is None or key < when:
                    best, when = entry, key
            assert best is not None, self.flags
            wish = best[0]
            if not isinstance(wish, (int, tuple, float)):
                self.now = max(self.now, self.due[id(wish)]) + WAIT
                if any(wish is copy for copy in self.local):
                    wish.wait()
                    self.local = [None if copy is wish else copy for copy in self.local]
                else:
                    wish.wait_recv()
            try:
                best[0] = next(best[3])
                if isinstance(best[0], float):
                    self.now += best[0]
            except StopIteration:
                self.chains = [entry for entry in self.chains if entry is not best]
        for copy, _ in self.sending:
            copy.wait_send()
        for copy in self.local:
            if copy is not None:
                copy.wait()


def stream(work, items):
    pending = []
    for wait, source, target, done in items:
        if wait is not None:
            while pending:
                yield pending[0][0]
                work.set(pending.pop(0)[1])
            yield wait
        pending.append((work.copy(source, target), done))
        if len(pending) > 1:
            yield pending[0][0]
            work.set(pending.pop(0)[1])
    while pending:
        yield pending[0][0]
        work.set(pending.pop(0)[1])


def pieces(wait, source, target, done):
    count = source.shape[0]
    return [
        (wait if number == 0 else None, source.at[number], target.at[number], done if number == count - 1 else (done, number))
        for number in range(count)
    ]


def gather_x(work, source, out, name, copy=False, hold=None):
    x, k = work.me["x"], work.me["k"]
    rows = source.shape[0]
    half = rows // 2
    low, high = pl.ds(0, half), pl.ds(half, half)
    right, left, other = ("x", 1), ("x", -1), ("k", 1)
    ahead, behind, across = wrap(x + 1), wrap(x - 1), wrap(x + 2)
    sib, own = [], []

    def relay(at, part):
        sib.append(work.send(out.at[at, k, part], out.at[at, k, part], other))
        work.set((name, SIB, len(sib)))

    def siblings():
        for number in range(1, 8):
            yield (name, SIB, number)
            yield sib[number - 1]
            if number == 1 and copy:
                yield own[0]
            if number in (1, 5, 7):
                work.set((name, {1: OWN, 5: NEAR, 7: ALL}[number]))

    work.add(siblings())
    yield (name, GO)
    r0 = work.send(source.at[low], out.at[x, k, low], right)
    l1 = work.send(source.at[high], out.at[x, k, high], left)
    r1 = work.send(source.at[high], out.at[x, k, high], right)
    l0 = work.send(source.at[low], out.at[x, k, low], left)
    sib.append(work.send(source, out.at[x, k], other))
    if copy:
        own.append(work.copy(source, out.at[x, k]))
    work.set((name, SIB, 1))
    work.set((name, SENT))
    if hold is not None:
        yield hold
    yield r0
    far0 = work.send(out.at[behind, k, low], out.at[behind, k, low], right)
    relay(behind, low)
    yield l1
    far1 = work.send(out.at[ahead, k, high], out.at[ahead, k, high], left)
    relay(ahead, high)
    work.set((name, FAR))
    yield r1
    relay(behind, high)
    yield l0
    relay(ahead, low)
    yield far0
    relay(across, low)
    yield far1
    relay(across, high)


def add_into(target, first, second):
    rows, lanes = target.shape[-2:]
    if rows * lanes <= 1 << 15:
        target[...] = first[...] + second[...]
        return
    strip = 32

    def body(step, _):
        at = pl.ds(pl.multiple_of(step * strip, strip), strip)
        target[at] = first[at] + second[at]
        return 0

    lax.fori_loop(0, rows // strip, body, 0)


def ring_places(x):
    return (wrap(x + 2), wrap(x + 1), wrap(x - 1), x)


def scatter_x(work, parts, box, hop, land, name):
    x, k = work.me["x"], work.me["k"]
    rows = box.shape[1]
    half = rows // 2
    low, high = pl.ds(0, half), pl.ds(half, half)
    right, left, other = ("x", 1), ("x", -1), ("k", 1)
    across, ahead, behind, own = ring_places(x)

    def swap():
        sib = {}
        for number, at in enumerate((across, ahead, behind, own)):
            yield (name, READY, number)
            sib[number] = work.send(parts.at[at, 1 - k], box.at[at], other)
            got.append(sib[number])
            work.set((name, SWAP, number))

    got = []
    work.add(swap(), 0)
    yield (name, SWAP, 0)
    yield got[0]
    add_into(box.at[across], parts.at[across, k], box.at[across])
    far0 = work.send(box.at[across, low], hop.at[0], right)
    far1 = work.send(box.at[across, high], hop.at[1], left)
    yield 0.3
    yield (name, SWAP, 1)
    yield got[1]
    add_into(box.at[ahead], parts.at[ahead, k], box.at[ahead])
    r1 = work.send(box.at[ahead, high], land.at[0, high], right)
    yield 0.3
    yield (name, SWAP, 2)
    yield got[2]
    add_into(box.at[behind], parts.at[behind, k], box.at[behind])
    l0 = work.send(box.at[behind, low], land.at[1, low], left)
    yield 0.3
    yield far0
    add_into(box.at[ahead, low], box.at[ahead, low], hop.at[0])
    r0 = work.send(box.at[ahead, low], land.at[0, low], right)
    yield 0.15
    yield far1
    add_into(box.at[behind, high], box.at[behind, high], hop.at[1])
    l1 = work.send(box.at[behind, high], land.at[1, high], left)
    work.set((name, SENT))
    yield 0.15
    yield (name, SWAP, 3)
    yield got[3]
    for copy in (r1, l0, r0, l1):
        yield copy
    work.set((name, DONE))


def block(ref, y, z, half, rows):
    column = pl.multiple_of((y * 2 + z % 2) * 256 + half * 128, 128)
    return ref.at[:, z // 2, rows, pl.ds(column, 128)]


def gather_yz(work, source, out, half, name):
    first, second = ("y", "z") if half == 0 else ("z", "y")
    rows = source.shape[1]
    cut = rows // 2
    low, high, whole = pl.ds(0, cut), pl.ds(cut, cut), pl.ds(0, rows)
    a, b = work.me[first], work.me[second]

    def slot(at_a, at_b, part):
        y, z = (at_a, at_b) if half == 0 else (at_b, at_a)
        return block(out, y, z, half, part)

    columns = pl.ds(half * 128, 128)
    up, down, forward, backward = (first, 1), (first, -1), (second, 1), (second, -1)
    a_behind, a_ahead, a_across = wrap(a - 1), wrap(a + 1), wrap(a + 2)
    b_behind, b_ahead = wrap(b - 1), wrap(b + 1)
    yield (name, GO, half)
    mine = work.copy(source.at[:, :, columns], slot(a, b, whole))
    r0 = work.send(source.at[:, low, columns], slot(a, b, low), up)
    l1 = work.send(source.at[:, high, columns], slot(a, b, high), down)
    r1 = work.send(source.at[:, high, columns], slot(a, b, high), up)
    l0 = work.send(source.at[:, low, columns], slot(a, b, low), down)
    waits, last = [], []

    def spread(at, part, ref=None):
        ref = slot(at, b, part) if ref is None else ref
        waits.append(
            (
                at,
                part,
                work.send(ref, slot(at, b, part), forward),
                work.send(ref, slot(at, b, part), backward),
            )
        )

    def onward(number):
        at, part, plus, minus = waits[number]
        yield plus
        if part is low:
            last.append(work.send(slot(at, b_behind, part), slot(at, b_behind, part), forward))
        yield minus
        if part is high:
            last.append(work.send(slot(at, b_ahead, part), slot(at, b_ahead, part), backward))

    spread(a, low, source.at[:, low, columns])
    spread(a, high, source.at[:, high, columns])
    yield r0
    f0 = work.send(slot(a_behind, b, low), slot(a_behind, b, low), up)
    spread(a_behind, low)
    yield l1
    f1 = work.send(slot(a_ahead, b, high), slot(a_ahead, b, high), down)
    spread(a_ahead, high)
    yield from onward(0)
    yield r1
    spread(a_behind, high)
    yield l0
    spread(a_ahead, low)
    yield from onward(1)
    yield f0
    spread(a_across, low)
    yield f1
    spread(a_across, high)
    work.set((name, SPREAD, half))
    for number in range(2, 8):
        yield from onward(number)
        if number == 5:
            work.set((name, MOST, half))
    work.set((name, SENT, half))
    for copy in last:
        yield copy
    yield mine
    work.set((name, ALL, half))


def scatter_yz(work, parts, box, out, half, name, where=None):
    first, second = ("z", "y") if half == 0 else ("y", "z")
    rows = parts.shape[2]
    cut = rows // 2
    low, high, whole = pl.ds(0, cut), pl.ds(cut, cut), pl.ds(0, rows)
    a, b = work.me[first], work.me[second]

    def slot(at_a, at_b, part):
        y, z = (at_b, at_a) if half == 0 else (at_a, at_b)
        return block(parts, y, z, half, part)

    across, ahead, behind, own = ring_places(a)
    up, down = (first, 1), (first, -1)

    def first_ring(number, at_b):
        base = 3 * number
        pick = lambda at, part: slot(at, at_b, part)
        yield (name, GO, half)
        far0 = work.send(pick(across, low), box.at[base, :, low], up)
        far1 = work.send(pick(across, high), box.at[base, :, high], down)
        r1 = work.send(pick(ahead, high), box.at[base + 1, :, high], up)
        l0 = work.send(pick(behind, low), box.at[base + 2, :, low], down)
        yield far0
        add_into(pick(ahead, low), pick(ahead, low), box.at[base, :, low])
        r0 = work.send(pick(ahead, low), box.at[base + 1, :, low], up)
        yield far1
        add_into(pick(behind, high), pick(behind, high), box.at[base, :, high])
        l1 = work.send(pick(behind, high), box.at[base + 2, :, high], down)
        yield r1
        add_into(pick(own, high), pick(own, high), box.at[base + 1, :, high])
        yield l0
        add_into(pick(own, low), pick(own, low), box.at[base + 2, :, low])
        yield r0
        add_into(pick(own, low), pick(own, low), box.at[base + 1, :, low])
        yield l1
        add_into(pick(own, high), pick(own, high), box.at[base + 2, :, high])
        work.set((name, FIRST, half, number))

    places = ring_places(b)
    for number, at_b in enumerate(places):
        work.add(first_ring(number, at_b))
    b_across, b_ahead, b_behind, b_own = places
    forward, backward = (second, 1), (second, -1)
    yield (name, FIRST, half, 0)
    far0 = work.send(slot(a, b_across, low), box.at[12, :, low], forward)
    far1 = work.send(slot(a, b_across, high), box.at[12, :, high], backward)
    yield (name, FIRST, half, 1)
    r1 = work.send(slot(a, b_ahead, high), box.at[13, :, high], forward)
    yield far0
    add_into(slot(a, b_ahead, low), slot(a, b_ahead, low), box.at[12, :, low])
    r0 = work.send(slot(a, b_ahead, low), box.at[13, :, low], forward)
    yield (name, FIRST, half, 2)
    l0 = work.send(slot(a, b_behind, low), box.at[14, :, low], backward)
    yield far1
    add_into(slot(a, b_behind, high), slot(a, b_behind, high), box.at[12, :, high])
    l1 = work.send(slot(a, b_behind, high), box.at[14, :, high], backward)
    yield (name, FIRST, half, 3)
    mine = slot(a, b_own, whole)
    for copy in (r1, r0, l0, l1):
        yield copy
    for m in range(parts.shape[0]):
        total = mine[m].astype(F32) + box[13, m].astype(F32) + box[14, m].astype(F32)
        if where is not None:
            out[where[m], half * 128 : (half + 1) * 128, :] = total.T
        else:
            out[m, :, half * 128 : (half + 1) * 128] = total
    work.set((name, DONE, half))


def sum_all(work, values, box, out, name):
    yield (name, GO)
    out[...] = values[...]
    me = work.me
    for turn, axis in enumerate(("k", "z", "y", "x")):
        length = 2 if axis == "k" else RING
        mine = box.at[turn, me[axis]]
        mine[...] = out[...]
        copies = [work.send(mine, mine, (axis, step)) for step in range(1, length)]
        for copy in copies:
            yield copy
        total = box[turn, 0]
        for number in range(1, length):
            total = total + box[turn, number]
        out[...] = total
    work.set((name, DONE))


ANY = pl.BlockSpec(memory_space=pl.ANY)
VMEM = pl.BlockSpec(memory_space=pltpu.VMEM)
SMEM = pl.BlockSpec(memory_space=pltpu.SMEM)
X_WAYS = (("x", 1), ("x", -1), ("k", 1))
YZ_WAYS = (("y", 1), ("y", -1), ("z", 1), ("z", -1))


def bf(*shape):
    return jax.ShapeDtypeStruct(shape, BF16)


def fl(*shape):
    return jax.ShapeDtypeStruct(shape, F32)


def call(name, number, body, args, outs, scratch, copies, ways, flops, room):
    def kernel(*refs):
        main, sems = refs[:-3], refs[-3:]
        work = Work(*sems)
        body(work, *main)
        work.barrier(ways)
        work.run()
        used = (len(work.sending), work.count, len(work.local))
        assert all(one <= most for one, most in zip(used, copies)), used

    sems = [pltpu.SemaphoreType.DMA((count,)) for count in copies]
    return pl.pallas_call(
        kernel,
        out_shape=[shape for shape, _ in outs],
        in_specs=[spec for _, spec in args],
        out_specs=[spec for _, spec in outs],
        scratch_shapes=list(scratch) + sems,
        compiler_params=pltpu.CompilerParams(
            collective_id=number, has_side_effects=True, vmem_limit_bytes=room << 20
        ),
        cost_estimate=pl.CostEstimate(flops=flops, bytes_accessed=40 << 20, transcendentals=0),
        name=name,
    )(*[array for array, _ in args])


def dot_nt(left, right):
    return lax.dot_general(left, right, (((1,), (1,)), ((), ())), preferred_element_type=F32)


def dot_tn(left, right):
    return lax.dot_general(left, right, (((0,), (0,)), ((), ())), preferred_element_type=F32)


def dot_nn(left, right):
    return lax.dot_general(left, right, (((1,), (0,)), ((), ())), preferred_element_type=F32)


def strips(rows, strip, body):
    def one(step, _):
        body(pl.ds(pl.multiple_of(step * strip, strip), strip))
        return 0

    lax.fori_loop(0, rows // strip, one, 0)


def keeps(starts, first, shape):
    places = first + lax.broadcasted_iota(jnp.int32, shape, 0)

    def keep(at):
        hit = at == starts[0]
        for number in range(1, 4):
            hit = jnp.logical_or(hit, at == starts[number])
        return jnp.where(hit, 0.0, 1.0).astype(F32)

    here = keep(places)
    return here, here * keep(places - 1)


def run_start(run, run_tokens):
    row, col = lax.axis_index("row"), lax.axis_index("col")
    return ((row * RING + run) * 2 + (col // 2) % 2) * run_tokens


SHARD, WIDTH = 128, 2048
RUN = 2 * SHARD
CH, HALF = 256, 128
HID = 352


def lags(ext, starts, run, at, lane):
    rows = 64
    lanes = slice(lane * HALF, (lane + 1) * HALF)
    one, two = keeps(starts, run_start(run, RUN) + at, (rows, HALF))
    mixed = ext[run, 8 + at : 8 + at + rows, lanes]
    return mixed, one * ext[run, 7 + at : 7 + at + rows, lanes], two * ext[run, 6 + at : 6 + at + rows, lanes]


def place_halo(ext, near, far):
    row, col = lax.axis_index("row"), lax.axis_index("col")
    late = (col // 2) % 2 == 1
    first = jnp.where(row > 0, far[...], 0.0)
    for run in range(RING):
        ext[run, 0:8] = jnp.where(late, near[run], first if run == 0 else near[run - 1])


def forward_mixer(tokens, cotangent, starts, mixer, ffn, gains, taps):
    def body(
        work, tokens_in, cotangent_in, starts, mixer_in, ffn_in, gains_in, taps_in,
        normed_out, cot_out, in_out, mix_out, ffn_out, proj_out, near_final, far_final, taps_final, residual_out, low_out,
        gains, taps, near_out, far_out, taps_out, tokens, cotangent, mixer_wide, ffn_wide, mixer, ffn, tap_rows,
        normed, weights, proj, ext, gated, parts, box, hop, land, cot, residual, low_rows,
    ):
        x, k = work.me["x"], work.me["k"]
        z_hi = (lax.axis_index("col") // 2) % 2
        w_in, w_out = weights.at[0:3], weights.at[3:4]
        sent = {}

        def opening():
            loads = [work.copy(gains_in, gains), work.copy(tokens_in, tokens)]
            loads += [work.copy(mixer_in, mixer_wide), work.copy(taps_in, taps)]
            yield loads[0]
            yield loads[1]

            def norm(at):
                rows = tokens[at]
                scale = lax.rsqrt(jnp.mean(rows * rows, axis=1, keepdims=True) + NORM_EPS)
                normed[x, k, at] = (rows * scale * gains[0:1]).astype(BF16)

            strips(SHARD, 16, norm)
            work.set((NORMED, GO))
            yield 1.0
            yield loads[2]
            loads.append(work.copy(ffn_in.at[0:2], ffn_wide))
            for number in range(4):
                mixer[number] = mixer_wide[number].T.astype(BF16)
            work.set((IN, GO, 0))
            work.set((IN, GO, 1))
            yield 0.6
            loads.append(work.copy(cotangent_in, cotangent))
            yield loads[3]
            tap_rows[...] = jnp.zeros_like(tap_rows)
            tap_rows[0:3] = taps[...]
            taps_out[z_hi] = tap_rows[...]
            sent[TAPS] = work.send(tap_rows, taps_out.at[z_hi], ("z", 2))
            work.set(TAPS_SENT)
            yield loads[4]
            for number in range(2):
                for at in range(0, HID, 88):
                    ffn[number, at : at + 88] = ffn_wide[number, at : at + 88].astype(BF16)
            work.set(FFN_LOW)
            yield 0.5
            yield loads[5]

            def cast(at):
                cot[at] = cotangent[at].astype(BF16)

            strips(SHARD, 16, cast)
            work.set(COT_LOW)
            yield 0.5

        def compute():
            yield TAPS_SENT
            yield sent[TAPS]
            yield (NORMED, ALL)
            yield (IN, ALL, 0)
            yield (IN, ALL, 1)
            tail = normed[:, 1, SHARD - 16 :].reshape(RING * 16, WIDTH)
            ends = dot_nt(tail, weights[0:3].reshape(3 * CH, WIDTH))
            mixed = (ends[:, :CH] * ends[:, 2 * CH :]).reshape(RING, 16, CH)
            ext[:, RUN - 8 : RUN + 8] = mixed
            halo = [
                work.send(ext.at[:, RUN : RUN + 8], near_out, ("z", 2)),
                work.send(ext.at[RING - 1, RUN : RUN + 8], far_out, ("row", 1)),
            ]
            yield 1.0

            for half in range(2):
                rows = normed[2 * half : 2 * half + 2].reshape(2 * RUN, WIDTH)
                out = dot_nt(rows, weights[0:3].reshape(3 * CH, WIDTH))
                proj[2 * half : 2 * half + 2] = out.reshape(2, RUN, 3 * CH)
                yield 2.0
            work.set(PROJ)

            def mix(run, _):
                for at in range(0, RUN, 64):
                    size = 64 if at + 64 < RUN else 56
                    rows = proj[run, at : at + size]
                    ext[run, 8 + at : 8 + at + size] = rows[:, :CH] * rows[:, 2 * CH :]
                return 0

            lax.fori_loop(0, RING, mix, 0)
            yield 0.7
            for copy in halo:
                yield copy
            place_halo(ext, near_out, far_out)
            for source, target in ((near_out, near_final), (far_out, far_final), (taps_out, taps_final)):
                work.copy(source, target)

            def convolve(run, _):
                for at in range(0, RUN, 64):
                    for lane in range(2):
                        mixed, one, two = lags(ext, starts, run, at, lane)
                        tap = taps_out[lane]
                        total = tap[2:3] * mixed + tap[1:2] * one + tap[0:1] * two
                        gate = proj[run, at : at + 64, CH + lane * HALF : CH + (lane + 1) * HALF]
                        gated[run, at : at + 64, lane * HALF : (lane + 1) * HALF] = (gate * total).astype(BF16)
                return 0

            lax.fori_loop(0, RING, convolve, 0)
            yield 1.5
            yield (MIX, ALL, 0)
            yield (MIX, ALL, 1)
            work.set(WEIGHTS)
            for number, at in enumerate(ring_places(x)):
                out = dot_nn(gated[at], weights[3].reshape(CH, WIDTH))
                parts[at] = out.astype(BF16).reshape(2, SHARD, WIDTH)
                work.set((OUT, READY, number))
                yield 0.6
            yield (OUT, DONE)

            def close(at):
                total = parts[x, k, at].astype(F32) + box[x, at].astype(F32)
                total = total + (land[0, at].astype(F32) + land[1, at].astype(F32))
                rows = tokens[at] + total
                scale = lax.rsqrt(jnp.mean(rows * rows, axis=1, keepdims=True) + NORM_EPS)
                residual[at] = rows
                low_rows[at] = (rows * scale * gains[1:2]).astype(BF16)

            strips(SHARD, 16, close)
            work.copy(low_rows, low_out)
            work.copy(residual, residual_out)
            yield 1.0

        def order():
            yield (NORMED, FAR)
            yield COT_LOW
            work.set((COT, GO))

        def follow(half):
            yield FFN_LOW
            yield (IN, MOST, half)
            work.set((MIX, GO, half))
            yield (MIX, MOST, half)
            work.set((GATE, GO, half))
            yield (GATE, MOST, half)
            work.set((UP, GO, half))

        work.add(opening(), 1)
        work.add(gather_x(work, normed.at[x, k], normed, NORMED))
        for half in (0, 1):
            work.add(gather_yz(work, mixer.at[0:3], w_in, half, IN))
        for half in (0, 1):
            work.add(gather_yz(work, mixer.at[3:4], w_out, half, MIX))
        for number, name in enumerate((GATE, UP)):
            for half in (0, 1):
                mat = pl.ds(number, 1)
                work.add(gather_yz(work, ffn.at[mat], ffn_out.at[mat], half, name))
        work.add(scatter_x(work, parts, box, hop, land, OUT))
        work.add(gather_x(work, cot, cot_out, COT, copy=True, hold=COT_HOLD), 0)
        outs = pieces((NORMED, ALL), normed, normed_out, NORMED_OUT)
        outs += pieces(PROJ, proj, proj_out, PROJ_OUT)
        outs += pieces(WEIGHTS, weights.at[0:3], in_out, IN_OUT) + pieces(WEIGHTS, weights.at[3:4], mix_out, W3)
        work.add(stream(work, outs), 3)
        work.add(order())
        work.add(follow(0))
        work.add(follow(1))
        work.add(compute(), 1)

    gathered = bf(RING, 2, SHARD, WIDTH)
    return call(
        "forward_mixer",
        0,
        body,
        [(tokens, ANY), (cotangent, ANY), (starts, SMEM), (mixer, ANY), (ffn, ANY), (gains, ANY), (taps, ANY)],
        [
            (gathered, ANY), (gathered, ANY), (bf(3, 2, HALF, WIDTH), ANY), (bf(1, 2, HALF, WIDTH), ANY),
            (bf(2, 2, HID, WIDTH), ANY), (fl(RING, RUN, 3 * CH), ANY), (fl(RING, 8, CH), ANY), (fl(8, CH), ANY),
            (fl(2, 8, HALF), ANY), (fl(SHARD, WIDTH), ANY), (bf(SHARD, WIDTH), ANY),
        ],
        [
            pltpu.VMEM((2, WIDTH), F32),
            pltpu.VMEM((3, HALF), F32),
            pltpu.VMEM((RING, 8, CH), F32),
            pltpu.VMEM((8, CH), F32),
            pltpu.VMEM((2, 8, HALF), F32),
            pltpu.VMEM((SHARD, WIDTH), F32),
            pltpu.VMEM((SHARD, WIDTH), F32),
            pltpu.VMEM((4, CH, HALF), F32),
            pltpu.VMEM((2, HID, CH), F32),
            pltpu.VMEM((4, HALF, CH), BF16),
            pltpu.VMEM((2, HID, CH), BF16),
            pltpu.VMEM((8, HALF), F32),
            pltpu.VMEM((RING, 2, SHARD, WIDTH), BF16),
            pltpu.VMEM((4, 2, HALF, WIDTH), BF16),
            pltpu.VMEM((RING, RUN, 3 * CH), F32),
            pltpu.VMEM((RING, RUN + 8, CH), F32),
            pltpu.VMEM((RING, RUN, CH), BF16),
            pltpu.VMEM((RING, 2, SHARD, WIDTH), BF16),
            pltpu.VMEM((RING, SHARD, WIDTH), BF16),
            pltpu.VMEM((2, SHARD // 2, WIDTH), BF16),
            pltpu.VMEM((2, SHARD, WIDTH), BF16),
            pltpu.VMEM((SHARD, WIDTH), BF16),
            pltpu.VMEM((SHARD, WIDTH), F32),
            pltpu.VMEM((SHARD, WIDTH), BF16),
        ],
        (90, 300, 20),
        X_WAYS + YZ_WAYS + (("z", 2), ("row", 1)),
        int(5e9),
        63,
    )


def feed_forward(rows, cot, ffn, ffn_wide, residual, cotangent, gains):
    def body(
        work, rows_in, cot, ffn, ffn_wide, residual_in, cotangent_in, gains_in,
        grad_out, low_out, down_out, down_grad_out, part_out, gain_out,
        gains, gain_part, fa, ca, w, down_part, down_wide, down_low, residual, cotangent, down_grad,
        gate, up, hid, gg, gu, gh, grad_low,
        parts_a, parts_b, box_b, hop_b, land_b, boxes,
    ):
        x, k = work.me["x"], work.me["k"]
        units = 2 * HID

        def mat(number):
            return w[number].reshape(units, WIDTH)

        def weight_grad(out, left, right):
            for step in range(WIDTH // 512):
                at = pl.ds(step * 512, 512)
                rows = right[:, :, :, at].reshape(RING * RUN, 512)
                grad = dot_tn(left[...].reshape(RING * RUN, units), rows)
                out[:, :, at] = grad.astype(BF16).reshape(2, HID, 512)
                yield 1.0

        def opening():
            yield START
            work.set((ENTRY, GO))
            yield work.copy(ffn_wide.at[2], down_wide)
            for at in range(0, HID, 88):
                down_low[0, at : at + 88] = down_wide[at : at + 88].astype(BF16)
            work.set((WD, GO, 0))
            work.set((WD, GO, 1))
            yield 0.2

        work.set(START)
        ins = pieces((WD, GO, 1), ffn.at[0], w.at[0], W0) + pieces(None, ffn.at[1], w.at[1], W1)
        ins += pieces(None, cot, ca, CA)
        ins += [(None, residual_in, residual, RESIDUAL), (None, cotangent_in, cotangent, COTANGENT), (None, gains_in, gains, GAINS)]
        outs = pieces(DOWN_PART, parts_a, down_out, OUT_A) + pieces(GRAD0, w.at[0], part_out.at[0], OUT0)
        outs += pieces(GRAD1, w.at[1], part_out.at[1], OUT1)

        def compute():
            across, ahead, behind, own = ring_places(x)

            def forward(at):
                rows = fa[at].reshape(RUN, WIDTH)
                gate[at] = dot_nt(rows, mat(0))
                up[at] = dot_nt(rows, mat(1))

                def activate(here):
                    value = gate[at, here]
                    hid[at, here] = (value * jax.nn.sigmoid(value) * up[at, here]).astype(BF16)

                strips(RUN, 16, activate)

            yield (ENTRY, OWN)
            yield W0
            yield W1
            forward(own)
            yield 2.9
            yield (ENTRY, NEAR)
            forward(behind)
            yield 2.9
            forward(ahead)
            yield 2.9
            yield (ENTRY, ALL)
            forward(across)
            yield 2.9
            yield CA
            yield from weight_grad(down_part.at[0], hid, ca)
            for half in (0, 1):
                work.set((DWD, GO, half))
            yield (WD, ALL, 0)
            yield (WD, ALL, 1)
            for pair in (0, 1):
                gh[...] = dot_nt(ca[pl.ds(2 * pair, 2)].reshape(2 * RUN, WIDTH), mat(2)).reshape(2, RUN, units)
                yield 2.0

                def one(at):
                    for here in (0, 1):
                        run = 2 * pair + here
                        value, grad = gate[run, at], gh[here, at]
                        sig = jax.nn.sigmoid(value)
                        gg[run, at] = (grad * up[run, at] * sig * (1.0 + value * (1.0 - sig))).astype(BF16)
                        gu[run, at] = (grad * (value * sig)).astype(BF16)

                strips(RUN, 16, one)
                yield 1.5
            for number, at in enumerate(ring_places(x)):
                grad = dot_nn(gg[at], mat(0)) + dot_nn(gu[at], mat(1))
                parts_b[at] = grad.astype(BF16).reshape(2, SHARD, WIDTH)
                work.set((GFFN, READY, number))
                yield 2.2
            for at in range(RING):
                parts_a[at] = dot_nn(hid[at], mat(2)).astype(BF16).reshape(2, SHARD, WIDTH)
                yield 1.1
            work.set(DOWN_PART)
            yield from weight_grad(w.at[0], gg, fa)
            work.set(GRAD0)
            yield from weight_grad(w.at[1], gu, fa)
            work.set(GRAD1)
            yield (DWD, DONE, 0)
            yield (DWD, DONE, 1)
            work.copy(down_grad, down_grad_out)

        def close_grad():
            yield (GFFN, DONE)
            yield RESIDUAL
            yield GAINS
            gain_part[...] = jnp.zeros_like(gain_part)

            def one(at):
                grad = parts_b[x, k, at].astype(F32) + box_b[x, at].astype(F32)
                grad = grad + (land_b[0, at].astype(F32) + land_b[1, at].astype(F32))
                rows = residual[at]
                scale = lax.rsqrt(jnp.mean(rows * rows, axis=1, keepdims=True) + NORM_EPS)
                normal = rows * scale
                gain = grad * normal
                gain_part[...] += gain[:8] + gain[8:]
                scaled = grad * gains[1:2]
                back = scale * (scaled - normal * jnp.mean(scaled * normal, axis=1, keepdims=True))
                total = cotangent[at] + back
                cotangent[at] = total
                grad_low[at] = total.astype(BF16)

            strips(SHARD, 16, one)
            work.copy(grad_low, low_out)
            work.copy(cotangent, grad_out)
            work.copy(gain_part, gain_out)
            yield 1.5

        work.add(opening(), 0)
        work.add(stream(work, ins), 1)
        work.add(stream(work, outs), 1)
        work.add(gather_x(work, rows_in, fa, ENTRY, copy=True))
        for half in (0, 1):
            work.add(gather_yz(work, down_low, w.at[2:3], half, WD))
        work.add(scatter_x(work, parts_b, box_b, hop_b, land_b, GFFN))
        for half in (0, 1):
            work.add(scatter_yz(work, down_part, boxes.at[half], down_grad, half, DWD))
        work.add(compute(), 2)
        work.add(close_grad(), 1)

    units = 2 * HID
    group = [
        pltpu.VMEM((RING, 2, SHARD, WIDTH), BF16),
        pltpu.VMEM((RING, SHARD, WIDTH), BF16),
        pltpu.VMEM((2, SHARD // 2, WIDTH), BF16),
        pltpu.VMEM((2, SHARD, WIDTH), BF16),
    ]
    return call(
        "feed_forward",
        1,
        body,
        [
            (rows, ANY), (cot, ANY), (ffn, ANY), (ffn_wide, ANY), (residual, ANY), (cotangent, ANY), (gains, ANY),
        ],
        [
            (fl(SHARD, WIDTH), ANY), (bf(SHARD, WIDTH), ANY), (bf(RING, 2, SHARD, WIDTH), ANY), (fl(1, HID, CH), ANY),
            (bf(2, 2, HID, WIDTH), ANY), (fl(8, WIDTH), ANY),
        ],
        [
            pltpu.VMEM((2, WIDTH), F32),
            pltpu.VMEM((8, WIDTH), F32),
            pltpu.VMEM((RING, 2, SHARD, WIDTH), BF16),
            pltpu.VMEM((RING, 2, SHARD, WIDTH), BF16),
            pltpu.VMEM((3, 2, HID, WIDTH), BF16),
            pltpu.VMEM((1, 2, HID, WIDTH), BF16),
            pltpu.VMEM((HID, CH), F32),
            pltpu.VMEM((1, HID, CH), BF16),
            pltpu.VMEM((SHARD, WIDTH), F32),
            pltpu.VMEM((SHARD, WIDTH), F32),
            pltpu.VMEM((1, HID, CH), F32),
            pltpu.VMEM((RING, RUN, units), F32),
            pltpu.VMEM((RING, RUN, units), F32),
            pltpu.VMEM((RING, RUN, units), BF16),
            pltpu.VMEM((RING, RUN, units), BF16),
            pltpu.VMEM((RING, RUN, units), BF16),
            pltpu.VMEM((2, RUN, units), F32),
            pltpu.VMEM((SHARD, WIDTH), BF16),
            group[0],
            *group,
            pltpu.VMEM((2, 15, 1, HID, HALF), BF16),
        ],
        (90, 300, 20),
        X_WAYS + YZ_WAYS,
        int(27e9),
        63,
    )


def backward_mixer(
    grad_low, ffn_part, down_part, down_grad, normed, w_in, w_out, proj, near, far, taps, starts, tokens, residual,
    grad_residual, gains, gain_two,
):
    def body(
        work, low_in, ffn_part, down_in, down_grad, normed, w_in, w_out, proj_in, near_in, far_in, taps_in, starts,
        tokens_in, residual_in, grad_in, gains_in, gain_two_in,
        output_out, input_grad_out, mixer_grad_out, ffn_grad_out, small_final,
        near, far, taps, gains, gain_two, mixer_grad, small_out, down_parts, down_box, down_hop, down_land, residual,
        ffn_w, ffn_grad, ffn_boxes, tokens, grad_residual,
        ga, na, w, proj, ext, ahead, conv, gated, gp, near_next, far_next, tap_sum, gain_sum, small,
        new, parts, box, hop, land, box_cin, box_in, box_small,
    ):
        x, k = work.me["x"], work.me["k"]
        row, col = lax.axis_index("row"), lax.axis_index("col")
        late = (col // 2) % 2 == 1

        def mat_in():
            return w[0:3].reshape(3 * CH, WIDTH)

        ins = pieces(None, ffn_part.at[0], ffn_w.at[0], FFN_W0) + pieces(None, ffn_part.at[1], ffn_w.at[1], FFN_W1)
        ins += [(None, near_in, near, NEAR), (None, far_in, far, FAR), (None, taps_in, taps, TAPS)]
        ins += pieces(None, proj_in, proj, PROJ) + [(None, w_out, w.at[3:4], W_OUT)]
        ins += pieces(None, normed, na, NORMED_IN) + pieces(None, w_in, w.at[0:3], W_IN)
        ins += pieces(None, down_in, down_parts, DOWN_PARTS) + [
            (None, residual_in, residual, RESIDUAL),
            (None, down_grad, ffn_grad.at[2:3], DOWN_GRAD),
            (None, gains_in, gains, GAINS),
            (None, gain_two_in, gain_two, GAIN_TWO),
            (None, tokens_in, tokens, TOKENS),
            (None, grad_in, grad_residual, GRAD_RESIDUAL),
        ]
        work.set(START)

        def opening():
            yield START
            work.set((GRAD, GO))
            yield FFN_W1
            for half in (0, 1):
                work.set((DWG, GO, half))

        def in_grads(numbers):
            for step in range(WIDTH // 512):
                at = pl.ds(step * 512, 512)
                rows = na[:, :, :, at].reshape(RING * RUN, 512)
                for number in numbers:
                    left = gp[:, :, number * CH : (number + 1) * CH].reshape(RING * RUN, CH)
                    grad = dot_tn(left, rows)
                    old = w[number, :, :, at].reshape(CH, 512).astype(F32)
                    gain_sum[:, at] += jnp.sum((grad * old).reshape(CH // 8, 8, 512), axis=0)
                    new[(2, 0, 3)[number], :, :, at] = grad.astype(BF16).reshape(2, HALF, 512)
                yield 0.4 * len(numbers)

        def compute():
            yield PROJ

            def mix(run, _):
                for at in range(0, RUN, 64):
                    rows = proj[run, at : at + 64]
                    ext[run, 8 + at : 8 + at + 64] = rows[:, :CH] * rows[:, 2 * CH :]
                return 0

            lax.fori_loop(0, RING, mix, 0)
            place_halo(ext, near, far)

            def convolve(run, _):
                for at in range(0, RUN, 64):
                    for lane in range(2):
                        lanes = slice(lane * HALF, (lane + 1) * HALF)
                        mixed, one, two = lags(ext, starts, run, at, lane)
                        tap = taps[lane]
                        total = tap[2:3] * mixed + tap[1:2] * one + tap[0:1] * two
                        gate = proj[run, at : at + 64, CH + lane * HALF : CH + (lane + 1) * HALF]
                        conv[run, at : at + 64, lanes] = total
                        gated[run, at : at + 64, lanes] = (gate * total).astype(BF16)
                return 0

            lax.fori_loop(0, RING, convolve, 0)
            yield 2.2
            yield W_OUT

            def gate_back(at):
                grad = dot_nt(ga[at].reshape(RUN, WIDTH), w[3].reshape(CH, WIDTH))
                ahead[at, 0:RUN] = grad * proj[at, :, CH : 2 * CH]
                gp[at, :, CH : 2 * CH] = (grad * conv[at]).astype(BF16)

            across, ahead_at, behind, own = ring_places(x)
            yield (GRAD, OWN)
            gate_back(own)
            yield 0.7
            yield (GRAD, NEAR)
            gate_back(behind)
            gate_back(ahead_at)
            yield 1.4
            yield (GRAD, ALL)
            gate_back(across)
            sent = [
                work.send(ahead.at[:, 0:8], near_next, ("z", 2)),
                work.send(ahead.at[0, 0:8], far_next, ("row", -1)),
            ]
            yield 0.7

            def out_grad(step, _):
                at = pl.ds(pl.multiple_of(step * 512, 512), 512)
                rows = ga[:, :, :, at].reshape(RING * RUN, 512)
                grad = dot_tn(gated[...].reshape(RING * RUN, CH), rows)
                new[1, :, :, at] = grad.astype(BF16).reshape(2, HALF, 512)
                return 0

            lax.fori_loop(0, WIDTH // 512, out_grad, 0)
            yield 1.7
            yield NORMED_IN
            yield W_IN
            gain_sum[...] = jnp.zeros_like(gain_sum)
            yield from in_grads((1,))
            for half in (0, 1):
                work.set((CIN, GO, half))
            for copy in sent:
                yield copy
            last = jnp.where(row < ROWS - 1, far_next[...], 0.0)
            for run in range(RING):
                after = last if run == RING - 1 else near_next[run + 1]
                ahead[run, RUN : RUN + 8] = jnp.where(late, after, near_next[run])
            tap_sum[...] = jnp.zeros_like(tap_sum)

            def unmix(run, _):
                for at in range(0, RUN, 64):
                    for lane in range(2):
                        lanes = slice(lane * HALF, (lane + 1) * HALF)
                        rows = slice(at, at + 64)
                        first = run_start(run, RUN) + at
                        one, _two = keeps(starts, first + 1, (64, HALF))
                        _one, two = keeps(starts, first + 2, (64, HALF))
                        tap = taps[lane]
                        grad = ahead[run, rows, lanes]
                        mixed, lag_one, lag_two = lags(ext, starts, run, at, lane)
                        for number, value in enumerate((lag_two, lag_one, mixed)):
                            tap_sum[number, :, lanes] += jnp.sum((grad * value).reshape(8, 8, HALF), axis=0)
                        total = tap[2:3] * grad + tap[1:2] * (one * ahead[run, at + 1 : at + 65, lanes])
                        total = total + tap[0:1] * (two * ahead[run, at + 2 : at + 66, lanes])
                        conv_in = proj[run, rows, 2 * CH + lane * HALF : 2 * CH + (lane + 1) * HALF]
                        gate = proj[run, rows, lanes]
                        gp[run, rows, lanes] = (total * conv_in).astype(BF16)
                        gp[run, rows, 2 * CH + lane * HALF : 2 * CH + (lane + 1) * HALF] = (total * gate).astype(BF16)
                return 0

            lax.fori_loop(0, RING, unmix, 0)
            yield 3.0
            places = ring_places(x)
            for number, at in enumerate(places[:1]):
                parts[at] = dot_nn(gp[at], mat_in()).astype(BF16).reshape(2, SHARD, WIDTH)
                work.set((NORMED, READY, number))
                yield 1.1
            yield from in_grads((0, 2))
            yield GAIN_TWO
            small[...] = jnp.zeros_like(small)
            small[0:1] = jnp.sum(gain_sum[...], axis=0, keepdims=True) / gains[0:1]
            small[1:2] = jnp.sum(gain_two[...], axis=0, keepdims=True)
            mine = pl.ds(pl.multiple_of((x * 2 + k) * CH, CH), CH)
            for number in range(3):
                small[2 + number : 3 + number, mine] = jnp.sum(tap_sum[number], axis=0, keepdims=True)
            work.set((SMALL, GO))
            for half in (0, 1):
                work.set((IN, GO, half))
            for number, at in enumerate(places[1:], 1):
                parts[at] = dot_nn(gp[at], mat_in()).astype(BF16).reshape(2, SHARD, WIDTH)
                work.set((NORMED, READY, number))
                yield 1.1
            yield 0.2
            yield DOWN_GRAD
            yield (DWG, DONE, 0)
            yield (DWG, DONE, 1)
            work.copy(ffn_grad, ffn_grad_out)
            for name in (CIN, IN):
                yield (name, DONE, 0)
                yield (name, DONE, 1)
            work.copy(mixer_grad, mixer_grad_out)
            yield (SMALL, DONE)
            work.copy(small_out, small_final)

        def close():
            yield (NORMED, DONE)
            yield TOKENS
            yield GRAD_RESIDUAL

            def one(at):
                grad = parts[x, k, at].astype(F32) + box[x, at].astype(F32)
                grad = grad + (land[0, at].astype(F32) + land[1, at].astype(F32))
                rows = tokens[at]
                scale = lax.rsqrt(jnp.mean(rows * rows, axis=1, keepdims=True) + NORM_EPS)
                normal = rows * scale
                scaled = grad * gains[0:1]
                back = scale * (scaled - normal * jnp.mean(scaled * normal, axis=1, keepdims=True))
                tokens[at] = grad_residual[at] + back

            strips(SHARD, 16, one)
            work.copy(tokens, input_grad_out)
            yield 1.2

        def close_down():
            yield DOWN_PARTS
            yield (GRAD, SIB, 7)
            for number in range(4):
                work.set((DOWN, READY, number))
            yield (DOWN, DONE)
            yield RESIDUAL

            def one(at):
                total = down_parts[x, k, at].astype(F32) + down_box[x, at].astype(F32)
                total = total + (down_land[0, at].astype(F32) + down_land[1, at].astype(F32))
                residual[at] = residual[at] + total

            strips(SHARD, 16, one)
            work.copy(residual, output_out)
            yield 0.4

        work.add(opening())
        work.add(gather_x(work, low_in, ga, GRAD, copy=True))
        work.add(stream(work, ins), 1)
        work.add(scatter_x(work, down_parts, down_box, down_hop, down_land, DOWN))
        work.add(scatter_x(work, parts, box, hop, land, NORMED))
        work.add(sum_all(work, small, box_small, small_out, SMALL))
        for half in (0, 1):
            work.add(scatter_yz(work, ffn_w, ffn_boxes.at[half], ffn_grad, half, DWG))
        for name, first, box_of, where in ((CIN, 0, box_cin, (1, 3)), (IN, 2, box_in, (0, 2))):
            for half in (0, 1):
                here = new.at[pl.ds(first, 2)]
                work.add(scatter_yz(work, here, box_of.at[half], mixer_grad, half, name, where))
        work.add(compute(), 1)
        work.add(close(), 1)
        work.add(close_down(), 2)

    return call(
        "backward_mixer",
        2,
        body,
        [
            (grad_low, ANY), (ffn_part, ANY), (down_part, ANY), (down_grad, ANY),
            (normed, ANY), (w_in, ANY), (w_out, ANY), (proj, ANY), (near, ANY), (far, ANY),
            (taps, ANY), (starts, SMEM), (tokens, ANY), (residual, ANY), (grad_residual, ANY), (gains, ANY),
            (gain_two, ANY),
        ],
        [
            (fl(SHARD, WIDTH), ANY), (fl(SHARD, WIDTH), ANY), (fl(4, CH, HALF), ANY), (fl(3, HID, CH), ANY),
            (fl(8, WIDTH), ANY),
        ],
        [
            pltpu.VMEM((RING, 8, CH), F32),
            pltpu.VMEM((8, CH), F32),
            pltpu.VMEM((2, 8, HALF), F32),
            pltpu.VMEM((2, WIDTH), F32),
            pltpu.VMEM((8, WIDTH), F32),
            pltpu.VMEM((4, CH, HALF), F32),
            pltpu.VMEM((8, WIDTH), F32),
            pltpu.VMEM((RING, 2, SHARD, WIDTH), BF16),
            pltpu.VMEM((RING, SHARD, WIDTH), BF16),
            pltpu.VMEM((2, SHARD // 2, WIDTH), BF16),
            pltpu.VMEM((2, SHARD, WIDTH), BF16),
            pltpu.VMEM((SHARD, WIDTH), F32),
            pltpu.VMEM((2, 2, HID, WIDTH), BF16),
            pltpu.VMEM((3, HID, CH), F32),
            pltpu.VMEM((2, 15, 2, HID, HALF), BF16),
            pltpu.VMEM((SHARD, WIDTH), F32),
            pltpu.VMEM((SHARD, WIDTH), F32),
            pltpu.VMEM((RING, 2, SHARD, WIDTH), BF16),
            pltpu.VMEM((RING, 2, SHARD, WIDTH), BF16),
            pltpu.VMEM((4, 2, HALF, WIDTH), BF16),
            pltpu.VMEM((RING, RUN, 3 * CH), F32),
            pltpu.VMEM((RING, RUN + 8, CH), F32),
            pltpu.VMEM((RING, RUN + 8, CH), F32),
            pltpu.VMEM((RING, RUN, CH), F32),
            pltpu.VMEM((RING, RUN, CH), BF16),
            pltpu.VMEM((RING, RUN, 3 * CH), BF16),
            pltpu.VMEM((RING, 8, CH), F32),
            pltpu.VMEM((8, CH), F32),
            pltpu.VMEM((3, 8, CH), F32),
            pltpu.VMEM((8, WIDTH), F32),
            pltpu.VMEM((8, WIDTH), F32),
            pltpu.VMEM((4, 2, HALF, WIDTH), BF16),
            pltpu.VMEM((RING, 2, SHARD, WIDTH), BF16),
            pltpu.VMEM((RING, SHARD, WIDTH), BF16),
            pltpu.VMEM((2, SHARD // 2, WIDTH), BF16),
            pltpu.VMEM((2, SHARD, WIDTH), BF16),
            *[pltpu.VMEM((2, 15, 2, HALF, HALF), BF16)] * 2,
            pltpu.VMEM((4, RING, 8, WIDTH), F32),
        ],
        (90, 300, 20),
        X_WAYS + YZ_WAYS + (("z", 2), ("y", 2), ("x", 2), ("row", -1)),
        int(9e9),
        63,
    )


def adam_update(weight, gradient, first, second, step_rate, decay_rate):
    first_new = BETA_ONE * first + (1.0 - BETA_ONE) * gradient
    second_new = BETA_TWO * second + (1.0 - BETA_TWO) * gradient * gradient
    first_hat = first_new / (1.0 - BETA_ONE**STEP)
    second_hat = second_new / (1.0 - BETA_TWO**STEP)
    weight_new = weight - step_rate * (
        first_hat / (jnp.sqrt(second_hat) + ADAM_EPS) + decay_rate * weight
    )
    return (weight_new, first_new, second_new)


def body(
    tokens,
    cotangent,
    doc_starts,
    mixer_w,
    ffn_w,
    gains,
    taps,
    mixer_m,
    mixer_v,
    ffn_m,
    ffn_v,
    gain_m,
    gain_v,
    tap_m,
    tap_v,
):
    col = lax.axis_index("col")
    ffn_turned = jnp.swapaxes(ffn_w, 1, 2)
    normed, cot, w_in, w_out, ffn, proj, near, far, taps_two, residual, rows = forward_mixer(
        tokens, cotangent, doc_starts, mixer_w, ffn_turned, gains, taps
    )
    grad_residual, grad_low, down_part, down_grad, ffn_part, gain_two = feed_forward(
        rows, cot, ffn, ffn_turned, residual, cotangent, gains
    )
    output, input_grad, mixer_grad, ffn_grad, total = backward_mixer(
        grad_low, ffn_part, down_part, down_grad, normed, w_in, w_out, proj, near, far, taps_two, doc_starts, tokens,
        residual, grad_residual, gains, gain_two,
    )
    ffn_grad = jnp.swapaxes(ffn_grad, 1, 2)
    gain_grad = total[:2]
    first = ((col // 4) * 2 + col % 2) * CH + (col // 2) % 2 * HALF
    tap_grad = lax.dynamic_slice(total, (2, first), (3, HALF))
    mixer_new, mixer_m_new, mixer_v_new = adam_update(
        mixer_w, mixer_grad, mixer_m, mixer_v, MATRIX_RATE, MATRIX_DECAY
    )
    ffn_new, ffn_m_new, ffn_v_new = adam_update(
        ffn_w, ffn_grad, ffn_m, ffn_v, MATRIX_RATE, MATRIX_DECAY
    )
    gain_new, gain_m_new, gain_v_new = adam_update(
        gains, gain_grad, gain_m, gain_v, SMALL_RATE, 0.0
    )
    tap_new, tap_m_new, tap_v_new = adam_update(taps, tap_grad, tap_m, tap_v, SMALL_RATE, 0.0)
    return (
        output,
        input_grad,
        mixer_grad,
        mixer_new,
        mixer_m_new,
        mixer_v_new,
        ffn_grad,
        ffn_new,
        ffn_m_new,
        ffn_v_new,
        gain_grad,
        gain_new,
        gain_m_new,
        gain_v_new,
        tap_grad,
        tap_new,
        tap_m_new,
        tap_v_new,
    )


def solution(mesh):
    placed = (
        P(("row", "col"), None),
        P(("row", "col"), None),
        P(),
        P(None, "row", "col"),
        P(None, "row", "col"),
        P(),
        P(None, "col"),
        P(None, "row", "col"),
        P(None, "row", "col"),
        P(None, "row", "col"),
        P(None, "row", "col"),
        P(),
        P(),
        P(None, "col"),
        P(None, "col"),
    )
    return jax.shard_map(
        body,
        mesh=mesh,
        in_specs=placed,
        out_specs=(
            P(("row", "col"), None),
            P(("row", "col"), None),
            P(None, "row", "col"),
            P(None, "row", "col"),
            P(None, "row", "col"),
            P(None, "row", "col"),
            P(None, "row", "col"),
            P(None, "row", "col"),
            P(None, "row", "col"),
            P(None, "row", "col"),
            P(),
            P(),
            P(),
            P(),
            P(None, "col"),
            P(None, "col"),
            P(None, "col"),
            P(None, "col"),
        ),
        check_vma=False,
    )
```
